32 devices in a mesh: parts: 2 (over y), tensor: 4 (over z), example: 2 (over x), test: 2 (over core).
Axes of the slice: x: 2, y: 2, z: 4, core: 2. Of those that a mesh axis runs over, the one named last changes fastest.
Arguments:
- activations: bfloat16 [8, 128, 5120], P(('parts', 'example'), None, 'tensor'), parts along dimension 0, may hold values from -6 to 6
- out_grad: bfloat16 [8, 128, 5120], P(('parts', 'example'), None, 'tensor'), parts along dimension 0, may hold values from -6 to 6
- w_gate: bfloat16 [5120, 16384], P(('example', 'test'), 'tensor'), may hold values from -0.078125 to 0.078125
- w_up: bfloat16 [5120, 16384], P(('example', 'test'), 'tensor'), may hold values from -0.078125 to 0.078125
- w_down: bfloat16 [16384, 5120], P('tensor', ('example', 'test')), may hold values from -0.046875 to 0.046875
- proj_model: bfloat16 [5120, 192], P('tensor'), may hold values from -0.078125 to 0.078125
- proj_hidden: bfloat16 [16384, 192], P('tensor'), may hold values from -0.046875 to 0.046875
- test_grads: bfloat16 [3, 64, 64, 1024], P(None, 'tensor', None, 'test'), may hold values from -0.0048828125 to 0.0048828125
- lengths: int32 [8], P(('parts', 'example')), parts along dimension 0, may hold values from 1 to 128, as said below
- groups: int32 [8], P(('parts', 'example')), parts along dimension 0, may hold values from 0 to 3, as said below
Outputs:
- scores: float32 [8, 1024], P(('parts', 'example'), 'test'), parts along dimension 0
- group_scores: float32 [8, 1024], P('parts', 'test'), parts along dimension 0
The draws below stay inside these ranges and needn't reach their ends.
There are 2 independent parts, one for each index of `parts`. The reference program is written for one: setup_inputs(seed, part) draws one part's arguments, and reference() takes and returns one part's arrays. A program takes and returns all parts, laid end to end along the dimension named above; an argument that names none is the same for every part. Nothing has to cross between parts.
Inputs may be any that keep to these rules, and one draw needn't show every extreme that they name: `lengths`: at least one example of each draw has all 128 tokens valid. At least two different groups occur in each draw.
All inputs are finite; a program needn't handle non-finite values.
Results may differ from the reference program's by a relative error of at most 0.003.
Values may be sent and summed in bfloat16 or wider, within the bound.
No kernel may reach another device: no remote copies, remote signals or barrier semaphores. Data moves between devices by JAX's collectives and lax.ppermute only.
A program may use at most 256 MiB of HBM per device.

```python
import jax
import jax.numpy as jnp
from jax import lax

D = 5120
FF = 16384
K = 64
NTEST = 1024
SEQ = 128
NGROUP = 4
BATCH = 4


def draw_lengths(key, part):
    key = jax.random.fold_in(key, 11)
    first_key, second_key = jax.random.split(key)
    values = jax.random.randint(first_key, (BATCH,), 1, SEQ + 1)
    chosen = jax.random.randint(second_key, (), 0, BATCH)
    return jnp.where(jnp.arange(BATCH) == chosen, SEQ, values).astype(jnp.int32)


def draw_groups(key, part):
    key = jax.random.fold_in(key, 23)
    first_key, second_key = jax.random.split(key)
    values = jax.random.randint(first_key, (BATCH,), 0, NGROUP)
    offset = jax.random.randint(second_key, (), 1, NGROUP)
    second = (values[0] + offset) % NGROUP
    return jnp.where(jnp.arange(BATCH) == 1, second, values).astype(jnp.int32)


def shard_levels(key, shape, shards, least, top_value):
    gain, own = 1.0, jax.random.fold_in(key, 6)
    for position, blocks in shards:
        steps = jnp.exp(jax.random.uniform(jax.random.fold_in(own, position), (blocks,), jnp.float32, least / len(shards), top_value / len(shards)))
        gain = gain * jnp.repeat(steps, shape[position] // blocks).reshape([-1 if axis == position else 1 for axis in range(len(shape))])
    return gain


def bell_draw(own_key, dims, width, most, cuts=(), kind=jnp.bfloat16):
    entries = width * jax.random.normal(own_key, dims, jnp.float32)
    if cuts:
        entries = entries * shard_levels(own_key, dims, cuts, -0.22, 0.18)
    return jnp.clip(entries, -most, most).astype(kind)


def setup_inputs(seed: int = 0, part: int = 0) -> dict:
    keys = jax.random.split(jax.random.key(seed), 11)
    part_keys = jax.random.split(jax.random.fold_in(keys[10], part), 11)
    return {
        "activations": bell_draw(part_keys[0], (BATCH, SEQ, D), 1.0, 6.0, ((0, 2), (2, 4))),
        "out_grad": bell_draw(part_keys[1], (BATCH, SEQ, D), 1.0, 6.0, ((0, 2), (2, 4))),
        "w_gate": bell_draw(keys[2], (D, FF), D ** -0.5, 0.078125, ((0, 4), (1, 4))),
        "w_up": bell_draw(keys[3], (D, FF), D ** -0.5, 0.078125, ((0, 4), (1, 4))),
        "w_down": bell_draw(keys[4], (FF, D), FF ** -0.5, 0.046875, ((0, 4), (1, 4))),
        "proj_model": bell_draw(keys[5], (D, 3 * K), D ** -0.5, 0.078125, ((0, 4),)),
        "proj_hidden": bell_draw(keys[6], (FF, 3 * K), FF ** -0.5, 0.046875, ((0, 4),)),
        "test_grads": bell_draw(keys[7], (3, K, K, NTEST), (3 * K * K * SEQ) ** -0.5, 0.0048828125, ((1, 4), (3, 2))),
        "lengths": draw_lengths(jax.random.fold_in(jax.random.fold_in(keys[10], part), 71), part),
        "groups": draw_groups(jax.random.fold_in(jax.random.fold_in(keys[10], part), 71), part),
    }


def reference(activations, out_grad, w_gate, w_up, w_down, proj_model, proj_hidden, test_grads, lengths, groups):
    tok_rows = BATCH * SEQ
    flat_acts = activations.reshape(tok_rows, D)
    flat_grad = out_grad.reshape(tok_rows, D)
    gate_act = jnp.dot(flat_acts, w_gate, preferred_element_type=jnp.float32)
    up_act = jnp.dot(flat_acts, w_up, preferred_element_type=jnp.float32)
    sigmoid_gate = jax.nn.sigmoid(gate_act)
    silu_gate = gate_act * sigmoid_gate
    hidden = (silu_gate * up_act).astype(jnp.bfloat16)
    d_hidden = lax.dot_general(flat_grad, w_down, (((1,), (1,)), ((), ())), preferred_element_type=jnp.float32)
    d_gate = (d_hidden * up_act * sigmoid_gate * (1.0 + gate_act * (1.0 - sigmoid_gate))).astype(jnp.bfloat16)
    d_up = (d_hidden * silu_gate).astype(jnp.bfloat16)
    inputs_proj = jnp.concatenate([
        jnp.dot(flat_acts, proj_model[:, :2 * K], preferred_element_type=jnp.float32),
        jnp.dot(hidden, proj_hidden[:, 2 * K:], preferred_element_type=jnp.float32)], 1)
    outputs_proj = jnp.concatenate([
        jnp.dot(d_gate, proj_hidden[:, :K], preferred_element_type=jnp.float32),
        jnp.dot(d_up, proj_hidden[:, K:2 * K], preferred_element_type=jnp.float32),
        jnp.dot(flat_grad, proj_model[:, 2 * K:], preferred_element_type=jnp.float32)], 1)
    inputs_proj = inputs_proj.reshape(BATCH, SEQ, 3, K)
    outputs_proj = outputs_proj.reshape(BATCH, SEQ, 3, K)
    positions = jnp.arange(SEQ, dtype=jnp.int32)
    token_mask = (positions[None, :] < lengths[:, None]).astype(jnp.float32)
    example_grads = jnp.einsum("bsli,bslj->blij", outputs_proj * token_mask[:, :, None, None], inputs_proj,
                               precision=lax.Precision.HIGHEST)
    scores = jnp.einsum("blij,lijn->bn", example_grads, test_grads.astype(jnp.float32),
                        precision=lax.Precision.HIGHEST)
    group_onehot = (groups[:, None] == jnp.arange(NGROUP, dtype=jnp.int32)[None, :]).astype(jnp.float32)
    group_scores = jnp.dot(group_onehot.T, scores, precision=lax.Precision.HIGHEST)
    return scores, group_scores
```

```python
import jax
import jax.numpy as jnp
from jax import lax
from jax.sharding import PartitionSpec as P

NGROUP = 4
F32 = jnp.float32
SEND_SCALE = 16.0


def shift(value, axis, step):
    n = lax.axis_size(axis)
    return lax.ppermute(value, axis, [(i, (i + step) % n) for i in range(n)])


def pack(value):
    return (value * SEND_SCALE).astype(jnp.float16)


def unpack(value):
    return value.astype(F32) * (1.0 / SEND_SCALE)


def gather_in_order(value, axis):
    n = lax.axis_size(axis)
    if n == 1:
        return value[None]
    if n > 8:
        return lax.all_gather(value, axis, axis=0)
    got = [shift(value, axis, step) for step in range(n - 1, 0, -1)] + [value]
    return lax.dynamic_slice_in_dim(
        jnp.stack(got + got), n - 1 - lax.axis_index(axis), n, 0
    )


def scatter_sum(value, axis, dim):
    n = lax.axis_size(axis)
    if n > 8:
        return lax.psum_scatter(value, axis, scatter_dimension=dim, tiled=True)
    me = lax.axis_index(axis)
    width = value.shape[dim] // n
    total = lax.dynamic_slice_in_dim(value, me * width, width, dim)
    for step in range(1, n):
        block = lax.dynamic_slice_in_dim(value, lax.rem(me + step, n) * width, width, dim)
        total = total + shift(block, axis, step)
    return total


def on_device(
    activations,
    out_grad,
    w_gate,
    w_up,
    w_down,
    proj_model,
    proj_hidden,
    test_grads,
    lengths,
    groups,
):
    ex_loc, seq_len, d_local = activations.shape
    tok_rows = ex_loc * seq_len
    width = proj_model.shape[1] // 3
    n_cores = lax.axis_size("test")
    core = lax.axis_index("test")
    n_ex = lax.axis_size("example")
    ex_index = lax.axis_index("example")
    hid_part = w_gate.shape[1] // n_cores
    rows_part = tok_rows // n_cores
    flat_acts = activations.reshape(tok_rows, d_local)
    flat_grad = out_grad.reshape(tok_rows, d_local)

    def features_here(flat):
        mine = lax.dynamic_slice_in_dim(flat, core * rows_part, rows_part, 0)
        whole = lax.all_gather(mine, "tensor", axis=1, tiled=True)
        return lax.all_to_all(whole, ("example", "test"), split_axis=1, concat_axis=0, tiled=True)

    acts_here = features_here(flat_acts)
    grad_here = features_here(flat_grad)

    def core_sum(product):
        kept = lax.dynamic_slice_in_dim(product, core * hid_part, hid_part, 1)
        for step in range(1, n_cores):
            to = lax.rem(core + step, n_cores)
            sent = pack(lax.dynamic_slice_in_dim(product, to * hid_part, hid_part, 1))
            kept = kept + unpack(shift(sent, "test", step))
        return kept

    def rows_of(tokens, owner):
        return lax.dynamic_slice_in_dim(tokens, owner * tok_rows, tok_rows, 0)

    def forward(tokens, weight):
        return jnp.dot(tokens, weight, preferred_element_type=F32)

    def backward(tokens, weight):
        return lax.dot_general(tokens, weight, (((1,), (1,)), ((), ())), preferred_element_type=F32)

    jobs = (
        (forward, acts_here, w_gate),
        (forward, acts_here, w_up),
        (backward, grad_here, w_down),
    )
    arrived = [[], [], []]
    for step in range(1, n_ex):
        owner = lax.rem(ex_index + step, n_ex)
        for place, (product, tokens, weight) in enumerate(jobs):
            partial = core_sum(product(rows_of(tokens, owner), weight))
            arrived[place].append(shift(pack(partial), "example", step))
    own = [
        core_sum(product(rows_of(tokens, ex_index), weight)) for product, tokens, weight in jobs
    ]
    for place in range(3):
        for received in arrived[place]:
            own[place] = own[place] + unpack(received)
    gate_act, up_act, d_hidden = own

    model_part = jnp.concatenate(
        [
            jnp.dot(flat_acts, proj_model[:, : 2 * width], preferred_element_type=F32),
            jnp.dot(flat_grad, proj_model[:, 2 * width :], preferred_element_type=F32),
        ],
        1,
    )
    model_sum = lax.psum(model_part, "tensor")

    sigmoid_gate = jax.nn.sigmoid(gate_act)
    silu_gate = gate_act * sigmoid_gate
    hidden = (silu_gate * up_act).astype(jnp.bfloat16)
    d_gate = (d_hidden * up_act * sigmoid_gate * (1.0 + gate_act * (1.0 - sigmoid_gate))).astype(
        jnp.bfloat16
    )
    d_up = (d_hidden * silu_gate).astype(jnp.bfloat16)
    hid_proj = lax.dynamic_slice_in_dim(proj_hidden, core * hid_part, hid_part, 0)
    out_gate = jnp.dot(d_gate, hid_proj[:, :width], preferred_element_type=F32)
    out_up = jnp.dot(d_up, hid_proj[:, width : 2 * width], preferred_element_type=F32)
    in_hidden = jnp.dot(hidden, hid_proj[:, 2 * width :], preferred_element_type=F32)

    positions = jnp.arange(seq_len, dtype=jnp.int32)
    token_mask = (positions[None, :] < lengths[:, None]).astype(F32)[:, :, None]
    model_sum = model_sum.reshape(ex_loc, seq_len, 3, width)

    def outer(outputs, inputs):
        return jnp.einsum(
            "bsi,bsj->bij", outputs * token_mask, inputs, precision=lax.Precision.HIGHEST
        )

    grads_part = jnp.stack(
        [
            outer(out_gate.reshape(ex_loc, seq_len, width), model_sum[:, :, 0]),
            outer(out_up.reshape(ex_loc, seq_len, width), model_sum[:, :, 1]),
            outer(model_sum[:, :, 2], in_hidden.reshape(ex_loc, seq_len, width)),
        ],
        1,
    )
    grads_half = scatter_sum(grads_part, "tensor", 2)
    grads_mine = grads_half
    for step in range(1, n_cores):
        grads_mine = grads_mine + shift(grads_half, "test", step)
    partial_scores = jnp.einsum(
        "blij,lijn->bn",
        grads_mine,
        test_grads.astype(F32),
        precision=lax.Precision.HIGHEST,
    )
    scores = jnp.sum(gather_in_order(partial_scores, "tensor"), 0)
    group_onehot = (groups[:, None] == jnp.arange(NGROUP, dtype=jnp.int32)[None, :]).astype(F32)
    group_part = jnp.dot(group_onehot.T, scores, precision=lax.Precision.HIGHEST)
    group_scores = jnp.sum(gather_in_order(group_part, "example"), 0)
    return (scores, group_scores)


def solution(mesh):
    placed = (
        P(("parts", "example"), None, "tensor"),
        P(("parts", "example"), None, "tensor"),
        P(("example", "test"), "tensor"),
        P(("example", "test"), "tensor"),
        P("tensor", ("example", "test")),
        P("tensor", None),
        P("tensor", None),
        P(None, "tensor", None, "test"),
        P(("parts", "example")),
        P(("parts", "example")),
    )
    return jax.shard_map(
        on_device,
        mesh=mesh,
        in_specs=placed,
        out_specs=(P(("parts", "example"), "test"), P("parts", "test")),
        check_vma=False,
    )
```

```python
import jax
import jax.numpy as jnp
from jax import lax
from jax.sharding import PartitionSpec as P

NGROUP = 4
F32 = jnp.float32
SEND_SCALE = 16.0


def shift(value, axis, step):
    n = lax.axis_size(axis)
    return lax.ppermute(value, axis, [(i, (i + step) % n) for i in range(n)])


def pack(value):
    return (value * SEND_SCALE).astype(jnp.float16)


def unpack(value):
    return value.astype(F32) * (1.0 / SEND_SCALE)


def gather_in_order(value, axis):
    n = lax.axis_size(axis)
    if n == 1:
        return value[None]
    if n > 8:
        return lax.all_gather(value, axis, axis=0)
    return in_order([value] + [shift(value, axis, step) for step in range(1, n)], axis)


def scatter_sum(value, axis, dim):
    n = lax.axis_size(axis)
    if n > 8:
        return lax.psum_scatter(value, axis, scatter_dimension=dim, tiled=True)
    me = lax.axis_index(axis)
    width = value.shape[dim] // n
    total = lax.dynamic_slice_in_dim(value, me * width, width, dim)
    for step in range(1, n):
        block = lax.dynamic_slice_in_dim(value, lax.rem(me + step, n) * width, width, dim)
        total = total + shift(block, axis, step)
    return total


def after(value, *earlier):
    return lax.optimization_barrier((value,) + earlier)[0]


def in_order(pieces, axis):
    n = len(pieces)
    back = pieces[:0:-1] + pieces[:1]
    return lax.dynamic_slice_in_dim(jnp.stack(back + back), n - 1 - lax.axis_index(axis), n, 0)


def gather_features(mine, marks=()):
    n = lax.axis_size("tensor")
    if n > 8:
        return lax.all_gather(mine, "tensor", axis=0)
    pieces = [mine]
    for step in range(1, n):
        start = after(mine, marks[min(step, len(marks)) - 1]) if marks else mine
        pieces.append(shift(start, "tensor", step))
    return in_order(pieces, "tensor")


def features_here(blocks):
    peers = lax.axis_size("example") * lax.axis_size("test")
    n, rows, d_local = blocks.shape
    if n == peers == 4:
        return swap_features(blocks)
    whole = jnp.transpose(blocks, (1, 0, 2)).reshape(rows, n * d_local)
    return lax.all_to_all(whole, ("example", "test"), split_axis=1, concat_axis=0, tiled=True)


def swap_features(blocks):
    ex_index, core = lax.axis_index("example"), lax.axis_index("test")
    got = {}
    for ex_step in (1, 0):
        for core_step in (0, 1):
            wanted = ((ex_index + ex_step) % 2) * 2 + (core + core_step) % 2
            piece = lax.dynamic_index_in_dim(blocks, wanted, 0, keepdims=False)
            if ex_step or core_step:
                pairs = [
                    (2 * e + c, 2 * ((e + ex_step) % 2) + (c + core_step) % 2)
                    for e in range(2)
                    for c in range(2)
                ]
                piece = lax.ppermute(piece, ("example", "test"), pairs)
            got[ex_step, core_step] = piece
    halves = [
        jnp.concatenate(
            [
                jnp.where(core == 0, got[ex_step, 0], got[ex_step, 1]),
                jnp.where(core == 0, got[ex_step, 1], got[ex_step, 0]),
            ]
        )
        for ex_step in (0, 1)
    ]
    return halves


def on_device(
    activations,
    out_grad,
    w_gate,
    w_up,
    w_down,
    proj_model,
    proj_hidden,
    test_grads,
    lengths,
    groups,
):
    ex_loc, seq_len, d_local = activations.shape
    tok_rows = ex_loc * seq_len
    width = proj_model.shape[1] // 3
    n_cores = lax.axis_size("test")
    core = lax.axis_index("test")
    n_ex = lax.axis_size("example")
    ex_index = lax.axis_index("example")
    hid_part = w_gate.shape[1] // n_cores
    rows_part = tok_rows // n_cores
    flat_acts = activations.reshape(tok_rows, d_local)
    flat_grad = out_grad.reshape(tok_rows, d_local)

    acts_mine = lax.dynamic_slice_in_dim(flat_acts, core * rows_part, rows_part, 0)
    grad_mine = lax.dynamic_slice_in_dim(flat_grad, core * rows_part, rows_part, 0)
    acts_blocks = gather_features(acts_mine)
    model_part = jnp.concatenate(
        [
            jnp.dot(flat_acts, proj_model[:, : 2 * width], preferred_element_type=F32),
            jnp.dot(flat_grad, proj_model[:, 2 * width :], preferred_element_type=F32),
        ],
        1,
    )
    model_sum = lax.psum(after(model_part, acts_blocks), "tensor")
    acts_here = features_here(acts_blocks)

    def rows_of(tokens, step):
        if isinstance(tokens, list):
            return tokens[step]
        owner = lax.rem(ex_index + step, n_ex)
        return lax.dynamic_slice_in_dim(tokens, owner * tok_rows, tok_rows, 0)

    def core_sum(product):
        kept = unpack(lax.dynamic_slice_in_dim(product, core * hid_part, hid_part, 1))
        for step in range(1, n_cores):
            to = lax.rem(core + step, n_cores)
            sent = lax.dynamic_slice_in_dim(product, to * hid_part, hid_part, 1)
            kept = kept + unpack(shift(sent, "test", step))
        return kept

    def forward(tokens, weight):
        return pack(jnp.dot(tokens, weight, preferred_element_type=F32))

    def backward(tokens, weight):
        return pack(
            lax.dot_general(tokens, weight, (((1,), (1,)), ((), ())), preferred_element_type=F32)
        )

    jobs = [(forward, acts_here, w_gate), (forward, acts_here, w_up)]

    def products(place, step, *earlier):
        product, tokens, weight = jobs[place]
        return product(after(rows_of(tokens, step), *earlier), weight)

    def send(place, step, whole):
        sent = pack(core_sum(whole))
        arrived[place].append(shift(sent, "example", step))
        return sent

    arrived = [[], [], []]
    last = acts_mine
    marks = [acts_blocks]
    for step in range(1, n_ex):
        gate_far = products(0, step, last)
        up_far = products(1, step, gate_far)
        gate_sent = send(0, step, gate_far)
        up_sent = send(1, step, up_far)
        last = up_far
        marks += [gate_far, gate_sent]
    grad_blocks = gather_features(grad_mine, marks)
    gate_near = products(0, 0, last, gate_sent)
    up_near = products(1, 0, gate_near, up_sent)
    last = up_near
    jobs.append((backward, features_here(grad_blocks), w_down))
    for step in range(1, n_ex):
        down_far = products(2, step, last, *arrived[0])
        down_sent = send(2, step, down_far)
        last = down_far
    down_near = products(2, 0, last)
    own = [core_sum(gate_near), core_sum(up_near), core_sum(down_near)]
    gate_act, up_act, d_hidden = [
        kept + sum(unpack(received) for received in got) for kept, got in zip(own, arrived)
    ]

    sigmoid_gate = jax.nn.sigmoid(gate_act)
    silu_gate = gate_act * sigmoid_gate
    hidden = (silu_gate * up_act).astype(jnp.bfloat16)
    d_gate = (d_hidden * up_act * sigmoid_gate * (1.0 + gate_act * (1.0 - sigmoid_gate))).astype(
        jnp.bfloat16
    )
    d_up = (d_hidden * silu_gate).astype(jnp.bfloat16)
    hid_proj = lax.dynamic_slice_in_dim(proj_hidden, core * hid_part, hid_part, 0)
    out_gate = jnp.dot(d_gate, hid_proj[:, :width], preferred_element_type=F32)
    out_up = jnp.dot(d_up, hid_proj[:, width : 2 * width], preferred_element_type=F32)
    in_hidden = jnp.dot(hidden, hid_proj[:, 2 * width :], preferred_element_type=F32)

    positions = jnp.arange(seq_len, dtype=jnp.int32)
    token_mask = (positions[None, :] < lengths[:, None]).astype(F32)[:, :, None]
    masked = model_sum.reshape(ex_loc, seq_len, 3 * width) * token_mask

    def outer(outputs, inputs):
        return jnp.einsum("bsi,bsj->bij", outputs, inputs, precision=lax.Precision.HIGHEST)

    by_token = (ex_loc, seq_len, width)
    grads_part = jnp.stack(
        [
            outer(out_gate.reshape(by_token), masked[:, :, :width]),
            outer(out_up.reshape(by_token), masked[:, :, width : 2 * width]),
            outer(masked[:, :, 2 * width :], in_hidden.reshape(by_token)),
        ],
        1,
    )
    grads_part = scatter_sum(grads_part, "tensor", 2)
    by_example = []
    for ex_step in range(n_ex):
        total = None
        for core_step in range(n_cores):
            piece = grads_part
            if ex_step or core_step:
                pairs = [
                    (e * n_cores + c, (e + ex_step) % n_ex * n_cores + (c + core_step) % n_cores)
                    for e in range(n_ex)
                    for c in range(n_cores)
                ]
                piece = lax.ppermute(piece, ("example", "test"), pairs)
            total = piece if total is None else total + piece
        by_example.append(total)
    grads_all = in_order(by_example, "example").reshape((n_ex * ex_loc,) + grads_part.shape[1:])
    partial_scores = jnp.einsum(
        "blij,lijn->bn",
        grads_all,
        test_grads.astype(F32),
        precision=lax.Precision.HIGHEST,
    )
    all_scores = jnp.sum(gather_in_order(partial_scores, "tensor"), 0)
    scores = lax.dynamic_slice_in_dim(all_scores, ex_index * ex_loc, ex_loc, 0)
    all_groups = gather_in_order(groups, "example").reshape(-1)
    group_onehot = (all_groups[:, None] == jnp.arange(NGROUP, dtype=jnp.int32)[None, :]).astype(F32)
    group_scores = jnp.dot(group_onehot.T, all_scores, precision=lax.Precision.HIGHEST)
    return (scores, group_scores)


def solution(mesh):
    placed = (
        P(("parts", "example"), None, "tensor"),
        P(("parts", "example"), None, "tensor"),
        P(("example", "test"), "tensor"),
        P(("example", "test"), "tensor"),
        P("tensor", ("example", "test")),
        P("tensor", None),
        P("tensor", None),
        P(None, "tensor", None, "test"),
        P(("parts", "example")),
        P(("parts", "example")),
    )
    return jax.shard_map(
        on_device,
        mesh=mesh,
        in_specs=placed,
        out_specs=(P(("parts", "example"), "test"), P("parts", "test")),
        check_vma=False,
    )
```

```python
import jax
import jax.numpy as jnp
from jax import lax
from jax.experimental import pallas as pl
from jax.experimental.pallas import tpu as pltpu
from jax.sharding import PartitionSpec as P

NGROUP = 4
F32 = jnp.float32
SEND_SCALE = 16.0


def shift(value, axis, step):
    n = lax.axis_size(axis)
    return lax.ppermute(value, axis, [(i, (i + step) % n) for i in range(n)])


def pack(value):
    return (value * SEND_SCALE).astype(jnp.float16)


def unpack(value):
    return value.astype(F32) * (1.0 / SEND_SCALE)


def gather_in_order(value, axis):
    n = lax.axis_size(axis)
    if n == 1:
        return value[None]
    if n > 8:
        return lax.all_gather(value, axis, axis=0)
    return in_order([value] + [shift(value, axis, step) for step in range(1, n)], axis)


def scatter_sum(value, axis, dim):
    n = lax.axis_size(axis)
    if n > 8:
        return lax.psum_scatter(value, axis, scatter_dimension=dim, tiled=True)
    me = lax.axis_index(axis)
    width = value.shape[dim] // n
    total = lax.dynamic_slice_in_dim(value, me * width, width, dim)
    for step in range(1, n):
        block = lax.dynamic_slice_in_dim(value, lax.rem(me + step, n) * width, width, dim)
        total = total + shift(block, axis, step)
    return total


def after(value, *earlier):
    return lax.optimization_barrier((value,) + earlier)[0]


def in_order(pieces, axis):
    n = len(pieces)
    back = pieces[:0:-1] + pieces[:1]
    return lax.dynamic_slice_in_dim(jnp.stack(back + back), n - 1 - lax.axis_index(axis), n, 0)


class Features:
    def __init__(self, flat):
        self.flat = flat
        self.n_ex, self.n_cores = lax.axis_size("example"), lax.axis_size("test")
        self.blocks = [None] * self.n_ex
        self.direct = (lax.axis_size("tensor"), self.n_ex, self.n_cores) == (4, 2, 2)

    def far(self, marks):
        if self.direct:
            self.blocks[1] = direct_features(self.flat, 1, marks)
            return
        rows = self.flat.shape[0]
        part = rows // self.n_cores
        mine = lax.dynamic_slice_in_dim(self.flat, lax.axis_index("test") * part, part, 0)
        whole = lax.all_gather(after(mine, marks[0]), "tensor", axis=1, tiled=True)
        whole = lax.all_to_all(
            whole, ("example", "test"), split_axis=1, concat_axis=0, tiled=True
        )
        for step in range(self.n_ex):
            owner = lax.rem(lax.axis_index("example") + step, self.n_ex)
            self.blocks[step] = lax.dynamic_slice_in_dim(whole, owner * rows, rows, 0)

    def near(self, marks):
        if self.direct:
            self.blocks[0] = direct_features(self.flat, 0, marks)


def direct_features(flat, ex_step, marks):
    pieces = []
    for turn in range(2):
        pairs = []
        for block in range(4):
            example, core = block // 2, block % 2
            for source_core in range(2):
                target = block ^ (2 * turn + (source_core ^ core))
                source = block * 4 + (example ^ ex_step) * 2 + source_core
                pairs.append((source, target * 4 + example * 2 + core))
        start = after(flat, marks[min(turn, len(marks) - 1)])
        pieces.append(lax.ppermute(start, ("tensor", "example", "test"), pairs))
    block = lax.axis_index("example") * 2 + lax.axis_index("test")
    return jnp.where((lax.axis_index("tensor") ^ block) < 2, pieces[0], pieces[1])


def dot_rows_kernel(tokens_ref, weight_ref, out_ref):
    out_ref[...] = lax.dot_general(
        tokens_ref[...], weight_ref[...], (((1,), (1,)), ((), ())), preferred_element_type=F32
    )


def dot_rows(tokens, weight):
    rows, depth = tokens.shape
    hidden = weight.shape[0]
    tile = min(512, hidden)
    return pl.pallas_call(
        dot_rows_kernel,
        out_shape=jax.ShapeDtypeStruct((rows, hidden), F32),
        grid=(hidden // tile,),
        in_specs=[
            pl.BlockSpec((rows, depth), lambda i: (0, 0)),
            pl.BlockSpec((tile, depth), lambda i: (i, 0)),
        ],
        out_specs=pl.BlockSpec((rows, tile), lambda i: (0, i)),
        compiler_params=pltpu.CompilerParams(vmem_limit_bytes=16 * 2**20),
        cost_estimate=pl.CostEstimate(
            flops=2 * rows * depth * hidden,
            bytes_accessed=2 * hidden * depth + 4 * rows * hidden,
            transcendentals=0,
        ),
    )(tokens, weight)


def on_device(
    activations,
    out_grad,
    w_gate,
    w_up,
    w_down,
    proj_model,
    proj_hidden,
    test_grads,
    lengths,
    groups,
):
    ex_loc, seq_len, d_local = activations.shape
    tok_rows = ex_loc * seq_len
    width = proj_model.shape[1] // 3
    n_cores = lax.axis_size("test")
    core = lax.axis_index("test")
    n_ex = lax.axis_size("example")
    ex_index = lax.axis_index("example")
    hid_part = w_gate.shape[1] // n_cores
    flat_acts = activations.reshape(tok_rows, d_local)
    flat_grad = out_grad.reshape(tok_rows, d_local)

    def forward(tokens, weight):
        return jnp.dot(tokens, weight, preferred_element_type=F32)

    def core_sum(product):
        kept = lax.dynamic_slice_in_dim(product, core * hid_part, hid_part, 1)
        for step in range(1, n_cores):
            to = lax.rem(core + step, n_cores)
            sent = pack(lax.dynamic_slice_in_dim(product, to * hid_part, hid_part, 1))
            kept = kept + unpack(shift(sent, "test", step))
        return kept

    def send(place, step, whole):
        sent = pack(core_sum(whole))
        arrived[place].append(shift(sent, "example", step))
        return sent

    arrived = [[], [], []]
    begin = lengths
    acts = Features(flat_acts)
    acts.far([begin])
    model_part = jnp.concatenate(
        [
            jnp.dot(flat_acts, proj_model[:, : 2 * width], preferred_element_type=F32),
            jnp.dot(flat_grad, proj_model[:, 2 * width :], preferred_element_type=F32),
        ],
        1,
    )
    last = begin
    for step in range(1, n_ex):
        gate_far = forward(after(acts.blocks[step], last), w_gate)
        up_far = forward(after(acts.blocks[step], gate_far), w_up)
        gate_sent = send(0, step, gate_far)
        up_sent = send(1, step, up_far)
        last = up_far
    grad = Features(flat_grad)
    grad.far([acts.blocks[1], gate_sent])
    acts.near([gate_far, gate_sent])
    model_sum = lax.psum(after(model_part, gate_sent), "tensor")
    gate_near = forward(after(acts.blocks[0], last, gate_sent), w_gate)
    up_near = forward(after(acts.blocks[0], gate_near, up_sent), w_up)
    grad.near([up_sent, up_near])
    last = up_near
    for step in range(1, n_ex):
        down_far = dot_rows(after(grad.blocks[step], last, *arrived[0]), w_down)
        down_sent = send(2, step, down_far)
        last = down_far
    down_near = dot_rows(after(grad.blocks[0], last, down_sent, *arrived[1]), w_down)
    own = [core_sum(gate_near), core_sum(up_near), core_sum(down_near)]
    gate_act, up_act, d_hidden = [
        kept + sum(unpack(received) for received in got) for kept, got in zip(own, arrived)
    ]

    sigmoid_gate = jax.nn.sigmoid(gate_act)
    silu_gate = gate_act * sigmoid_gate
    hidden = (silu_gate * up_act).astype(jnp.bfloat16)
    d_gate = (d_hidden * up_act * sigmoid_gate * (1.0 + gate_act * (1.0 - sigmoid_gate))).astype(
        jnp.bfloat16
    )
    d_up = (d_hidden * silu_gate).astype(jnp.bfloat16)
    hid_proj = lax.dynamic_slice_in_dim(proj_hidden, core * hid_part, hid_part, 0)
    out_gate = jnp.dot(d_gate, hid_proj[:, :width], preferred_element_type=F32)
    out_up = jnp.dot(d_up, hid_proj[:, width : 2 * width], preferred_element_type=F32)
    in_hidden = jnp.dot(hidden, hid_proj[:, 2 * width :], preferred_element_type=F32)

    positions = jnp.arange(seq_len, dtype=jnp.int32)
    token_mask = (positions[None, :] < lengths[:, None]).astype(F32)[:, :, None]
    masked = model_sum.reshape(ex_loc, seq_len, 3 * width) * token_mask

    def outer(outputs, inputs):
        return jnp.einsum("bsi,bsj->bij", outputs, inputs, precision=lax.Precision.HIGHEST)

    by_token = (ex_loc, seq_len, width)
    grads_part = jnp.stack(
        [
            outer(out_gate.reshape(by_token), masked[:, :, :width]),
            outer(out_up.reshape(by_token), masked[:, :, width : 2 * width]),
            outer(masked[:, :, 2 * width :], in_hidden.reshape(by_token)),
        ],
        1,
    )
    grads_part = scatter_sum(grads_part, "tensor", 2)
    by_example = []
    for ex_step in range(n_ex):
        total = None
        for core_step in range(n_cores):
            piece = grads_part
            if ex_step or core_step:
                pairs = [
                    (e * n_cores + c, (e + ex_step) % n_ex * n_cores + (c + core_step) % n_cores)
                    for e in range(n_ex)
                    for c in range(n_cores)
                ]
                piece = lax.ppermute(piece, ("example", "test"), pairs)
            total = piece if total is None else total + piece
        by_example.append(total)
    grads_all = in_order(by_example, "example").reshape((n_ex * ex_loc,) + grads_part.shape[1:])
    partial_scores = jnp.einsum(
        "blij,lijn->bn",
        grads_all,
        test_grads.astype(F32),
        precision=lax.Precision.HIGHEST,
    )
    all_scores = jnp.sum(gather_in_order(partial_scores, "tensor"), 0)
    scores = lax.dynamic_slice_in_dim(all_scores, ex_index * ex_loc, ex_loc, 0)
    all_groups = gather_in_order(groups, "example").reshape(-1)
    group_onehot = (all_groups[:, None] == jnp.arange(NGROUP, dtype=jnp.int32)[None, :]).astype(F32)
    group_scores = jnp.dot(group_onehot.T, all_scores, precision=lax.Precision.HIGHEST)
    return (scores, group_scores)


def solution(mesh):
    placed = (
        P(("parts", "example"), None, "tensor"),
        P(("parts", "example"), None, "tensor"),
        P(("example", "test"), "tensor"),
        P(("example", "test"), "tensor"),
        P("tensor", ("example", "test")),
        P("tensor", None),
        P("tensor", None),
        P(None, "tensor", None, "test"),
        P(("parts", "example")),
        P(("parts", "example")),
    )
    return jax.shard_map(
        on_device,
        mesh=mesh,
        in_specs=placed,
        out_specs=(P(("parts", "example"), "test"), P("parts", "test")),
        check_vma=False,
    )
```

```python
import functools

import jax
import jax.numpy as jnp
from jax import lax
from jax.experimental import pallas as pl
from jax.experimental.pallas import tpu as pltpu
from jax.sharding import PartitionSpec as P

NGROUP = 4
F32 = jnp.float32
SEND_SCALE = 16.0


def shift(value, axis, step):
    n = lax.axis_size(axis)
    return lax.ppermute(value, axis, [(i, (i + step) % n) for i in range(n)])


def pack(value):
    return (value * SEND_SCALE).astype(jnp.float16)


def unpack(value):
    return value.astype(F32) * (1.0 / SEND_SCALE)


def exchange(blocks, axis):
    return lax.all_to_all(blocks, axis, split_axis=0, concat_axis=0, tiled=True)


def share(value, axis, n):
    return exchange(jnp.broadcast_to(value[None], (n,) + value.shape), axis)


def token(value):
    corner = value[(0,) * (value.ndim - 2)]
    return corner[:16, :128].astype(F32) if value.dtype == jnp.float16 else value


def after(value, *earlier):
    earlier = [token(one) for one in earlier]
    anywhere = pl.BlockSpec(memory_space=pl.ANY)
    return pl.pallas_call(
        lambda *refs: None,
        out_shape=jax.ShapeDtypeStruct(value.shape, value.dtype),
        in_specs=[anywhere] * (1 + len(earlier)),
        out_specs=anywhere,
        input_output_aliases={0: 0},
        cost_estimate=pl.CostEstimate(flops=1, bytes_accessed=1, transcendentals=0),
    )(value, *earlier)


def direct_features(starts, ex_step):
    pieces = []
    for turn in range(2):
        pairs = []
        for block in range(4):
            example, core = block // 2, block % 2
            for source_core in range(2):
                target = block ^ (2 * turn + (source_core ^ core))
                source = block * 4 + (example ^ ex_step) * 2 + source_core
                pairs.append((source, target * 4 + example * 2 + core))
        pieces.append(lax.ppermute(starts[turn], ("tensor", "example", "test"), pairs))
    return pieces


def gathered_features(flat, n_ex, n_cores):
    rows = flat.shape[0]
    part = rows // n_cores
    mine = lax.dynamic_slice_in_dim(flat, lax.axis_index("test") * part, part, 0)
    whole = lax.all_gather(mine, "tensor", axis=1, tiled=True)
    whole = lax.all_to_all(whole, ("example", "test"), split_axis=1, concat_axis=0, tiled=True)
    owners = [lax.rem(lax.axis_index("example") + step, n_ex) for step in range(n_ex)]
    return [lax.dynamic_slice_in_dim(whole, owner * rows, rows, 0) for owner in owners]


def products_kernel(by_rows, n_pieces, n_weights, place_ref, *refs):
    pieces, refs = refs[:n_pieces], refs[n_pieces:]
    weight_refs, refs = refs[:n_weights], refs[n_weights:]
    kept_refs, sent_refs = refs[-1 - 2 * n_weights : -1 : 2], refs[-2 * n_weights : -1 : 2]
    tokens_ref = refs[-1]
    keep = pl.program_id(0) == pl.num_programs(0) - 1

    @pl.when((pl.program_id(0) == 0) & (pl.program_id(1) == 0))
    def _():
        for place, piece in enumerate(pieces):

            @pl.when(place_ref[1] == place)
            def _():
                tokens_ref[...] = piece[...]

    contract = (((1,), (1 if by_rows else 0,)), ((), ()))
    for weight_ref, kept_ref, sent_ref in zip(weight_refs, kept_refs, sent_refs):
        product = lax.dot_general(
            tokens_ref[...], weight_ref[...], contract, preferred_element_type=F32
        )

        @pl.when(keep)
        def _():
            kept_ref[...] = product

        @pl.when(jnp.logical_not(keep))
        def _():
            sent_ref[0] = product


def products(pieces, weights, by_rows, n_cores, *earlier):
    earlier = [token(one) for one in earlier]
    rows, depth = pieces[0].shape
    hidden = weights[0].shape[0 if by_rows else 1] // n_cores
    tile = min(512, hidden)
    tiles = hidden // tile

    def weight_block(turn, i, place_ref):
        block = lax.rem(place_ref[0] + turn + 1, n_cores) * tiles + i
        return (block, 0) if by_rows else (0, block)

    core = lax.axis_index("test")
    holder = lax.axis_index("example") * n_cores + core
    piece = (lax.axis_index("tensor") ^ holder) // 2 if len(pieces) == 2 else 0 * core

    def kept_block(turn, i, place_ref):
        return (0, jnp.where(turn == n_cores - 1, i, 0))

    def sent_block(turn, i, place_ref):
        return (jnp.minimum(turn, n_cores - 2), 0, jnp.where(turn == n_cores - 1, tiles - 1, i))

    outs = pl.pallas_call(
        functools.partial(products_kernel, by_rows, len(pieces), len(weights)),
        out_shape=[
            jax.ShapeDtypeStruct((rows, hidden), F32),
            jax.ShapeDtypeStruct((n_cores - 1, rows, hidden), F32),
        ]
        * len(weights),
        grid_spec=pltpu.PrefetchScalarGridSpec(
            num_scalar_prefetch=1,
            grid=(n_cores, tiles),
            in_specs=[pl.BlockSpec((rows, depth), lambda turn, i, place_ref: (0, 0))] * len(pieces)
            + [pl.BlockSpec((tile, depth) if by_rows else (depth, tile), weight_block)]
            * len(weights)
            + [pl.BlockSpec(memory_space=pl.ANY)] * len(earlier),
            out_specs=[
                pl.BlockSpec((rows, tile), kept_block),
                pl.BlockSpec((1, rows, tile), sent_block),
            ]
            * len(weights),
            scratch_shapes=[pltpu.VMEM((rows, depth), jnp.bfloat16)],
        ),
        compiler_params=pltpu.CompilerParams(vmem_limit_bytes=24 * 2**20),
        cost_estimate=pl.CostEstimate(flops=1, bytes_accessed=1, transcendentals=0),
    )(jnp.stack([core, piece]), *pieces, *weights, *earlier)
    return list(zip(outs[::2], outs[1::2]))


def on_device(
    activations,
    out_grad,
    w_gate,
    w_up,
    w_down,
    proj_model,
    proj_hidden,
    test_grads,
    lengths,
    groups,
):
    ex_loc, seq_len, d_local = activations.shape
    tok_rows = ex_loc * seq_len
    width = proj_model.shape[1] // 3
    n_z = lax.axis_size("tensor")
    n_cores = lax.axis_size("test")
    core = lax.axis_index("test")
    n_ex = lax.axis_size("example")
    ex_index = lax.axis_index("example")
    hid_part = w_gate.shape[1] // n_cores

    def core_swap(product):
        kept, others = product
        packed = [pack(others[step - 1]) for step in range(1, n_cores)]
        got = [shift(sent, "test", step + 1) for step, sent in enumerate(packed)]
        return kept, packed, got

    def core_sum(kept, got):
        return kept + sum(unpack(one) for one in got)

    arrived = [[[] for _ in range(ex_loc)] for _ in range(3)]
    queue = []

    def send(which, e, step, kept, got, *earlier):
        earlier = queue[-2:-1] + list(earlier)
        if earlier:
            kept = after(kept, *earlier)
        sent = pack(core_sum(kept, got))
        queue.append(shift(sent, "example", step))
        arrived[which][e].append(queue[-1])
        return sent

    flat_acts = activations.reshape(tok_rows, d_local)
    flat_grad = out_grad.reshape(tok_rows, d_local)
    model_part = jnp.concatenate(
        [
            jnp.dot(flat_acts, proj_model[:, : 2 * width], preferred_element_type=F32),
            jnp.dot(flat_grad, proj_model[:, 2 * width :], preferred_element_type=F32),
        ],
        1,
    )
    direct = (n_z, n_ex, n_cores) == (4, 2, 2)
    examples = [slice(e * seq_len, (e + 1) * seq_len) for e in range(ex_loc)]
    if direct:
        acts_far = [[direct_features([activations[e]] * 2, 1) for e in range(ex_loc)]]
    else:
        acts_here = gathered_features(flat_acts, n_ex, n_cores)
        grad_here = gathered_features(flat_grad, n_ex, n_cores)
        acts_far = [[[block[rows]] for rows in examples] for block in acts_here[1:]]
    earlier = []
    marks = []
    for e in range(ex_loc):
        for step in range(1, n_ex):
            far = products(acts_far[step - 1][e], (w_gate, w_up), False, n_cores, *earlier)
            swapped = [core_swap(one) for one in far]
            earlier = [packed[-1] for _, packed, _ in swapped]
            marks.append(earlier)
            for which, (kept, _, got) in enumerate(swapped):
                sent = send(which, e, step, kept, got)
    model_sum = lax.psum(after(model_part, marks[0][0]), "tensor")
    if direct:
        start = after(flat_grad, marks[0][1])
        later = after(start, marks[-1][0])
        grad_far = [direct_features([start, later], 1)]
        start = after(flat_acts, marks[-1][1])
        acts_near = direct_features([start, start], 0)
        acts_near = [after(piece, *marks[-1]) for piece in acts_near]
    else:
        grad_far = [[block] for block in grad_here[1:]]
        acts_near = acts_here[:1]
    acts_near = products(acts_near, (w_gate, w_up), False, n_cores, *marks[-1])
    grad_far = [[after(piece, acts_near[0][0]) for piece in pieces] for pieces in grad_far]
    for step in range(1, n_ex):
        (far,) = products(grad_far[step - 1], (w_down,), True, n_cores)
        kept, packed, got = core_swap(far)
        for e, rows in enumerate(examples):
            sent = send(2, e, step, kept[rows], [one[rows] for one in got])
    if direct:
        start = after(flat_grad, acts_near[0][0])
        grad_near = direct_features([start, start], 0)
        grad_near = [after(piece, packed[-1]) for piece in grad_near]
    else:
        grad_near = grad_here[:1]
    (grad_near,) = products(grad_near, (w_down,), True, n_cores, packed[-1])
    model_sum = after(model_sum, grad_near[0])
    own = []
    for near in (*acts_near, grad_near):
        kept, _, got = core_swap(near)
        own.append(lax.optimization_barrier(core_sum(kept, got)))

    def total(which, e):
        kept = own[which][e * seq_len : (e + 1) * seq_len]
        return kept + sum(unpack(one) for one in arrived[which][e])

    hid_proj = lax.dynamic_slice_in_dim(proj_hidden, core * hid_part, hid_part, 0)
    positions = jnp.arange(seq_len, dtype=jnp.int32)
    token_mask = (positions[None, :] < lengths[:, None]).astype(F32)[:, :, None]
    masked = model_sum.reshape(ex_loc, seq_len, 3 * width) * token_mask

    def outer(outputs, inputs):
        product = lax.dot_general(
            outputs, inputs, (((0,), (0,)), ((), ())), precision=lax.Precision.HIGHEST
        )
        return product.reshape(n_z, width // n_z, width)

    factors, hidden_grads = [], []
    for e in range(ex_loc):
        gate_act, up_act = total(0, e), total(1, e)
        sigmoid_gate = jax.nn.sigmoid(gate_act)
        silu_gate = gate_act * sigmoid_gate
        hidden = (silu_gate * up_act).astype(jnp.bfloat16)
        gate_factor = up_act * sigmoid_gate * (1.0 + gate_act * (1.0 - sigmoid_gate))
        factors.append(lax.optimization_barrier((gate_factor, silu_gate)))
        in_hidden = jnp.dot(hidden, hid_proj[:, 2 * width :], preferred_element_type=F32)
        hidden_grads.append(outer(masked[e, :, 2 * width :], in_hidden))
    grads = []
    for e in range(ex_loc):
        d_hidden = total(2, e)
        d_gate = (d_hidden * factors[e][0]).astype(jnp.bfloat16)
        d_up = (d_hidden * factors[e][1]).astype(jnp.bfloat16)
        out_gate = jnp.dot(d_gate, hid_proj[:, :width], preferred_element_type=F32)
        out_up = jnp.dot(d_up, hid_proj[:, width : 2 * width], preferred_element_type=F32)
        grads += [
            outer(out_gate, masked[e, :, :width]),
            outer(out_up, masked[e, :, width : 2 * width]),
            hidden_grads[e],
        ]
    grads = jnp.sum(exchange(jnp.stack(grads, 1), "tensor"), 0)
    grads = share(grads, ("example", "test"), n_ex * n_cores)
    grads = jnp.sum(grads.reshape((n_ex, n_cores) + grads.shape[1:]), 1)
    partial_scores = lax.dot_general(
        grads.reshape(n_ex * ex_loc, -1),
        test_grads.astype(F32).reshape(-1, test_grads.shape[-1]),
        (((1,), (0,)), ((), ())),
        precision=lax.Precision.HIGHEST,
    )
    all_scores = jnp.sum(share(partial_scores, "tensor", n_z), 0)
    scores = lax.dynamic_slice_in_dim(all_scores, ex_index * ex_loc, ex_loc, 0)
    all_groups = [groups] + [shift(groups, "example", step) for step in range(1, n_ex)]
    owners = jnp.stack([lax.rem(ex_index + n_ex - step, n_ex) for step in range(n_ex)])
    all_groups = jnp.zeros((n_ex, ex_loc), jnp.int32).at[owners].set(jnp.stack(all_groups))
    group_onehot = (
        all_groups.reshape(-1)[:, None] == jnp.arange(NGROUP, dtype=jnp.int32)[None, :]
    ).astype(F32)
    group_scores = jnp.dot(group_onehot.T, all_scores, precision=lax.Precision.HIGHEST)
    return (scores, group_scores)


def solution(mesh):
    placed = (
        P(("parts", "example"), None, "tensor"),
        P(("parts", "example"), None, "tensor"),
        P(("example", "test"), "tensor"),
        P(("example", "test"), "tensor"),
        P("tensor", ("example", "test")),
        P("tensor", None),
        P("tensor", None),
        P(None, "tensor", None, "test"),
        P(("parts", "example")),
        P(("parts", "example")),
    )
    return jax.shard_map(
        on_device,
        mesh=mesh,
        in_specs=placed,
        out_specs=(P(("parts", "example"), "test"), P("parts", "test")),
        check_vma=False,
    )
```

```python
import functools

import jax
import jax.numpy as jnp
from jax import lax
from jax.experimental import pallas as pl
from jax.experimental.pallas import tpu as pltpu
from jax.sharding import PartitionSpec as P

NGROUP = 4
F32 = jnp.float32
SEND_SCALE = 16.0


def shift(value, axis, step):
    n = lax.axis_size(axis)
    return lax.ppermute(value, axis, [(i, (i + step) % n) for i in range(n)])


def pack(value):
    return (value * SEND_SCALE).astype(jnp.float16)


def unpack(value):
    return value.astype(F32) * (1.0 / SEND_SCALE)


def in_order(pieces, axis):
    n = len(pieces)
    back = pieces[:0:-1] + pieces[:1]
    return lax.dynamic_slice_in_dim(jnp.stack(back + back), n - 1 - lax.axis_index(axis), n, 0)


def gather_in_order(value, axis):
    n = lax.axis_size(axis)
    if n > 8:
        return lax.all_gather(value, axis, axis=0)
    return in_order([value] + [shift(value, axis, step) for step in range(1, n)], axis)


def scatter_sum(blocks, axis):
    n = lax.axis_size(axis)
    if n > 8:
        return lax.psum_scatter(blocks, axis, scatter_dimension=0, tiled=True)[0]
    me = lax.axis_index(axis)
    total = lax.dynamic_index_in_dim(blocks, me, 0, keepdims=False)
    for step in range(1, n):
        block = lax.dynamic_index_in_dim(blocks, lax.rem(me + step, n), 0, keepdims=False)
        total = total + shift(block, axis, step)
    return total


def token(value):
    corner = value[(0,) * (value.ndim - 2)]
    return corner[:16, :128].astype(F32) if value.dtype == jnp.float16 else value


def after(value, *earlier):
    earlier = [token(one) for one in earlier]
    anywhere = pl.BlockSpec(memory_space=pl.ANY)
    return pl.pallas_call(
        lambda *refs: None,
        out_shape=jax.ShapeDtypeStruct(value.shape, value.dtype),
        in_specs=[anywhere] * (1 + len(earlier)),
        out_specs=anywhere,
        input_output_aliases={0: 0},
        cost_estimate=pl.CostEstimate(flops=1, bytes_accessed=1, transcendentals=0),
    )(value, *earlier)


def spread_features(starts, far, cross):
    pieces = []
    for turn in range(2):
        pairs = []
        for block in range(4):
            example, core = block // 2, block % 2
            for source_core in range(2):
                target = block ^ (2 * turn + (source_core ^ core))
                source = block * 4 + (example ^ far) * 2 + source_core
                landing = example if cross else example ^ far
                pairs.append((source, target * 4 + landing * 2 + core))
        pieces.append(lax.ppermute(starts[turn], ("tensor", "example", "test"), pairs))
    return pieces


def piece_index(across):
    example = lax.axis_index("example") ^ across
    return (lax.axis_index("tensor") ^ (example * 2 + lax.axis_index("test"))) // 2


def gathered_features(flat, n_ex, n_cores):
    rows = flat.shape[0]
    part = rows // n_cores
    mine = lax.dynamic_slice_in_dim(flat, lax.axis_index("test") * part, part, 0)
    whole = lax.all_gather(mine, "tensor", axis=1, tiled=True)
    whole = lax.all_to_all(whole, ("example", "test"), split_axis=1, concat_axis=0, tiled=True)
    owners = [lax.rem(lax.axis_index("example") + step, n_ex) for step in range(n_ex)]
    return [lax.dynamic_slice_in_dim(whole, owner * rows, rows, 0) for owner in owners]


def products_kernel(by_rows, n_pieces, n_weights, place_ref, *refs):
    pieces, refs = refs[:n_pieces], refs[n_pieces:]
    weight_refs, refs = refs[:n_weights], refs[n_weights:]
    kept_refs, sent_refs = refs[-1 - 2 * n_weights : -1 : 2], refs[-2 * n_weights : -1 : 2]
    tokens_ref = refs[-1]
    keep = pl.program_id(0) == pl.num_programs(0) - 1

    @pl.when((pl.program_id(0) == 0) & (pl.program_id(1) == 0))
    def _():
        for place, piece in enumerate(pieces):

            @pl.when(place_ref[1] == place)
            def _():
                tokens_ref[...] = piece[...]

    contract = (((1,), (1 if by_rows else 0,)), ((), ()))
    for weight_ref, kept_ref, sent_ref in zip(weight_refs, kept_refs, sent_refs):
        product = lax.dot_general(
            tokens_ref[...], weight_ref[...], contract, preferred_element_type=F32
        )

        @pl.when(keep)
        def _():
            kept_ref[...] = product

        @pl.when(jnp.logical_not(keep))
        def _():
            sent_ref[0] = product


def products(pieces, weights, by_rows, n_cores, *earlier):
    earlier = [token(one) for one in earlier]
    rows, depth = pieces[0].shape
    hidden = weights[0].shape[0 if by_rows else 1] // n_cores
    tile = min(512, hidden)
    tiles = hidden // tile

    def weight_block(turn, i, place_ref):
        block = lax.rem(place_ref[0] + turn + 1, n_cores) * tiles + i
        return (block, 0) if by_rows else (0, block)

    core = lax.axis_index("test")
    piece = piece_index(0) if len(pieces) == 2 else 0 * core

    def kept_block(turn, i, place_ref):
        return (0, jnp.where(turn == n_cores - 1, i, 0))

    def sent_block(turn, i, place_ref):
        return (jnp.minimum(turn, n_cores - 2), 0, jnp.where(turn == n_cores - 1, tiles - 1, i))

    outs = pl.pallas_call(
        functools.partial(products_kernel, by_rows, len(pieces), len(weights)),
        out_shape=[
            jax.ShapeDtypeStruct((rows, hidden), F32),
            jax.ShapeDtypeStruct((n_cores - 1, rows, hidden), F32),
        ]
        * len(weights),
        grid_spec=pltpu.PrefetchScalarGridSpec(
            num_scalar_prefetch=1,
            grid=(n_cores, tiles),
            in_specs=[pl.BlockSpec((rows, depth), lambda turn, i, place_ref: (0, 0))] * len(pieces)
            + [pl.BlockSpec((tile, depth) if by_rows else (depth, tile), weight_block)]
            * len(weights)
            + [pl.BlockSpec(memory_space=pl.ANY)] * len(earlier),
            out_specs=[
                pl.BlockSpec((rows, tile), kept_block),
                pl.BlockSpec((1, rows, tile), sent_block),
            ]
            * len(weights),
            scratch_shapes=[pltpu.VMEM((rows, depth), jnp.bfloat16)],
        ),
        compiler_params=pltpu.CompilerParams(vmem_limit_bytes=48 * 2**20),
        cost_estimate=pl.CostEstimate(flops=1, bytes_accessed=1, transcendentals=0),
    )(jnp.stack([core, piece]), *pieces, *weights, *earlier)
    return list(zip(outs[::2], outs[1::2]))


def on_device(
    activations,
    out_grad,
    w_gate,
    w_up,
    w_down,
    proj_model,
    proj_hidden,
    test_grads,
    lengths,
    groups,
):
    ex_loc, seq_len, d_local = activations.shape
    tok_rows = ex_loc * seq_len
    width = proj_model.shape[1] // 3
    n_z = lax.axis_size("tensor")
    n_cores = lax.axis_size("test")
    core = lax.axis_index("test")
    n_ex = lax.axis_size("example")
    ex_index = lax.axis_index("example")
    hid_part = w_gate.shape[1] // n_cores

    def core_swap(product):
        kept, others = product
        packed = [pack(others[step - 1]) for step in range(1, n_cores)]
        got = [shift(sent, "test", step + 1) for step, sent in enumerate(packed)]
        return kept, packed, got

    def core_sum(kept, got):
        return kept + sum(unpack(one) for one in got)

    arrived = [[[] for _ in range(ex_loc)] for _ in range(3)]
    queue = []

    def send(which, e, step, kept, got, *earlier):
        earlier = queue[-2:-1] + list(earlier)
        if earlier:
            kept = after(kept, *earlier)
        sent = pack(core_sum(kept, got))
        queue.append(shift(sent, "example", step))
        arrived[which][e].append(queue[-1])
        return sent

    flat_acts = activations.reshape(tok_rows, d_local)
    flat_grad = out_grad.reshape(tok_rows, d_local)
    model_part = jnp.concatenate(
        [
            jnp.dot(flat_acts, proj_model[:, : 2 * width], preferred_element_type=F32),
            jnp.dot(flat_grad, proj_model[:, 2 * width :], preferred_element_type=F32),
        ],
        1,
    )
    direct = (n_z, n_ex, n_cores) == (4, 2, 2)
    examples = [slice(e * seq_len, (e + 1) * seq_len) for e in range(ex_loc)]
    if direct:
        starts = [activations[0]] + [after(one, model_part) for one in activations[1:]]
        acts_far = [[spread_features([start, start], 1, True) for start in starts]]
    else:
        acts_here = gathered_features(flat_acts, n_ex, n_cores)
        grad_here = gathered_features(flat_grad, n_ex, n_cores)
        acts_far = [[[block[rows]] for rows in examples] for block in acts_here[1:]]
    earlier, marks = [], []
    for e in range(ex_loc):
        for step in range(1, n_ex):
            sent = []
            for which, weight in enumerate((w_gate, w_up)):
                pieces = acts_far[step - 1][e]
                (far,) = products(pieces, (weight,), False, n_cores, *earlier)
                kept, packed, got = core_swap(far)
                sent.append(send(which, e, step, kept, got))
                earlier = earlier[-1:] + [packed[-1]]
            earlier = [earlier[-1]] + sent[:1]
            marks.append(sent)
    model_sum = lax.psum(after(model_part, marks[0][0]), "tensor")
    if direct:
        start = after(flat_grad, marks[0][1])
        pieces = spread_features([start, start], 1, False)
        pieces = [after(piece, marks[-1][0]) for piece in pieces]
        grad_far = [[shift(jnp.where(piece_index(1) == 0, *pieces), "example", 1)]]
        start = after(flat_acts, marks[-1][0])
        acts_near = spread_features([start, start], 0, False)
    else:
        grad_far = [[block] for block in grad_here[1:]]
        acts_near = acts_here[:1]
    for step in range(1, n_ex):
        (far,) = products(grad_far[step - 1], (w_down,), True, n_cores, *marks[-1])
        kept, packed, got = core_swap(far)
        for e, rows in enumerate(examples):
            sent = send(2, e, step, kept[rows], [one[rows] for one in got])
    if direct:
        acts_near = [after(piece, packed[-1]) for piece in acts_near]
    acts_near = products(acts_near, (w_gate, w_up), False, n_cores)
    if direct:
        start = after(flat_grad, acts_near[0][0])
        grad_near = spread_features([start, start], 0, False)
    else:
        grad_near = grad_here[:1]
    (grad_near,) = products(grad_near, (w_down,), True, n_cores, sent)
    model_sum = after(model_sum, grad_near[0])
    own = []
    for near in (*acts_near, grad_near):
        kept, _, got = core_swap(near)
        own.append(lax.optimization_barrier(core_sum(kept, got)))

    def total(which, e):
        kept = own[which][e * seq_len : (e + 1) * seq_len]
        return kept + sum(unpack(one) for one in arrived[which][e])

    hid_proj = lax.dynamic_slice_in_dim(proj_hidden, core * hid_part, hid_part, 0)
    positions = jnp.arange(seq_len, dtype=jnp.int32)
    token_mask = (positions[None, :] < lengths[:, None]).astype(F32)[:, :, None]
    masked = model_sum.reshape(ex_loc, seq_len, 3 * width) * token_mask

    def outer(outputs, inputs):
        product = lax.dot_general(
            outputs, inputs, (((0,), (0,)), ((), ())), precision=lax.Precision.HIGHEST
        )
        return product.reshape(n_z, width // n_z, width)

    factors, hidden_grads = [], []
    for e in range(ex_loc):
        gate_act, up_act = total(0, e), total(1, e)
        sigmoid_gate = jax.nn.sigmoid(gate_act)
        silu_gate = gate_act * sigmoid_gate
        hidden = (silu_gate * up_act).astype(jnp.bfloat16)
        gate_factor = up_act * sigmoid_gate * (1.0 + gate_act * (1.0 - sigmoid_gate))
        factors.append(lax.optimization_barrier((gate_factor, silu_gate)))
        in_hidden = jnp.dot(hidden, hid_proj[:, 2 * width :], preferred_element_type=F32)
        hidden_grads.append(outer(masked[e, :, 2 * width :], in_hidden))
    grads = []
    for e in range(ex_loc):
        d_hidden = total(2, e)
        d_gate = (d_hidden * factors[e][0]).astype(jnp.bfloat16)
        d_up = (d_hidden * factors[e][1]).astype(jnp.bfloat16)
        out_gate = jnp.dot(d_gate, hid_proj[:, :width], preferred_element_type=F32)
        out_up = jnp.dot(d_up, hid_proj[:, width : 2 * width], preferred_element_type=F32)
        grads += [
            outer(out_gate, masked[e, :, :width]),
            outer(out_up, masked[e, :, width : 2 * width]),
            hidden_grads[e],
        ]
    grads = scatter_sum(jnp.stack(grads, 1), "tensor")
    by_example = []
    for ex_step in range(n_ex):
        total = 0.0
        for core_step in range(n_cores):
            piece = grads
            if ex_step or core_step:
                pairs = [
                    (i * n_cores + c, (i + ex_step) % n_ex * n_cores + (c + core_step) % n_cores)
                    for i in range(n_ex)
                    for c in range(n_cores)
                ]
                piece = lax.ppermute(piece, ("example", "test"), pairs)
            total = total + piece
        by_example.append(total)
    grads = in_order(by_example, "example")
    partial_scores = lax.dot_general(
        grads.reshape(n_ex * ex_loc, -1),
        test_grads.astype(F32).reshape(-1, test_grads.shape[-1]),
        (((1,), (0,)), ((), ())),
        precision=lax.Precision.HIGHEST,
    )
    all_scores = jnp.sum(gather_in_order(partial_scores, "tensor"), 0)
    scores = lax.dynamic_slice_in_dim(all_scores, ex_index * ex_loc, ex_loc, 0)
    all_groups = gather_in_order(groups, "example")
    group_onehot = (
        all_groups.reshape(-1)[:, None] == jnp.arange(NGROUP, dtype=jnp.int32)[None, :]
    ).astype(F32)
    group_scores = jnp.dot(group_onehot.T, all_scores, precision=lax.Precision.HIGHEST)
    return (scores, group_scores)


def solution(mesh):
    placed = (
        P(("parts", "example"), None, "tensor"),
        P(("parts", "example"), None, "tensor"),
        P(("example", "test"), "tensor"),
        P(("example", "test"), "tensor"),
        P("tensor", ("example", "test")),
        P("tensor", None),
        P("tensor", None),
        P(None, "tensor", None, "test"),
        P(("parts", "example")),
        P(("parts", "example")),
    )
    return jax.shard_map(
        on_device,
        mesh=mesh,
        in_specs=placed,
        out_specs=(P(("parts", "example"), "test"), P("parts", "test")),
        check_vma=False,
    )
```

```python
import functools

import jax
import jax.numpy as jnp
from jax import lax
from jax.experimental import pallas as pl
from jax.experimental.pallas import tpu as pltpu
from jax.sharding import PartitionSpec as P

NGROUP = 4
F32 = jnp.float32
SEND_SCALE = 16.0


def shift(value, axis, step):
    n = lax.axis_size(axis)
    return lax.ppermute(value, axis, [(i, (i + step) % n) for i in range(n)])


def pack(value):
    return (value * SEND_SCALE).astype(jnp.float16)


def unpack(value):
    return value.astype(F32) * (1.0 / SEND_SCALE)


def in_order(pieces, axis):
    n = len(pieces)
    back = pieces[:0:-1] + pieces[:1]
    return lax.dynamic_slice_in_dim(jnp.stack(back + back), n - 1 - lax.axis_index(axis), n, 0)


def gather_in_order(value, axis):
    n = lax.axis_size(axis)
    if n > 8:
        return lax.all_gather(value, axis, axis=0)
    return in_order([value] + [shift(value, axis, step) for step in range(1, n)], axis)


def scatter_sum(blocks, axis):
    n = lax.axis_size(axis)
    if n > 8:
        return lax.psum_scatter(blocks, axis, scatter_dimension=0, tiled=True)[0]
    me = lax.axis_index(axis)
    total = lax.dynamic_index_in_dim(blocks, me, 0, keepdims=False)
    for step in range(1, n):
        block = lax.dynamic_index_in_dim(blocks, lax.rem(me + step, n), 0, keepdims=False)
        total = total + shift(block, axis, step)
    return total


def after(value, *earlier):
    anywhere = pl.BlockSpec(memory_space=pl.ANY)
    return pl.pallas_call(
        lambda *refs: None,
        out_shape=jax.ShapeDtypeStruct(value.shape, value.dtype),
        in_specs=[anywhere] * (1 + len(earlier)),
        out_specs=anywhere,
        input_output_aliases={0: 0},
        cost_estimate=pl.CostEstimate(flops=1, bytes_accessed=1, transcendentals=0),
    )(value, *earlier)


def spread_features(starts, far, cross):
    pieces = []
    for turn in range(2):
        pairs = []
        for block in range(4):
            example, core = block // 2, block % 2
            for source_core in range(2):
                target = block ^ (2 * turn + (source_core ^ core))
                source = block * 4 + (example ^ far) * 2 + source_core
                landing = example if cross else example ^ far
                pairs.append((source, target * 4 + landing * 2 + core))
        pieces.append(lax.ppermute(starts[turn], ("tensor", "example", "test"), pairs))
    return pieces


def piece_index(across):
    example = lax.axis_index("example") ^ across
    return (lax.axis_index("tensor") ^ (example * 2 + lax.axis_index("test"))) // 2


def gathered_features(flat, n_ex, n_cores):
    rows = flat.shape[0]
    part = rows // n_cores
    mine = lax.dynamic_slice_in_dim(flat, lax.axis_index("test") * part, part, 0)
    whole = lax.all_gather(mine, "tensor", axis=1, tiled=True)
    whole = lax.all_to_all(whole, ("example", "test"), split_axis=1, concat_axis=0, tiled=True)
    owners = [lax.rem(lax.axis_index("example") + step, n_ex) for step in range(n_ex)]
    return [lax.dynamic_slice_in_dim(whole, owner * rows, rows, 0) for owner in owners]


def products_kernel(by_rows, tokens_ref, *refs):
    contract = (((1,), (1 if by_rows else 0,)), ((), ()))
    for weight_ref, out_ref in zip(refs, refs[len(refs) // 2 :]):
        out_ref[...] = lax.dot_general(
            tokens_ref[...], weight_ref[...], contract, preferred_element_type=F32
        )


def products(tokens, weights, by_rows, vmem_mib):
    rows, depth = tokens.shape
    hidden = weights[0].shape[0 if by_rows else 1]
    tile = min(512, hidden)
    block = ((tile, depth), lambda i: (i, 0)) if by_rows else ((depth, tile), lambda i: (0, i))
    return pl.pallas_call(
        functools.partial(products_kernel, by_rows),
        out_shape=[jax.ShapeDtypeStruct((rows, hidden), F32)] * len(weights),
        grid=(hidden // tile,),
        in_specs=[pl.BlockSpec((rows, depth), lambda i: (0, 0))]
        + [pl.BlockSpec(*block)] * len(weights),
        out_specs=[pl.BlockSpec((rows, tile), lambda i: (0, i))] * len(weights),
        compiler_params=pltpu.CompilerParams(vmem_limit_bytes=vmem_mib * 2**20),
        cost_estimate=pl.CostEstimate(flops=1, bytes_accessed=1, transcendentals=0),
    )(tokens, *weights)


def on_device(
    activations,
    out_grad,
    w_gate,
    w_up,
    w_down,
    proj_model,
    proj_hidden,
    test_grads,
    lengths,
    groups,
):
    ex_loc, seq_len, d_local = activations.shape
    tok_rows = ex_loc * seq_len
    width = proj_model.shape[1] // 3
    n_z = lax.axis_size("tensor")
    n_cores = lax.axis_size("test")
    core = lax.axis_index("test")
    n_ex = lax.axis_size("example")
    ex_index = lax.axis_index("example")
    hid_part = w_gate.shape[1] // n_cores

    def forward(tokens, weight):
        return jnp.dot(tokens, weight, preferred_element_type=F32)

    def core_sum(product):
        kept = lax.dynamic_slice_in_dim(product, core * hid_part, hid_part, 1)
        for step in range(1, n_cores):
            to = lax.rem(core + step, n_cores)
            sent = pack(lax.dynamic_slice_in_dim(product, to * hid_part, hid_part, 1))
            kept = kept + unpack(shift(sent, "test", step))
        return kept

    flat_acts = activations.reshape(tok_rows, d_local)
    flat_grad = out_grad.reshape(tok_rows, d_local)
    model_part = jnp.concatenate(
        [
            jnp.dot(flat_acts, proj_model[:, : 2 * width], preferred_element_type=F32),
            jnp.dot(flat_grad, proj_model[:, 2 * width :], preferred_element_type=F32),
        ],
        1,
    )

    direct = (n_z, n_ex, n_cores) == (4, 2, 2)
    examples = [slice(e * seq_len, (e + 1) * seq_len) for e in range(ex_loc)]
    arrived = [[[] for _ in range(ex_loc)] for _ in range(3)]
    if direct:
        acts_far = spread_features([flat_acts] * 2, 1, True)
        acts_far = [jnp.where(piece_index(0) == 0, after(acts_far[0], model_part), acts_far[1])]
        grad_across = spread_features([flat_grad] * 2, 1, False)
    else:
        acts_here = gathered_features(flat_acts, n_ex, n_cores)
        grad_here = gathered_features(flat_grad, n_ex, n_cores)
        acts_far, grad_far = acts_here[1:], grad_here[1:]
    for step in range(1, n_ex):
        gate_far = forward(acts_far[step - 1], w_gate)
        up_far = forward(after(acts_far[step - 1], gate_far), w_up)
        if direct:
            grad_across = [after(piece, gate_far) for piece in grad_across]
            grad_far = [shift(jnp.where(piece_index(1) == 0, *grad_across), "example", 1)]
        both = jnp.stack([core_sum(gate_far), core_sum(up_far)])
        received = unpack(shift(pack(both), "example", step))
        for e, rows in enumerate(examples):
            for which in range(2):
                arrived[which][e].append(received[which, rows])
        (down_far,) = products(after(grad_far[step - 1], both), [w_down], True, 16)
        summed = core_sum(down_far)
        for e, rows in enumerate(examples):
            arrived[2][e].append(unpack(shift(pack(summed[rows]), "example", step)))
    model_sum = lax.psum(after(model_part, gate_far), "tensor")
    if direct:
        start = after(flat_acts, summed)
        acts_near = spread_features([start, start], 0, False)
        acts_near = jnp.where(piece_index(0) == 0, *acts_near)
        start = after(flat_grad, acts_near)
        grad_near = spread_features([start, start], 0, False)
    else:
        acts_near, grad_near = acts_here[0], grad_here[0]
    (gate_near,) = products(acts_near, [w_gate], False, 48)
    (up_near,) = products(after(acts_near, received), [w_up], False, 48)
    if direct:
        grad_near = [after(piece, gate_near) for piece in grad_near]
        grad_near = jnp.where(piece_index(0) == 0, *grad_near)
    (grad_near,) = products(grad_near, [w_down], True, 48)
    model_sum = after(model_sum, grad_near)
    own = [core_sum(near) for near in (gate_near, up_near, grad_near)]

    def total(which, e):
        kept = own[which][e * seq_len : (e + 1) * seq_len]
        return kept + sum(arrived[which][e])

    hid_proj = lax.dynamic_slice_in_dim(proj_hidden, core * hid_part, hid_part, 0)
    positions = jnp.arange(seq_len, dtype=jnp.int32)
    token_mask = (positions[None, :] < lengths[:, None]).astype(F32)[:, :, None]
    masked = model_sum.reshape(ex_loc, seq_len, 3 * width) * token_mask

    def outer(outputs, inputs):
        product = lax.dot_general(
            outputs, inputs, (((0,), (0,)), ((), ())), precision=lax.Precision.HIGHEST
        )
        return product.reshape(n_z, width // n_z, width)

    factors, hidden_grads = [], []
    for e in range(ex_loc):
        gate_act, up_act = total(0, e), total(1, e)
        sigmoid_gate = jax.nn.sigmoid(gate_act)
        silu_gate = gate_act * sigmoid_gate
        hidden = (silu_gate * up_act).astype(jnp.bfloat16)
        gate_factor = up_act * sigmoid_gate * (1.0 + gate_act * (1.0 - sigmoid_gate))
        factors.append(lax.optimization_barrier((gate_factor, silu_gate)))
        in_hidden = jnp.dot(hidden, hid_proj[:, 2 * width :], preferred_element_type=F32)
        hidden_grads.append(outer(masked[e, :, 2 * width :], in_hidden))
    grads = []
    for e in range(ex_loc):
        d_hidden = total(2, e)
        d_gate = (d_hidden * factors[e][0]).astype(jnp.bfloat16)
        d_up = (d_hidden * factors[e][1]).astype(jnp.bfloat16)
        out_gate = jnp.dot(d_gate, hid_proj[:, :width], preferred_element_type=F32)
        out_up = jnp.dot(d_up, hid_proj[:, width : 2 * width], preferred_element_type=F32)
        grads += [
            outer(out_gate, masked[e, :, :width]),
            outer(out_up, masked[e, :, width : 2 * width]),
            hidden_grads[e],
        ]
    grads = scatter_sum(jnp.stack(grads, 1), "tensor")
    by_example = []
    for ex_step in range(n_ex):
        total = 0.0
        for core_step in range(n_cores):
            piece = grads
            if ex_step or core_step:
                pairs = [
                    (i * n_cores + c, (i + ex_step) % n_ex * n_cores + (c + core_step) % n_cores)
                    for i in range(n_ex)
                    for c in range(n_cores)
                ]
                piece = lax.ppermute(piece, ("example", "test"), pairs)
            total = total + piece
        by_example.append(total)
    grads = in_order(by_example, "example")
    partial_scores = lax.dot_general(
        grads.reshape(n_ex * ex_loc, -1),
        test_grads.astype(F32).reshape(-1, test_grads.shape[-1]),
        (((1,), (0,)), ((), ())),
        precision=lax.Precision.HIGHEST,
    )
    all_scores = jnp.sum(gather_in_order(partial_scores, "tensor"), 0)
    scores = lax.dynamic_slice_in_dim(all_scores, ex_index * ex_loc, ex_loc, 0)
    all_groups = gather_in_order(groups, "example")
    group_onehot = (
        all_groups.reshape(-1)[:, None] == jnp.arange(NGROUP, dtype=jnp.int32)[None, :]
    ).astype(F32)
    group_scores = jnp.dot(group_onehot.T, all_scores, precision=lax.Precision.HIGHEST)
    return (scores, group_scores)


def solution(mesh):
    placed = (
        P(("parts", "example"), None, "tensor"),
        P(("parts", "example"), None, "tensor"),
        P(("example", "test"), "tensor"),
        P(("example", "test"), "tensor"),
        P("tensor", ("example", "test")),
        P("tensor", None),
        P("tensor", None),
        P(None, "tensor", None, "test"),
        P(("parts", "example")),
        P(("parts", "example")),
    )
    return jax.shard_map(
        on_device,
        mesh=mesh,
        in_specs=placed,
        out_specs=(P(("parts", "example"), "test"), P("parts", "test")),
        check_vma=False,
    )
```

```python
import jax
import jax.numpy as jnp
from jax import lax
from jax.experimental import pallas as pl
from jax.experimental.pallas import tpu as pltpu
from jax.sharding import PartitionSpec as P

NGROUP = 4
F32 = jnp.float32
SEND_SCALE = 16.0


def shift(value, axis, step):
    n = lax.axis_size(axis)
    return lax.ppermute(value, axis, [(i, (i + step) % n) for i in range(n)])


def pack(value):
    return (value * SEND_SCALE).astype(jnp.float16)


def unpack(value):
    return value.astype(F32) * (1.0 / SEND_SCALE)


def in_order(pieces, axis):
    n = len(pieces)
    back = pieces[:0:-1] + pieces[:1]
    return lax.dynamic_slice_in_dim(jnp.stack(back + back), n - 1 - lax.axis_index(axis), n, 0)


def gather_in_order(value, axis):
    n = lax.axis_size(axis)
    if n > 8:
        return lax.all_gather(value, axis, axis=0)
    return in_order([value] + [shift(value, axis, step) for step in range(1, n)], axis)


def scatter_sum(blocks, axis):
    n = lax.axis_size(axis)
    if n > 8:
        return lax.psum_scatter(blocks, axis, scatter_dimension=0, tiled=True)[0]
    me = lax.axis_index(axis)
    total = lax.dynamic_index_in_dim(blocks, me, 0, keepdims=False)
    for step in range(1, n):
        block = lax.dynamic_index_in_dim(blocks, lax.rem(me + step, n), 0, keepdims=False)
        total = total + shift(block, axis, step)
    return total


def after(value, *earlier):
    return lax.optimization_barrier((value,) + earlier)[0]


def spread_features(flat, far, *earlier):
    pieces = []
    for turn in range(2):
        pairs = []
        for block in range(4):
            example, core = block // 2, block % 2
            for source_core in range(2):
                target = block ^ (2 * turn + (source_core ^ core))
                source = block * 4 + (example ^ far) * 2 + source_core
                pairs.append((source, target * 4 + example * 2 + core))
        pieces.append(lax.ppermute(flat, ("tensor", "example", "test"), pairs))
    if earlier:
        pieces = lax.optimization_barrier((*pieces, *earlier))
    holder = lax.axis_index("example") * 2 + lax.axis_index("test")
    return jnp.where((lax.axis_index("tensor") ^ holder) < 2, pieces[0], pieces[1])


def gathered_features(flat, n_ex, n_cores):
    rows = flat.shape[0]
    part = rows // n_cores
    mine = lax.dynamic_slice_in_dim(flat, lax.axis_index("test") * part, part, 0)
    whole = lax.all_gather(mine, "tensor", axis=1, tiled=True)
    whole = lax.all_to_all(whole, ("example", "test"), split_axis=1, concat_axis=0, tiled=True)
    owners = [lax.rem(lax.axis_index("example") + step, n_ex) for step in range(n_ex)]
    return [lax.dynamic_slice_in_dim(whole, owner * rows, rows, 0) for owner in owners]


def dot_rows_kernel(tokens_ref, weight_ref, out_ref):
    out_ref[...] = lax.dot_general(
        tokens_ref[...], weight_ref[...], (((1,), (1,)), ((), ())), preferred_element_type=F32
    )


def dot_rows(tokens, weight):
    rows, depth = tokens.shape
    hidden = weight.shape[0]
    tile = min(512, hidden)
    return pl.pallas_call(
        dot_rows_kernel,
        out_shape=jax.ShapeDtypeStruct((rows, hidden), F32),
        grid=(hidden // tile,),
        in_specs=[
            pl.BlockSpec((rows, depth), lambda i: (0, 0)),
            pl.BlockSpec((tile, depth), lambda i: (i, 0)),
        ],
        out_specs=pl.BlockSpec((rows, tile), lambda i: (0, i)),
        compiler_params=pltpu.CompilerParams(vmem_limit_bytes=16 * 2**20),
        cost_estimate=pl.CostEstimate(flops=1, bytes_accessed=1, transcendentals=0),
    )(tokens, weight)


def on_device(
    activations,
    out_grad,
    w_gate,
    w_up,
    w_down,
    proj_model,
    proj_hidden,
    test_grads,
    lengths,
    groups,
):
    ex_loc, seq_len, d_local = activations.shape
    tok_rows = ex_loc * seq_len
    width = proj_model.shape[1] // 3
    n_z = lax.axis_size("tensor")
    n_cores = lax.axis_size("test")
    core = lax.axis_index("test")
    n_ex = lax.axis_size("example")
    ex_index = lax.axis_index("example")
    hid_part = w_gate.shape[1] // n_cores

    def forward(tokens, weight):
        return jnp.dot(tokens, weight, preferred_element_type=F32)

    def core_sum(product):
        kept = lax.dynamic_slice_in_dim(product, core * hid_part, hid_part, 1)
        for step in range(1, n_cores):
            to = lax.rem(core + step, n_cores)
            sent = pack(lax.dynamic_slice_in_dim(product, to * hid_part, hid_part, 1))
            kept = kept + unpack(shift(sent, "test", step))
        return kept

    flat_acts = activations.reshape(tok_rows, d_local)
    flat_grad = out_grad.reshape(tok_rows, d_local)
    model_part = jnp.concatenate(
        [
            jnp.dot(flat_acts, proj_model[:, : 2 * width], preferred_element_type=F32),
            jnp.dot(flat_grad, proj_model[:, 2 * width :], preferred_element_type=F32),
        ],
        1,
    )

    direct = (n_z, n_ex, n_cores) == (4, 2, 2)
    examples = [slice(e * seq_len, (e + 1) * seq_len) for e in range(ex_loc)]
    arrived = [[[] for _ in range(ex_loc)] for _ in range(3)]
    if direct:
        acts_far = [spread_features(flat_acts, 1)]
    else:
        acts_near, *acts_far = gathered_features(flat_acts, n_ex, n_cores)
        grad_near, *grad_far = gathered_features(flat_grad, n_ex, n_cores)
    for step in range(1, n_ex):
        gate_far = forward(acts_far[step - 1], w_gate)
        up_far = forward(after(acts_far[step - 1], gate_far), w_up)
        both = pack(jnp.stack([core_sum(gate_far), core_sum(up_far)]))
        received = shift(both, "example", step)
        for e, rows in enumerate(examples):
            for which in range(2):
                arrived[which][e].append(received[which, rows])
    if direct:
        acts_near = spread_features(flat_acts, 0, up_far)
    gate_near = forward(after(acts_near, both), w_gate)
    up_near = forward(after(acts_near, gate_near), w_up)
    if direct:
        grad_ready = after(flat_grad, acts_far[0])
        grad_far = [spread_features(grad_ready, 1, up_near)]
    for step in range(1, n_ex):
        down_far = dot_rows(grad_far[step - 1], w_down)
        summed = core_sum(down_far)
        for e, rows in enumerate(examples):
            sent = pack(summed[rows])
            arrived[2][e].append(shift(sent, "example", step))
    if direct:
        grad_near = spread_features(grad_ready, 0, sent)
    grad_near = dot_rows(grad_near, w_down)
    model_sum = lax.psum(after(model_part, acts_far[0]), "tensor")
    model_sum = after(model_sum, grad_near)
    own = [core_sum(near) for near in (gate_near, up_near, grad_near)]

    def total(which, e):
        kept = own[which][e * seq_len : (e + 1) * seq_len]
        return kept + sum(unpack(one) for one in arrived[which][e])

    hid_proj = lax.dynamic_slice_in_dim(proj_hidden, core * hid_part, hid_part, 0)
    positions = jnp.arange(seq_len, dtype=jnp.int32)
    token_mask = (positions[None, :] < lengths[:, None]).astype(F32)[:, :, None]
    masked = model_sum.reshape(ex_loc, seq_len, 3 * width) * token_mask

    def outer(outputs, inputs):
        product = lax.dot_general(
            outputs, inputs, (((0,), (0,)), ((), ())), precision=lax.Precision.HIGHEST
        )
        return product.reshape(n_z, width // n_z, width)

    factors, hidden_grads = [], []
    for e in range(ex_loc):
        gate_act, up_act = total(0, e), total(1, e)
        sigmoid_gate = jax.nn.sigmoid(gate_act)
        silu_gate = gate_act * sigmoid_gate
        hidden = (silu_gate * up_act).astype(jnp.bfloat16)
        gate_factor = up_act * sigmoid_gate * (1.0 + gate_act * (1.0 - sigmoid_gate))
        factors.append(lax.optimization_barrier((gate_factor, silu_gate)))
        in_hidden = jnp.dot(hidden, hid_proj[:, 2 * width :], preferred_element_type=F32)
        hidden_grads.append(outer(masked[e, :, 2 * width :], in_hidden))
    grads = []
    for e in range(ex_loc):
        d_hidden = total(2, e)
        d_gate = (d_hidden * factors[e][0]).astype(jnp.bfloat16)
        d_up = (d_hidden * factors[e][1]).astype(jnp.bfloat16)
        out_gate = jnp.dot(d_gate, hid_proj[:, :width], preferred_element_type=F32)
        out_up = jnp.dot(d_up, hid_proj[:, width : 2 * width], preferred_element_type=F32)
        grads += [
            outer(out_gate, masked[e, :, :width]),
            outer(out_up, masked[e, :, width : 2 * width]),
            hidden_grads[e],
        ]
    grads = scatter_sum(jnp.stack(grads, 1), "tensor")
    by_example = []
    for ex_step in range(n_ex):
        total = 0.0
        for core_step in range(n_cores):
            piece = grads
            if ex_step or core_step:
                pairs = [
                    (i * n_cores + c, (i + ex_step) % n_ex * n_cores + (c + core_step) % n_cores)
                    for i in range(n_ex)
                    for c in range(n_cores)
                ]
                piece = lax.ppermute(piece, ("example", "test"), pairs)
            total = total + piece
        by_example.append(total)
    grads = in_order(by_example, "example")
    partial_scores = lax.dot_general(
        grads.reshape(n_ex * ex_loc, -1),
        test_grads.astype(F32).reshape(-1, test_grads.shape[-1]),
        (((1,), (0,)), ((), ())),
        precision=lax.Precision.HIGHEST,
    )
    all_scores = jnp.sum(gather_in_order(partial_scores, "tensor"), 0)
    scores = lax.dynamic_slice_in_dim(all_scores, ex_index * ex_loc, ex_loc, 0)
    all_groups = gather_in_order(groups, "example")
    group_onehot = (
        all_groups.reshape(-1)[:, None] == jnp.arange(NGROUP, dtype=jnp.int32)[None, :]
    ).astype(F32)
    group_scores = jnp.dot(group_onehot.T, all_scores, precision=lax.Precision.HIGHEST)
    return (scores, group_scores)


def solution(mesh):
    placed = (
        P(("parts", "example"), None, "tensor"),
        P(("parts", "example"), None, "tensor"),
        P(("example", "test"), "tensor"),
        P(("example", "test"), "tensor"),
        P("tensor", ("example", "test")),
        P("tensor", None),
        P("tensor", None),
        P(None, "tensor", None, "test"),
        P(("parts", "example")),
        P(("parts", "example")),
    )
    return jax.shard_map(
        on_device,
        mesh=mesh,
        in_specs=placed,
        out_specs=(P(("parts", "example"), "test"), P("parts", "test")),
        check_vma=False,
    )
```

```python
import jax
import jax.numpy as jnp
from jax import lax
from jax.experimental import pallas as pl
from jax.experimental.pallas import tpu as pltpu
from jax.sharding import PartitionSpec as P

NGROUP = 4
F32 = jnp.float32
SEND_SCALE = 16.0


def shift(value, axis, step):
    n = lax.axis_size(axis)
    return lax.ppermute(value, axis, [(i, (i + step) % n) for i in range(n)])


def pack(value):
    return (value * SEND_SCALE).astype(jnp.float16)


def unpack(value):
    return value.astype(F32) * (1.0 / SEND_SCALE)


def in_order(pieces, axis):
    n = len(pieces)
    back = pieces[:0:-1] + pieces[:1]
    return lax.dynamic_slice_in_dim(jnp.stack(back + back), n - 1 - lax.axis_index(axis), n, 0)


def gather_in_order(value, axis):
    n = lax.axis_size(axis)
    if n > 8:
        return lax.all_gather(value, axis, axis=0)
    return in_order([value] + [shift(value, axis, step) for step in range(1, n)], axis)


def scatter_sum(blocks, axis):
    n = lax.axis_size(axis)
    if n > 8:
        return lax.psum_scatter(blocks, axis, scatter_dimension=0, tiled=True)[0]
    me = lax.axis_index(axis)
    total = lax.dynamic_index_in_dim(blocks, me, 0, keepdims=False)
    for step in range(1, n):
        block = lax.dynamic_index_in_dim(blocks, lax.rem(me + step, n), 0, keepdims=False)
        total = total + shift(block, axis, step)
    return total


def after(value, *earlier):
    return lax.optimization_barrier((value,) + earlier)[0]


def spread_features(flat, far):
    pieces = []
    for turn in range(2):
        pairs = []
        for block in range(4):
            example, core = block // 2, block % 2
            for source_core in range(2):
                target = block ^ (2 * turn + (source_core ^ core))
                source = block * 4 + (example ^ far) * 2 + source_core
                pairs.append((source, target * 4 + example * 2 + core))
        pieces.append(lax.ppermute(flat, ("tensor", "example", "test"), pairs))
    return pieces


def arrived_features(far, near, *earlier):
    pieces = lax.optimization_barrier((*far, *near, *earlier))[:4]
    holder = lax.axis_index("example") * 2 + lax.axis_index("test")
    first = (lax.axis_index("tensor") ^ holder) < 2
    return jnp.concatenate(
        [jnp.where(first, pieces[0], pieces[1]), jnp.where(first, pieces[2], pieces[3])]
    )


def gathered_features(flat, n_ex, n_cores):
    rows = flat.shape[0]
    part = rows // n_cores
    mine = lax.dynamic_slice_in_dim(flat, lax.axis_index("test") * part, part, 0)
    whole = lax.all_gather(mine, "tensor", axis=1, tiled=True)
    whole = lax.all_to_all(whole, ("example", "test"), split_axis=1, concat_axis=0, tiled=True)
    begin = lax.rem(lax.axis_index("example") + 1, n_ex) * rows
    return lax.dynamic_slice_in_dim(jnp.concatenate([whole, whole]), begin, n_ex * rows, 0)


def dot_rows_kernel(tokens_ref, weight_ref, out_ref):
    out_ref[...] = lax.dot_general(
        tokens_ref[...], weight_ref[...], (((1,), (1,)), ((), ())), preferred_element_type=F32
    )


def dot_rows(tokens, weight):
    rows, depth = tokens.shape
    hidden = weight.shape[0]
    tile = min(512, hidden)
    return pl.pallas_call(
        dot_rows_kernel,
        out_shape=jax.ShapeDtypeStruct((rows, hidden), F32),
        grid=(hidden // tile,),
        in_specs=[
            pl.BlockSpec((rows, depth), lambda i: (0, 0)),
            pl.BlockSpec((tile, depth), lambda i: (i, 0)),
        ],
        out_specs=pl.BlockSpec((rows, tile), lambda i: (0, i)),
        compiler_params=pltpu.CompilerParams(vmem_limit_bytes=16 * 2**20),
        cost_estimate=pl.CostEstimate(flops=1, bytes_accessed=1, transcendentals=0),
    )(tokens, weight)


def gradients_kernel(down_ref, *refs):
    factor_refs, proj_refs, (model_ref, hidden_ref, out_ref) = refs[:2], refs[2:4], refs[4:]
    n_z, _, share, width = out_ref.shape
    ex_loc, seq_len, _ = model_ref.shape
    hidden = down_ref.shape[1]
    chunk = min(512, hidden)
    for layer in range(2):
        outputs = jnp.zeros((ex_loc * seq_len, width), F32)
        for begin in range(0, hidden, chunk):
            part = pl.ds(begin, chunk)
            rounded = (down_ref[:, part] * factor_refs[layer][:, part]).astype(jnp.bfloat16)
            outputs += jnp.dot(rounded, proj_refs[layer][part, :], preferred_element_type=F32)
        for e in range(ex_loc):
            grad = lax.dot_general(
                outputs[e * seq_len : (e + 1) * seq_len],
                model_ref[e, :, layer * width : (layer + 1) * width],
                (((0,), (0,)), ((), ())),
                precision=lax.Precision.HIGHEST,
                preferred_element_type=F32,
            )
            for z in range(n_z):
                out_ref[z, 3 * e + layer] = grad[z * share : (z + 1) * share]
    for e in range(ex_loc):
        out_ref[:, 3 * e + 2] = hidden_ref[e]


def gradients(d_hidden, factors, hid_proj, model, hidden_grads, n_z):
    width = hid_proj.shape[1] // 3
    rows, hidden = d_hidden.shape
    ex_loc = model.shape[0]
    projs = [hid_proj[:, :width], hid_proj[:, width : 2 * width]]
    return pl.pallas_call(
        gradients_kernel,
        out_shape=jax.ShapeDtypeStruct((n_z, 3 * ex_loc, width // n_z, width), F32),
        compiler_params=pltpu.CompilerParams(vmem_limit_bytes=32 * 2**20),
        cost_estimate=pl.CostEstimate(
            flops=4 * rows * hidden * width, bytes_accessed=12 * rows * hidden, transcendentals=0
        ),
    )(d_hidden, *factors, *projs, model, hidden_grads)


def on_device(
    activations,
    out_grad,
    w_gate,
    w_up,
    w_down,
    proj_model,
    proj_hidden,
    test_grads,
    lengths,
    groups,
):
    ex_loc, seq_len, d_local = activations.shape
    tok_rows = ex_loc * seq_len
    width = proj_model.shape[1] // 3
    n_z = lax.axis_size("tensor")
    n_cores = lax.axis_size("test")
    core = lax.axis_index("test")
    n_ex = lax.axis_size("example")
    ex_index = lax.axis_index("example")
    hid_part = w_gate.shape[1] // n_cores

    def forward(tokens, weight):
        return jnp.dot(tokens, weight, preferred_element_type=F32)

    def core_sum(product, step):
        begin = (step - 1) % n_ex * tok_rows

        def share_of(index):
            return lax.dynamic_slice(product, (begin, index * hid_part), (tok_rows, hid_part))

        kept = share_of(core)
        for core_step in range(1, n_cores):
            sent = pack(share_of(lax.rem(core + core_step, n_cores)))
            kept = kept + unpack(shift(sent, "test", core_step))
        return kept

    flat_acts = activations.reshape(tok_rows, d_local)
    flat_grad = out_grad.reshape(tok_rows, d_local)
    model_part = jnp.concatenate(
        [
            jnp.dot(flat_acts, proj_model[:, : 2 * width], preferred_element_type=F32),
            jnp.dot(flat_grad, proj_model[:, 2 * width :], preferred_element_type=F32),
        ],
        1,
    )

    direct = (n_z, n_ex, n_cores) == (4, 2, 2)
    examples = [slice(e * seq_len, (e + 1) * seq_len) for e in range(ex_loc)]
    arrived, arrived_down = [], []
    if direct:
        acts_all = arrived_features(
            spread_features(flat_acts, 1), spread_features(flat_acts, 0), model_part
        )
        grad_ready = after(flat_grad, acts_all)
        grad_all = spread_features(grad_ready, 1), spread_features(grad_ready, 0)
    else:
        acts_all = gathered_features(flat_acts, n_ex, n_cores)
        grad_all = gathered_features(flat_grad, n_ex, n_cores)
    model_sum = lax.psum(after(model_part, acts_all), "tensor")
    gate_all = forward(acts_all, w_gate)
    up_all = forward(after(acts_all, gate_all), w_up)
    for step in range(1, n_ex):
        both = pack(jnp.stack([core_sum(gate_all, step), core_sum(up_all, step)]))
        received = shift(both, "example", step)
        arrived.append(received)
    if direct:
        grad_all = arrived_features(*grad_all, both)
    down_all = dot_rows(grad_all, w_down)
    for step in range(1, n_ex):
        sent = pack(core_sum(down_all, step))
        arrived_down.append(shift(sent, "example", step))
    own = [core_sum(one, 0) for one in (gate_all, up_all, after(down_all, received))]
    model_sum = after(model_sum, received)

    hid_proj = lax.dynamic_slice_in_dim(proj_hidden, core * hid_part, hid_part, 0)
    positions = jnp.arange(seq_len, dtype=jnp.int32)
    token_mask = (positions[None, :] < lengths[:, None]).astype(F32)[:, :, None]
    masked = model_sum.reshape(ex_loc, seq_len, 3 * width) * token_mask

    def outer(outputs, inputs):
        product = lax.dot_general(
            outputs, inputs, (((0,), (0,)), ((), ())), precision=lax.Precision.HIGHEST
        )
        return product.reshape(n_z, width // n_z, width)

    gate_act, up_act = [
        kept + sum(unpack(one[which]) for one in arrived) for which, kept in enumerate(own[:2])
    ]
    d_hidden = own[2] + sum(unpack(one) for one in arrived_down)
    sigmoid_gate = jax.nn.sigmoid(gate_act)
    silu_gate = gate_act * sigmoid_gate
    hidden = (silu_gate * up_act).astype(jnp.bfloat16)
    gate_factor = up_act * sigmoid_gate * (1.0 + gate_act * (1.0 - sigmoid_gate))
    in_hidden = jnp.dot(hidden, hid_proj[:, 2 * width :], preferred_element_type=F32)
    hidden_grads = jnp.stack(
        [outer(masked[e, :, 2 * width :], in_hidden[rows]) for e, rows in enumerate(examples)]
    )
    factors = [gate_factor, silu_gate]
    grads = gradients(
        d_hidden, factors, hid_proj, masked[:, :, : 2 * width], hidden_grads, n_z
    )
    grads = scatter_sum(grads, "tensor")
    by_example = []
    for ex_step in range(n_ex):
        total = 0.0
        for core_step in range(n_cores):
            piece = grads
            if ex_step or core_step:
                pairs = [
                    (i * n_cores + c, (i + ex_step) % n_ex * n_cores + (c + core_step) % n_cores)
                    for i in range(n_ex)
                    for c in range(n_cores)
                ]
                piece = lax.ppermute(piece, ("example", "test"), pairs)
            total = total + piece
        by_example.append(total)
    grads = in_order(by_example, "example")
    partial_scores = lax.dot_general(
        grads.reshape(n_ex * ex_loc, -1),
        test_grads.astype(F32).reshape(-1, test_grads.shape[-1]),
        (((1,), (0,)), ((), ())),
        precision=lax.Precision.HIGHEST,
    )
    all_scores = jnp.sum(gather_in_order(partial_scores, "tensor"), 0)
    scores = lax.dynamic_slice_in_dim(all_scores, ex_index * ex_loc, ex_loc, 0)
    all_groups = gather_in_order(groups, "example")
    group_onehot = (
        all_groups.reshape(-1)[:, None] == jnp.arange(NGROUP, dtype=jnp.int32)[None, :]
    ).astype(F32)
    group_scores = jnp.dot(group_onehot.T, all_scores, precision=lax.Precision.HIGHEST)
    return (scores, group_scores)


def solution(mesh):
    placed = (
        P(("parts", "example"), None, "tensor"),
        P(("parts", "example"), None, "tensor"),
        P(("example", "test"), "tensor"),
        P(("example", "test"), "tensor"),
        P("tensor", ("example", "test")),
        P("tensor", None),
        P("tensor", None),
        P(None, "tensor", None, "test"),
        P(("parts", "example")),
        P(("parts", "example")),
    )
    return jax.shard_map(
        on_device,
        mesh=mesh,
        in_specs=placed,
        out_specs=(P(("parts", "example"), "test"), P("parts", "test")),
        check_vma=False,
    )
```

```python
import jax
import jax.numpy as jnp
from jax import lax
from jax.experimental import pallas as pl
from jax.experimental.pallas import tpu as pltpu
from jax.sharding import PartitionSpec as P

NGROUP = 4
F32 = jnp.float32
SEND_SCALE = 16.0


def shift(value, axis, step):
    n = lax.axis_size(axis)
    return lax.ppermute(value, axis, [(i, (i + step) % n) for i in range(n)])


def pack(value):
    return (value * SEND_SCALE).astype(jnp.float16)


def unpack(value):
    return value.astype(F32) * (1.0 / SEND_SCALE)


def in_order(pieces, axis):
    n = len(pieces)
    back = pieces[:0:-1] + pieces[:1]
    return lax.dynamic_slice_in_dim(jnp.stack(back + back), n - 1 - lax.axis_index(axis), n, 0)


def gather_in_order(value, axis):
    n = lax.axis_size(axis)
    if n > 8:
        return lax.all_gather(value, axis, axis=0)
    return in_order([value] + [shift(value, axis, step) for step in range(1, n)], axis)


def scatter_sum(blocks, axis):
    n = lax.axis_size(axis)
    if n > 8:
        return lax.psum_scatter(blocks, axis, scatter_dimension=0, tiled=True)[0]
    me = lax.axis_index(axis)
    total = lax.dynamic_index_in_dim(blocks, me, 0, keepdims=False)
    for step in range(1, n):
        block = lax.dynamic_index_in_dim(blocks, lax.rem(me + step, n), 0, keepdims=False)
        total = total + shift(block, axis, step)
    return total


def after(value, *earlier):
    return lax.optimization_barrier((value,) + earlier)[0]


def spread_features(flat, far):
    pieces = []
    for turn in range(2):
        pairs = []
        for block in range(4):
            example, core = block // 2, block % 2
            for source_core in range(2):
                target = block ^ (2 * turn + (source_core ^ core))
                source = block * 4 + (example ^ far) * 2 + source_core
                pairs.append((source, target * 4 + example * 2 + core))
        pieces.append(lax.ppermute(flat, ("tensor", "example", "test"), pairs))
    return pieces


def arrived_features(pieces, *earlier):
    pieces = lax.optimization_barrier((*pieces, *earlier))
    holder = lax.axis_index("example") * 2 + lax.axis_index("test")
    return jnp.where((lax.axis_index("tensor") ^ holder) < 2, pieces[0], pieces[1])


def gathered_features(flat, n_ex, n_cores):
    rows = flat.shape[0]
    part = rows // n_cores
    mine = lax.dynamic_slice_in_dim(flat, lax.axis_index("test") * part, part, 0)
    whole = lax.all_gather(mine, "tensor", axis=1, tiled=True)
    whole = lax.all_to_all(whole, ("example", "test"), split_axis=1, concat_axis=0, tiled=True)
    owners = [lax.rem(lax.axis_index("example") + step, n_ex) for step in range(n_ex)]
    return [lax.dynamic_slice_in_dim(whole, owner * rows, rows, 0) for owner in owners]


def dot_rows_kernel(tokens_ref, weight_ref, out_ref):
    out_ref[...] = lax.dot_general(
        tokens_ref[...], weight_ref[...], (((1,), (1,)), ((), ())), preferred_element_type=F32
    )


def dot_rows(tokens, weight):
    rows, depth = tokens.shape
    hidden = weight.shape[0]
    tile = min(512, hidden)
    return pl.pallas_call(
        dot_rows_kernel,
        out_shape=jax.ShapeDtypeStruct((rows, hidden), F32),
        grid=(hidden // tile,),
        in_specs=[
            pl.BlockSpec((rows, depth), lambda i: (0, 0)),
            pl.BlockSpec((tile, depth), lambda i: (i, 0)),
        ],
        out_specs=pl.BlockSpec((rows, tile), lambda i: (0, i)),
        compiler_params=pltpu.CompilerParams(vmem_limit_bytes=16 * 2**20),
        cost_estimate=pl.CostEstimate(flops=1, bytes_accessed=1, transcendentals=0),
    )(tokens, weight)


def gradients_kernel(down_ref, *refs):
    factor_refs, proj_refs, (model_ref, hidden_ref, out_ref) = refs[:2], refs[2:4], refs[4:]
    n_z, _, share, width = out_ref.shape
    ex_loc, seq_len, _ = model_ref.shape
    hidden = down_ref.shape[1]
    chunk = min(512, hidden)
    for layer in range(2):
        outputs = jnp.zeros((ex_loc * seq_len, width), F32)
        for begin in range(0, hidden, chunk):
            part = pl.ds(begin, chunk)
            rounded = (down_ref[:, part] * factor_refs[layer][:, part]).astype(jnp.bfloat16)
            outputs += jnp.dot(rounded, proj_refs[layer][part, :], preferred_element_type=F32)
        for e in range(ex_loc):
            grad = lax.dot_general(
                outputs[e * seq_len : (e + 1) * seq_len],
                model_ref[e, :, layer * width : (layer + 1) * width],
                (((0,), (0,)), ((), ())),
                precision=lax.Precision.HIGHEST,
                preferred_element_type=F32,
            )
            for z in range(n_z):
                out_ref[z, 3 * e + layer] = grad[z * share : (z + 1) * share]
    for e in range(ex_loc):
        out_ref[:, 3 * e + 2] = hidden_ref[e]


def gradients(d_hidden, factors, projs, model, hidden_grads, n_z):
    width = projs[0].shape[1]
    rows, hidden = d_hidden.shape
    ex_loc = model.shape[0]
    return pl.pallas_call(
        gradients_kernel,
        out_shape=jax.ShapeDtypeStruct((n_z, 3 * ex_loc, width // n_z, width), F32),
        compiler_params=pltpu.CompilerParams(vmem_limit_bytes=32 * 2**20),
        cost_estimate=pl.CostEstimate(
            flops=4 * rows * hidden * width, bytes_accessed=12 * rows * hidden, transcendentals=0
        ),
    )(d_hidden, *factors, *projs, model, hidden_grads)


def on_device(
    activations,
    out_grad,
    w_gate,
    w_up,
    w_down,
    proj_model,
    proj_hidden,
    test_grads,
    lengths,
    groups,
):
    ex_loc, seq_len, d_local = activations.shape
    tok_rows = ex_loc * seq_len
    width = proj_model.shape[1] // 3
    n_z = lax.axis_size("tensor")
    n_cores = lax.axis_size("test")
    core = lax.axis_index("test")
    n_ex = lax.axis_size("example")
    ex_index = lax.axis_index("example")
    hid_part = w_gate.shape[1] // n_cores

    def forward(tokens, weight):
        return jnp.dot(tokens, weight, preferred_element_type=F32)

    def core_sum(product, begin, *earlier):
        def share_of(index):
            return lax.dynamic_slice(product, (begin, index * hid_part), (tok_rows, hid_part))

        kept = share_of(core)
        for step in range(1, n_cores):
            sent = pack(share_of(lax.rem(core + step, n_cores)))
            kept = kept + unpack(after(shift(sent, "test", step), *earlier))
        return kept

    flat_acts = activations.reshape(tok_rows, d_local)
    flat_grad = out_grad.reshape(tok_rows, d_local)
    model_acts = jnp.dot(flat_acts, proj_model[:, : 2 * width], preferred_element_type=F32)
    model_grad = jnp.dot(flat_grad, proj_model[:, 2 * width :], preferred_element_type=F32)
    model_part = jnp.concatenate([model_acts, model_grad], 1)

    hid_proj = lax.dynamic_slice_in_dim(proj_hidden, core * hid_part, hid_part, 0)
    projs = [hid_proj[:, layer * width : (layer + 1) * width] for layer in range(3)]
    positions = jnp.arange(seq_len, dtype=jnp.int32)
    token_mask = (positions[None, :] < lengths[:, None]).astype(F32)
    early = (model_acts, model_grad, token_mask, *projs)

    direct = (n_z, n_ex, n_cores) == (4, 2, 2)
    examples = [slice(e * seq_len, (e + 1) * seq_len) for e in range(ex_loc)]
    arrived, arrived_down = [], []
    if direct:
        acts_far = [arrived_features(spread_features(flat_acts, 1), *early)]
        acts_near = spread_features(flat_acts, 0)
    else:
        acts_near, *acts_far = gathered_features(flat_acts, n_ex, n_cores)
        grad_near, *grad_far = gathered_features(flat_grad, n_ex, n_cores)
    gate_far = [forward(one, w_gate) for one in acts_far]
    up_far = [forward(after(one, *gate_far), w_up) for one in acts_far]
    if direct:
        grad_ready = after(flat_grad, *up_far)
        grad_far, grad_near = spread_features(grad_ready, 1), spread_features(grad_ready, 0)
        acts_near = arrived_features(acts_near, *up_far)
    gate_near = forward(after(acts_near, *up_far), w_gate)
    up_near = forward(after(acts_near, gate_near), w_up)
    for step, (gate, up) in enumerate(zip(gate_far, up_far), 1):
        both = pack(jnp.stack([core_sum(gate, 0, up_near), core_sum(up, 0, up_near)]))
        received = shift(both, "example", step)
        arrived.append(received)
    if direct:
        grad_far = [arrived_features(grad_far, both)]
        grad_near = arrived_features(grad_near, both)
    down_all = dot_rows(jnp.concatenate([*grad_far, grad_near]), w_down)
    for step in range(1, n_ex):
        sent = pack(core_sum(down_all, (step - 1) * tok_rows))
        arrived_down.append(shift(sent, "example", step))
    down_near = after(down_all, received)
    own = [
        core_sum(gate_near, 0),
        core_sum(up_near, 0),
        core_sum(down_near, (n_ex - 1) * tok_rows),
    ]
    if n_z > 8:
        model_sum = lax.psum(model_part, "tensor")
    else:
        model_sent = after(pack(model_part), sent)
        others = [shift(model_sent, "tensor", step) for step in range(1, n_z)]
        others = lax.optimization_barrier((*others, received))[:-1]
        model_sum = model_part + sum(unpack(one) for one in others)

    masked = model_sum.reshape(ex_loc, seq_len, 3 * width) * token_mask[:, :, None]

    def outer(outputs, inputs):
        product = lax.dot_general(
            outputs, inputs, (((0,), (0,)), ((), ())), precision=lax.Precision.HIGHEST
        )
        return product.reshape(n_z, width // n_z, width)

    gate_act, up_act = [
        kept + sum(unpack(one[which]) for one in arrived) for which, kept in enumerate(own[:2])
    ]
    d_hidden = own[2] + sum(unpack(one) for one in arrived_down)
    sigmoid_gate = jax.nn.sigmoid(gate_act)
    silu_gate = gate_act * sigmoid_gate
    hidden = (silu_gate * up_act).astype(jnp.bfloat16)
    gate_factor = up_act * sigmoid_gate * (1.0 + gate_act * (1.0 - sigmoid_gate))
    in_hidden = jnp.dot(hidden, projs[2], preferred_element_type=F32)
    hidden_grads = jnp.stack(
        [outer(masked[e, :, 2 * width :], in_hidden[rows]) for e, rows in enumerate(examples)]
    )
    factors = [gate_factor, silu_gate]
    grads = gradients(
        d_hidden, factors, projs[:2], masked[:, :, : 2 * width], hidden_grads, n_z
    )
    grads = scatter_sum(grads, "tensor")
    by_example = []
    for ex_step in range(n_ex):
        total = 0.0
        for core_step in range(n_cores):
            piece = grads
            if ex_step or core_step:
                pairs = [
                    (i * n_cores + c, (i + ex_step) % n_ex * n_cores + (c + core_step) % n_cores)
                    for i in range(n_ex)
                    for c in range(n_cores)
                ]
                piece = lax.ppermute(piece, ("example", "test"), pairs)
            total = total + piece
        by_example.append(total)
    grads = in_order(by_example, "example")
    partial_scores = lax.dot_general(
        grads.reshape(n_ex * ex_loc, -1),
        test_grads.astype(F32).reshape(-1, test_grads.shape[-1]),
        (((1,), (0,)), ((), ())),
        precision=lax.Precision.HIGHEST,
    )
    all_scores = jnp.sum(gather_in_order(partial_scores, "tensor"), 0)
    scores = lax.dynamic_slice_in_dim(all_scores, ex_index * ex_loc, ex_loc, 0)
    all_groups = gather_in_order(groups, "example")
    group_onehot = (
        all_groups.reshape(-1)[:, None] == jnp.arange(NGROUP, dtype=jnp.int32)[None, :]
    ).astype(F32)
    group_scores = jnp.dot(group_onehot.T, all_scores, precision=lax.Precision.HIGHEST)
    return (scores, group_scores)


def solution(mesh):
    placed = (
        P(("parts", "example"), None, "tensor"),
        P(("parts", "example"), None, "tensor"),
        P(("example", "test"), "tensor"),
        P(("example", "test"), "tensor"),
        P("tensor", ("example", "test")),
        P("tensor", None),
        P("tensor", None),
        P(None, "tensor", None, "test"),
        P(("parts", "example")),
        P(("parts", "example")),
    )
    return jax.shard_map(
        on_device,
        mesh=mesh,
        in_specs=placed,
        out_specs=(P(("parts", "example"), "test"), P("parts", "test")),
        check_vma=False,
    )
```

```python
import functools

import jax
import jax.numpy as jnp
from jax import lax
from jax.experimental import pallas as pl
from jax.experimental.pallas import tpu as pltpu
from jax.sharding import PartitionSpec as P

NGROUP = 4
F32 = jnp.float32
SEND_SCALE = 16.0


def shift(value, axis, step):
    n = lax.axis_size(axis)
    return lax.ppermute(value, axis, [(i, (i + step) % n) for i in range(n)])


def pack(value):
    return (value * SEND_SCALE).astype(jnp.float16)


def unpack(value):
    return value.astype(F32) * (1.0 / SEND_SCALE)


def in_order(pieces, axis):
    n = len(pieces)
    back = pieces[:0:-1] + pieces[:1]
    return lax.dynamic_slice_in_dim(jnp.stack(back + back), n - 1 - lax.axis_index(axis), n, 0)


def gather_in_order(value, axis):
    n = lax.axis_size(axis)
    if n > 8:
        return lax.all_gather(value, axis, axis=0)
    return in_order([value] + [shift(value, axis, step) for step in range(1, n)], axis)


def scatter_sum(blocks, axis):
    n = lax.axis_size(axis)
    if n > 8:
        return lax.psum_scatter(blocks, axis, scatter_dimension=0, tiled=True)[0]
    me = lax.axis_index(axis)
    total = lax.dynamic_index_in_dim(blocks, me, 0, keepdims=False)
    for step in range(1, n):
        block = lax.dynamic_index_in_dim(blocks, lax.rem(me + step, n), 0, keepdims=False)
        total = total + shift(block, axis, step)
    return total


def after(value, *earlier):
    return lax.optimization_barrier((value,) + earlier)[0]


def spread_features(flat, far):
    pieces = []
    for turn in range(2):
        pairs = []
        for block in range(4):
            example, core = block // 2, block % 2
            for source_core in range(2):
                target = block ^ (2 * turn + (source_core ^ core))
                source = block * 4 + (example ^ far) * 2 + source_core
                pairs.append((source, target * 4 + example * 2 + core))
        pieces.append(lax.ppermute(flat, ("tensor", "example", "test"), pairs))
    return pieces


def arrived_features(pieces, *earlier):
    pieces = lax.optimization_barrier((*pieces, *earlier))
    holder = lax.axis_index("example") * 2 + lax.axis_index("test")
    return jnp.where((lax.axis_index("tensor") ^ holder) < 2, pieces[0], pieces[1])


def gathered_features(flat, n_ex, n_cores):
    rows = flat.shape[0]
    part = rows // n_cores
    mine = lax.dynamic_slice_in_dim(flat, lax.axis_index("test") * part, part, 0)
    whole = lax.all_gather(mine, "tensor", axis=1, tiled=True)
    whole = lax.all_to_all(whole, ("example", "test"), split_axis=1, concat_axis=0, tiled=True)
    owners = [lax.rem(lax.axis_index("example") + step, n_ex) for step in range(n_ex)]
    return [lax.dynamic_slice_in_dim(whole, owner * rows, rows, 0) for owner in owners]


def dot_rows_kernel(tokens_ref, weight_ref, out_ref):
    out_ref[...] = lax.dot_general(
        tokens_ref[...], weight_ref[...], (((1,), (1,)), ((), ())), preferred_element_type=F32
    )


def dot_rows(tokens, weight):
    rows, depth = tokens.shape
    hidden = weight.shape[0]
    tile = min(512, hidden)
    return pl.pallas_call(
        dot_rows_kernel,
        out_shape=jax.ShapeDtypeStruct((rows, hidden), F32),
        grid=(hidden // tile,),
        in_specs=[
            pl.BlockSpec((rows, depth), lambda i: (0, 0)),
            pl.BlockSpec((tile, depth), lambda i: (i, 0)),
        ],
        out_specs=pl.BlockSpec((rows, tile), lambda i: (0, i)),
        compiler_params=pltpu.CompilerParams(vmem_limit_bytes=16 * 2**20),
        cost_estimate=pl.CostEstimate(flops=1, bytes_accessed=1, transcendentals=0),
    )(tokens, weight)


def products_kernel(by_rows, tile, tokens_ref, *refs):
    count = len(refs) // 2
    contract = (((1,), (1 if by_rows else 0,)), ((), ()))

    def step(*tiles):
        for weight_ref, out_ref in zip(tiles, tiles[count:]):
            out_ref[...] = lax.dot_general(
                tokens_ref[...], weight_ref[...], contract, preferred_element_type=F32
            )

    rows, depth = tokens_ref.shape
    hidden = refs[-1].shape[1]
    block = ((tile, depth), lambda i: (i, 0)) if by_rows else ((depth, tile), lambda i: (0, i))
    pltpu.emit_pipeline(
        step,
        grid=(hidden // tile,),
        in_specs=[pl.BlockSpec(*block, pipeline_mode=pl.Buffered(3))] * count,
        out_specs=[pl.BlockSpec((rows, tile), lambda i: (0, i))] * count,
    )(*refs)


def products(tokens, weights, by_rows):
    rows, depth = tokens.shape
    hidden = weights[0].shape[0 if by_rows else 1]
    far_memory = pl.BlockSpec(memory_space=pltpu.HBM)
    return pl.pallas_call(
        functools.partial(products_kernel, by_rows, min(512, hidden)),
        out_shape=[jax.ShapeDtypeStruct((rows, hidden), F32)] * len(weights),
        in_specs=[pl.BlockSpec(memory_space=pltpu.VMEM)] + [far_memory] * len(weights),
        out_specs=[pl.BlockSpec(memory_space=pl.ANY)] * len(weights),
        compiler_params=pltpu.CompilerParams(vmem_limit_bytes=20 * 2**20),
        cost_estimate=pl.CostEstimate(flops=1, bytes_accessed=1, transcendentals=0),
    )(tokens, *weights)


def gradients_kernel(down_ref, *refs):
    factor_refs, proj_refs, (model_ref, hidden_ref, out_ref) = refs[:2], refs[2:4], refs[4:]
    n_z, _, share, width = out_ref.shape
    ex_loc, seq_len, _ = model_ref.shape
    hidden = down_ref.shape[1]
    chunk = min(512, hidden)
    for layer in range(2):
        outputs = jnp.zeros((ex_loc * seq_len, width), F32)
        for begin in range(0, hidden, chunk):
            part = pl.ds(begin, chunk)
            rounded = (down_ref[:, part] * factor_refs[layer][:, part]).astype(jnp.bfloat16)
            outputs += jnp.dot(rounded, proj_refs[layer][part, :], preferred_element_type=F32)
        for e in range(ex_loc):
            grad = lax.dot_general(
                outputs[e * seq_len : (e + 1) * seq_len],
                model_ref[e, :, layer * width : (layer + 1) * width],
                (((0,), (0,)), ((), ())),
                precision=lax.Precision.HIGHEST,
                preferred_element_type=F32,
            )
            for z in range(n_z):
                out_ref[z, 3 * e + layer] = grad[z * share : (z + 1) * share]
    for e in range(ex_loc):
        out_ref[:, 3 * e + 2] = hidden_ref[e]


def gradients(d_hidden, factors, projs, model, hidden_grads, n_z):
    width = projs[0].shape[1]
    rows, hidden = d_hidden.shape
    ex_loc = model.shape[0]
    return pl.pallas_call(
        gradients_kernel,
        out_shape=jax.ShapeDtypeStruct((n_z, 3 * ex_loc, width // n_z, width), F32),
        compiler_params=pltpu.CompilerParams(vmem_limit_bytes=32 * 2**20),
        cost_estimate=pl.CostEstimate(
            flops=4 * rows * hidden * width, bytes_accessed=12 * rows * hidden, transcendentals=0
        ),
    )(d_hidden, *factors, *projs, model, hidden_grads)


def on_device(
    activations,
    out_grad,
    w_gate,
    w_up,
    w_down,
    proj_model,
    proj_hidden,
    test_grads,
    lengths,
    groups,
):
    ex_loc, seq_len, d_local = activations.shape
    tok_rows = ex_loc * seq_len
    width = proj_model.shape[1] // 3
    n_z = lax.axis_size("tensor")
    n_cores = lax.axis_size("test")
    core = lax.axis_index("test")
    n_ex = lax.axis_size("example")
    ex_index = lax.axis_index("example")
    hid_part = w_gate.shape[1] // n_cores

    def forward(tokens, weight):
        return jnp.dot(tokens, weight, preferred_element_type=F32)

    def core_sum(product, begin, *earlier):
        def share_of(index):
            return lax.dynamic_slice(product, (begin, index * hid_part), (tok_rows, hid_part))

        kept = share_of(core)
        for step in range(1, n_cores):
            sent = pack(share_of(lax.rem(core + step, n_cores)))
            kept = kept + unpack(after(shift(sent, "test", step), *earlier))
        return kept

    flat_acts = activations.reshape(tok_rows, d_local)
    flat_grad = out_grad.reshape(tok_rows, d_local)
    model_acts = jnp.dot(flat_acts, proj_model[:, : 2 * width], preferred_element_type=F32)
    model_grad = jnp.dot(flat_grad, proj_model[:, 2 * width :], preferred_element_type=F32)
    model_part = jnp.concatenate([model_acts, model_grad], 1)

    hid_proj = lax.dynamic_slice_in_dim(proj_hidden, core * hid_part, hid_part, 0)
    projs = [hid_proj[:, layer * width : (layer + 1) * width] for layer in range(3)]
    positions = jnp.arange(seq_len, dtype=jnp.int32)
    token_mask = (positions[None, :] < lengths[:, None]).astype(F32)
    early = (model_acts, model_grad, token_mask, *projs)

    direct = (n_z, n_ex, n_cores) == (4, 2, 2)
    examples = [slice(e * seq_len, (e + 1) * seq_len) for e in range(ex_loc)]
    arrived, arrived_down = [], []
    if direct:
        acts_far = [arrived_features(spread_features(flat_acts, 1), *early)]
        acts_near = spread_features(flat_acts, 0)
    else:
        acts_near, *acts_far = gathered_features(flat_acts, n_ex, n_cores)
        grad_near, *grad_far = gathered_features(flat_grad, n_ex, n_cores)
    gate_far = [forward(one, w_gate) for one in acts_far]
    up_far = [forward(after(one, *gate_far), w_up) for one in acts_far]
    if direct:
        grad_ready = after(flat_grad, *up_far)
        grad_far, grad_near = spread_features(grad_ready, 1), spread_features(grad_ready, 0)
        acts_near = arrived_features(acts_near, *up_far)
    for step, (gate, up) in enumerate(zip(gate_far, up_far), 1):
        both = pack(jnp.stack([core_sum(gate, 0, acts_near), core_sum(up, 0, acts_near)]))
        received = shift(both, "example", step)
        arrived.append(received)
    if direct:
        grad_far = [arrived_features(grad_far, both)]
        grad_near = arrived_features(grad_near, both)
    down_all = dot_rows(jnp.concatenate([*grad_far, grad_near]), w_down)
    for step in range(1, n_ex):
        sent = pack(core_sum(down_all, (step - 1) * tok_rows))
        arrived_down.append(shift(sent, "example", step))
    gate_near, up_near = products(after(acts_near, sent), [w_gate, w_up], False)
    down_near = after(down_all, received)
    own = [
        core_sum(gate_near, 0),
        core_sum(up_near, 0),
        core_sum(down_near, (n_ex - 1) * tok_rows),
    ]
    if n_z > 8:
        model_sum = lax.psum(model_part, "tensor")
    else:
        model_sent = after(pack(model_part), sent)
        others = [shift(model_sent, "tensor", step) for step in range(1, n_z)]
        others = lax.optimization_barrier((*others, received))[:-1]
        model_sum = model_part + sum(unpack(one) for one in others)

    masked = model_sum.reshape(ex_loc, seq_len, 3 * width) * token_mask[:, :, None]

    def outer(outputs, inputs):
        product = lax.dot_general(
            outputs, inputs, (((0,), (0,)), ((), ())), precision=lax.Precision.HIGHEST
        )
        return product.reshape(n_z, width // n_z, width)

    gate_act, up_act = [
        kept + sum(unpack(one[which]) for one in arrived) for which, kept in enumerate(own[:2])
    ]
    d_hidden = own[2] + sum(unpack(one) for one in arrived_down)
    sigmoid_gate = jax.nn.sigmoid(gate_act)
    silu_gate = gate_act * sigmoid_gate
    hidden = (silu_gate * up_act).astype(jnp.bfloat16)
    gate_factor = up_act * sigmoid_gate * (1.0 + gate_act * (1.0 - sigmoid_gate))
    in_hidden = jnp.dot(hidden, projs[2], preferred_element_type=F32)
    hidden_grads = jnp.stack(
        [outer(masked[e, :, 2 * width :], in_hidden[rows]) for e, rows in enumerate(examples)]
    )
    factors = [gate_factor, silu_gate]
    grads = gradients(
        d_hidden, factors, projs[:2], masked[:, :, : 2 * width], hidden_grads, n_z
    )
    grads = scatter_sum(grads, "tensor")
    by_example = []
    for ex_step in range(n_ex):
        total = 0.0
        for core_step in range(n_cores):
            piece = grads
            if ex_step or core_step:
                pairs = [
                    (i * n_cores + c, (i + ex_step) % n_ex * n_cores + (c + core_step) % n_cores)
                    for i in range(n_ex)
                    for c in range(n_cores)
                ]
                piece = lax.ppermute(piece, ("example", "test"), pairs)
            total = total + piece
        by_example.append(total)
    grads = in_order(by_example, "example")
    partial_scores = lax.dot_general(
        grads.reshape(n_ex * ex_loc, -1),
        test_grads.astype(F32).reshape(-1, test_grads.shape[-1]),
        (((1,), (0,)), ((), ())),
        precision=lax.Precision.HIGHEST,
    )
    all_scores = jnp.sum(gather_in_order(partial_scores, "tensor"), 0)
    scores = lax.dynamic_slice_in_dim(all_scores, ex_index * ex_loc, ex_loc, 0)
    all_groups = gather_in_order(groups, "example")
    group_onehot = (
        all_groups.reshape(-1)[:, None] == jnp.arange(NGROUP, dtype=jnp.int32)[None, :]
    ).astype(F32)
    group_scores = jnp.dot(group_onehot.T, all_scores, precision=lax.Precision.HIGHEST)
    return (scores, group_scores)


def solution(mesh):
    placed = (
        P(("parts", "example"), None, "tensor"),
        P(("parts", "example"), None, "tensor"),
        P(("example", "test"), "tensor"),
        P(("example", "test"), "tensor"),
        P("tensor", ("example", "test")),
        P("tensor", None),
        P("tensor", None),
        P(None, "tensor", None, "test"),
        P(("parts", "example")),
        P(("parts", "example")),
    )
    return jax.shard_map(
        on_device,
        mesh=mesh,
        in_specs=placed,
        out_specs=(P(("parts", "example"), "test"), P("parts", "test")),
        check_vma=False,
    )
```

```python
import jax
import jax.numpy as jnp
from jax import lax
from jax.experimental import pallas as pl
from jax.experimental.pallas import tpu as pltpu
from jax.sharding import PartitionSpec as P

NGROUP = 4
F32 = jnp.float32
SEND_SCALE = 16.0


def shift(value, axis, step):
    n = lax.axis_size(axis)
    return lax.ppermute(value, axis, [(i, (i + step) % n) for i in range(n)])


def pack(value):
    return (value * SEND_SCALE).astype(jnp.float16)


def unpack(value):
    return value.astype(F32) * (1.0 / SEND_SCALE)


def in_order(pieces, axis):
    n = len(pieces)
    back = pieces[:0:-1] + pieces[:1]
    return lax.dynamic_slice_in_dim(jnp.stack(back + back), n - 1 - lax.axis_index(axis), n, 0)


def gather_in_order(value, axis):
    n = lax.axis_size(axis)
    if n > 8:
        return lax.all_gather(value, axis, axis=0)
    return in_order([value] + [shift(value, axis, step) for step in range(1, n)], axis)


def scatter_sum(blocks, axis):
    n = lax.axis_size(axis)
    if n > 8:
        return lax.psum_scatter(blocks, axis, scatter_dimension=0, tiled=True)[0]
    me = lax.axis_index(axis)
    total = lax.dynamic_index_in_dim(blocks, me, 0, keepdims=False)
    for step in range(1, n):
        block = lax.dynamic_index_in_dim(blocks, lax.rem(me + step, n), 0, keepdims=False)
        total = total + shift(block, axis, step)
    return total


def after(value, *earlier):
    return lax.optimization_barrier((value,) + earlier)[0]


def spread_features(flat):
    pieces = []
    for turn in range(2):
        pairs = []
        for block in range(4):
            example, core = block // 2, block % 2
            for far in range(2):
                for source_core in range(2):
                    target = block ^ (2 * (turn if far else 1 - turn) + (source_core ^ core))
                    source = block * 4 + (example ^ far) * 2 + source_core
                    pairs.append((source, target * 4 + example * 2 + core))
        pieces.append(lax.ppermute(flat, ("tensor", "example", "test"), pairs))
    return pieces


def arrived_features(pieces, *earlier):
    pieces = lax.optimization_barrier((*pieces, *earlier))
    holder = lax.axis_index("example") * 2 + lax.axis_index("test")
    far_first = (lax.axis_index("tensor") ^ holder) < 2
    return [jnp.where(far_first, *pieces[:2]), jnp.where(far_first, *pieces[1::-1])]


def gathered_features(flat, n_ex, n_cores):
    rows = flat.shape[0]
    part = rows // n_cores
    mine = lax.dynamic_slice_in_dim(flat, lax.axis_index("test") * part, part, 0)
    whole = lax.all_gather(mine, "tensor", axis=1, tiled=True)
    whole = lax.all_to_all(whole, ("example", "test"), split_axis=1, concat_axis=0, tiled=True)
    owners = [lax.rem(lax.axis_index("example") + step, n_ex) for step in range(n_ex)]
    return [lax.dynamic_slice_in_dim(whole, owner * rows, rows, 0) for owner in owners]


def dot_rows_kernel(tokens_ref, weight_ref, out_ref):
    out_ref[...] = lax.dot_general(
        tokens_ref[...], weight_ref[...], (((1,), (1,)), ((), ())), preferred_element_type=F32
    )


def dot_rows(tokens, weight):
    rows, depth = tokens.shape
    hidden = weight.shape[0]
    tile = min(512, hidden)
    return pl.pallas_call(
        dot_rows_kernel,
        out_shape=jax.ShapeDtypeStruct((rows, hidden), F32),
        grid=(hidden // tile,),
        in_specs=[
            pl.BlockSpec((rows, depth), lambda i: (0, 0)),
            pl.BlockSpec((tile, depth), lambda i: (i, 0)),
        ],
        out_specs=pl.BlockSpec((rows, tile), lambda i: (0, i)),
        compiler_params=pltpu.CompilerParams(vmem_limit_bytes=16 * 2**20),
        cost_estimate=pl.CostEstimate(flops=1, bytes_accessed=1, transcendentals=0),
    )(tokens, weight)


def gradients_kernel(down_ref, *refs):
    factor_refs, proj_refs, (model_ref, hidden_ref, out_ref) = refs[:2], refs[2:4], refs[4:]
    n_z, _, share, width = out_ref.shape
    ex_loc, seq_len, _ = model_ref.shape
    hidden = down_ref.shape[1]
    chunk = min(512, hidden)
    for layer in range(2):
        outputs = jnp.zeros((ex_loc * seq_len, width), F32)
        for begin in range(0, hidden, chunk):
            part = pl.ds(begin, chunk)
            rounded = (down_ref[:, part] * factor_refs[layer][:, part]).astype(jnp.bfloat16)
            outputs += jnp.dot(rounded, proj_refs[layer][part, :], preferred_element_type=F32)
        for e in range(ex_loc):
            grad = lax.dot_general(
                outputs[e * seq_len : (e + 1) * seq_len],
                model_ref[e, :, layer * width : (layer + 1) * width],
                (((0,), (0,)), ((), ())),
                precision=lax.Precision.HIGHEST,
                preferred_element_type=F32,
            )
            for z in range(n_z):
                out_ref[z, 3 * e + layer] = grad[z * share : (z + 1) * share]
    for e in range(ex_loc):
        out_ref[:, 3 * e + 2] = hidden_ref[e]


def gradients(d_hidden, factors, projs, model, hidden_grads, n_z):
    width = projs[0].shape[1]
    rows, hidden = d_hidden.shape
    ex_loc = model.shape[0]
    return pl.pallas_call(
        gradients_kernel,
        out_shape=jax.ShapeDtypeStruct((n_z, 3 * ex_loc, width // n_z, width), F32),
        compiler_params=pltpu.CompilerParams(vmem_limit_bytes=32 * 2**20),
        cost_estimate=pl.CostEstimate(
            flops=4 * rows * hidden * width, bytes_accessed=12 * rows * hidden, transcendentals=0
        ),
    )(d_hidden, *factors, *projs, model, hidden_grads)


def on_device(
    activations,
    out_grad,
    w_gate,
    w_up,
    w_down,
    proj_model,
    proj_hidden,
    test_grads,
    lengths,
    groups,
):
    ex_loc, seq_len, d_local = activations.shape
    tok_rows = ex_loc * seq_len
    width = proj_model.shape[1] // 3
    n_z = lax.axis_size("tensor")
    n_cores = lax.axis_size("test")
    core = lax.axis_index("test")
    n_ex = lax.axis_size("example")
    ex_index = lax.axis_index("example")
    hid_part = w_gate.shape[1] // n_cores

    def forward(tokens, weight):
        return pack(jnp.dot(tokens, weight, preferred_element_type=F32))

    def core_sum(product, begin, *earlier):
        packed = product.dtype == jnp.float16

        def share_of(index):
            return lax.dynamic_slice(product, (begin, index * hid_part), (tok_rows, hid_part))

        kept = share_of(core)
        if packed:
            kept = unpack(kept)
        for step in range(1, n_cores):
            sent = share_of(lax.rem(core + step, n_cores))
            got = shift(sent if packed else pack(sent), "test", step)
            kept = kept + unpack(after(got, *earlier))
        return kept

    flat_acts = activations.reshape(tok_rows, d_local)
    flat_grad = out_grad.reshape(tok_rows, d_local)
    model_acts = jnp.dot(flat_acts, proj_model[:, : 2 * width], preferred_element_type=F32)
    model_grad = jnp.dot(flat_grad, proj_model[:, 2 * width :], preferred_element_type=F32)
    model_part = jnp.concatenate([model_acts, model_grad], 1)

    hid_proj = lax.dynamic_slice_in_dim(proj_hidden, core * hid_part, hid_part, 0)
    projs = [hid_proj[:, layer * width : (layer + 1) * width] for layer in range(3)]
    positions = jnp.arange(seq_len, dtype=jnp.int32)
    token_mask = (positions[None, :] < lengths[:, None]).astype(F32)
    all_groups = gather_in_order(groups, "example")
    early = (all_groups, model_acts, model_grad, token_mask, *projs)

    direct = (n_z, n_ex, n_cores) == (4, 2, 2)
    examples = [slice(e * seq_len, (e + 1) * seq_len) for e in range(ex_loc)]
    arrived, arrived_down = [], []
    if direct:
        acts_far, acts_near = arrived_features(spread_features(flat_acts), *early)
        acts_far = [acts_far]
    else:
        acts_near, *acts_far = gathered_features(flat_acts, n_ex, n_cores)
        grad_near, *grad_far = gathered_features(flat_grad, n_ex, n_cores)
    gate_far = [forward(one, w_gate) for one in acts_far]
    up_far = [forward(after(one, *gate_far), w_up) for one in acts_far]
    if direct:
        grad_all = spread_features(after(flat_grad, *up_far))
    gate_near = forward(after(acts_near, *up_far), w_gate)
    up_near = forward(after(acts_near, gate_near), w_up)
    for step, (gate, up) in enumerate(zip(gate_far, up_far), 1):
        both = pack(jnp.stack([core_sum(gate, 0, up_near), core_sum(up, 0, up_near)]))
        received = shift(both, "example", step)
        arrived.append(received)
    if direct:
        grad_all = arrived_features(grad_all, both)
    else:
        grad_all = [*grad_far, grad_near]
    down_all = dot_rows(jnp.concatenate(grad_all), w_down)
    for step in range(1, n_ex):
        sent = pack(core_sum(down_all, (step - 1) * tok_rows))
        arrived_down.append(shift(sent, "example", step))
    down_near = after(down_all, received)
    own = [
        core_sum(gate_near, 0),
        core_sum(up_near, 0),
        core_sum(down_near, (n_ex - 1) * tok_rows),
    ]
    if n_z > 8:
        model_sum = lax.psum(model_part, "tensor")
    else:
        model_sent = after(pack(model_part), sent)
        others = [shift(model_sent, "tensor", step) for step in range(1, n_z)]
        others = lax.optimization_barrier((*others, received))[:-1]
        model_sum = model_part + sum(unpack(one) for one in others)

    masked = model_sum.reshape(ex_loc, seq_len, 3 * width) * token_mask[:, :, None]

    def outer(outputs, inputs):
        product = lax.dot_general(
            outputs, inputs, (((0,), (0,)), ((), ())), precision=lax.Precision.HIGHEST
        )
        return product.reshape(n_z, width // n_z, width)

    gate_act, up_act = [
        kept + sum(unpack(one[which]) for one in arrived) for which, kept in enumerate(own[:2])
    ]
    d_hidden = own[2] + sum(unpack(one) for one in arrived_down)
    sigmoid_gate = jax.nn.sigmoid(gate_act)
    silu_gate = gate_act * sigmoid_gate
    hidden = (silu_gate * up_act).astype(jnp.bfloat16)
    gate_factor = up_act * sigmoid_gate * (1.0 + gate_act * (1.0 - sigmoid_gate))
    in_hidden = jnp.dot(hidden, projs[2], preferred_element_type=F32)
    hidden_grads = jnp.stack(
        [outer(masked[e, :, 2 * width :], in_hidden[rows]) for e, rows in enumerate(examples)]
    )
    factors = [gate_factor, silu_gate]
    grads = gradients(
        d_hidden, factors, projs[:2], masked[:, :, : 2 * width], hidden_grads, n_z
    )
    grads = scatter_sum(grads, "tensor")
    by_example = []
    for ex_step in range(n_ex):
        total = 0.0
        for core_step in range(n_cores):
            piece = grads
            if ex_step or core_step:
                pairs = [
                    (i * n_cores + c, (i + ex_step) % n_ex * n_cores + (c + core_step) % n_cores)
                    for i in range(n_ex)
                    for c in range(n_cores)
                ]
                piece = lax.ppermute(piece, ("example", "test"), pairs)
            total = total + piece
        by_example.append(total)
    grads = in_order(by_example, "example")
    partial_scores = lax.dot_general(
        grads.reshape(n_ex * ex_loc, -1),
        test_grads.astype(F32).reshape(-1, test_grads.shape[-1]),
        (((1,), (0,)), ((), ())),
        precision=lax.Precision.HIGHEST,
    )
    all_scores = jnp.sum(gather_in_order(partial_scores, "tensor"), 0)
    scores = lax.dynamic_slice_in_dim(all_scores, ex_index * ex_loc, ex_loc, 0)
    group_onehot = (
        all_groups.reshape(-1)[:, None] == jnp.arange(NGROUP, dtype=jnp.int32)[None, :]
    ).astype(F32)
    group_scores = jnp.dot(group_onehot.T, all_scores, precision=lax.Precision.HIGHEST)
    return (scores, group_scores)


def solution(mesh):
    placed = (
        P(("parts", "example"), None, "tensor"),
        P(("parts", "example"), None, "tensor"),
        P(("example", "test"), "tensor"),
        P(("example", "test"), "tensor"),
        P("tensor", ("example", "test")),
        P("tensor", None),
        P("tensor", None),
        P(None, "tensor", None, "test"),
        P(("parts", "example")),
        P(("parts", "example")),
    )
    return jax.shard_map(
        on_device,
        mesh=mesh,
        in_specs=placed,
        out_specs=(P(("parts", "example"), "test"), P("parts", "test")),
        check_vma=False,
    )
```

```python
import jax
import jax.numpy as jnp
from jax import lax
from jax.experimental import pallas as pl
from jax.experimental.pallas import tpu as pltpu
from jax.sharding import PartitionSpec as P

NGROUP = 4
F32 = jnp.float32
SEND_SCALE = 16.0


def shift(value, axis, step):
    n = lax.axis_size(axis)
    return lax.ppermute(value, axis, [(i, (i + step) % n) for i in range(n)])


def pack(value):
    return (value * SEND_SCALE).astype(jnp.float16)


def unpack(value):
    return value.astype(F32) * (1.0 / SEND_SCALE)


def in_order(pieces, axis):
    n = len(pieces)
    back = pieces[:0:-1] + pieces[:1]
    return lax.dynamic_slice_in_dim(jnp.stack(back + back), n - 1 - lax.axis_index(axis), n, 0)


def gather_in_order(value, axis):
    n = lax.axis_size(axis)
    if n > 8:
        return lax.all_gather(value, axis, axis=0)
    return in_order([value] + [shift(value, axis, step) for step in range(1, n)], axis)


def scatter_sum(blocks, axis):
    n = lax.axis_size(axis)
    if n > 8:
        return lax.psum_scatter(blocks, axis, scatter_dimension=0, tiled=True)[0]
    me = lax.axis_index(axis)
    total = lax.dynamic_index_in_dim(blocks, me, 0, keepdims=False)
    for step in range(1, n):
        block = lax.dynamic_index_in_dim(blocks, lax.rem(me + step, n), 0, keepdims=False)
        total = total + shift(block, axis, step)
    return total


def after(value, *earlier):
    return lax.optimization_barrier((value,) + earlier)[0]


def spread_features(flat):
    pieces = []
    for turn in range(2):
        pairs = []
        for block in range(4):
            example, core = block // 2, block % 2
            for far in range(2):
                for source_core in range(2):
                    target = block ^ (2 * (turn if far else 1 - turn) + (source_core ^ core))
                    source = block * 4 + (example ^ far) * 2 + source_core
                    pairs.append((source, target * 4 + example * 2 + core))
        pieces.append(lax.ppermute(flat, ("tensor", "example", "test"), pairs))
    return pieces


def arrived_features(pieces, *earlier):
    pieces = lax.optimization_barrier((*pieces, *earlier))
    holder = lax.axis_index("example") * 2 + lax.axis_index("test")
    far_first = (lax.axis_index("tensor") ^ holder) < 2
    return [jnp.where(far_first, *pieces[:2]), jnp.where(far_first, *pieces[1::-1])]


def cross_features(rows):
    pairs = []
    for block in range(4):
        for core in range(2):
            line = block * 4 + core
            pairs.append((line + 2 * (1 - block // 2), line + 2 * (block // 2)))
    return lax.ppermute(rows, ("tensor", "example", "test"), pairs)


def spread_on_line(rows):
    pieces = []
    for turn in range(2):
        pairs = []
        for block in range(4):
            for source_core in range(2):
                line = block // 2 * 2
                target = block ^ (2 * turn + (source_core ^ (block % 2)))
                pairs.append((block * 4 + line + source_core, target * 4 + line + block % 2))
        pieces.append(lax.ppermute(rows, ("tensor", "example", "test"), pairs))
    return pieces


def arrived_on_line(pieces, *earlier):
    pieces = lax.optimization_barrier((*pieces, *earlier))
    holder = lax.axis_index("example") * 2 + lax.axis_index("test")
    return jnp.where((lax.axis_index("tensor") ^ holder) < 2, *pieces[:2])


def gathered_features(flat, n_ex, n_cores):
    rows = flat.shape[0]
    part = rows // n_cores
    mine = lax.dynamic_slice_in_dim(flat, lax.axis_index("test") * part, part, 0)
    whole = lax.all_gather(mine, "tensor", axis=1, tiled=True)
    whole = lax.all_to_all(whole, ("example", "test"), split_axis=1, concat_axis=0, tiled=True)
    owners = [lax.rem(lax.axis_index("example") + step, n_ex) for step in range(n_ex)]
    return [lax.dynamic_slice_in_dim(whole, owner * rows, rows, 0) for owner in owners]


def dot_rows_kernel(tokens_ref, weight_ref, out_ref):
    out_ref[...] = lax.dot_general(
        tokens_ref[...], weight_ref[...], (((1,), (1,)), ((), ())), preferred_element_type=F32
    )


def dot_rows(tokens, weight):
    rows, depth = tokens.shape
    hidden = weight.shape[0]
    tile = min(512, hidden)
    return pl.pallas_call(
        dot_rows_kernel,
        out_shape=jax.ShapeDtypeStruct((rows, hidden), F32),
        grid=(hidden // tile,),
        in_specs=[
            pl.BlockSpec((rows, depth), lambda i: (0, 0)),
            pl.BlockSpec((tile, depth), lambda i: (i, 0)),
        ],
        out_specs=pl.BlockSpec((rows, tile), lambda i: (0, i)),
        compiler_params=pltpu.CompilerParams(vmem_limit_bytes=16 * 2**20),
        cost_estimate=pl.CostEstimate(flops=1, bytes_accessed=1, transcendentals=0),
    )(tokens, weight)


def gradients_kernel(down_ref, *refs):
    factor_refs, proj_refs, (model_ref, hidden_ref, out_ref) = refs[:2], refs[2:4], refs[4:]
    n_z, _, share, width = out_ref.shape
    ex_loc, seq_len, _ = model_ref.shape
    hidden = down_ref.shape[1]
    chunk = min(512, hidden)
    for layer in range(2):
        outputs = jnp.zeros((ex_loc * seq_len, width), F32)
        for begin in range(0, hidden, chunk):
            part = pl.ds(begin, chunk)
            rounded = (down_ref[:, part] * factor_refs[layer][:, part]).astype(jnp.bfloat16)
            outputs += jnp.dot(rounded, proj_refs[layer][part, :], preferred_element_type=F32)
        for e in range(ex_loc):
            grad = lax.dot_general(
                outputs[e * seq_len : (e + 1) * seq_len],
                model_ref[e, :, layer * width : (layer + 1) * width],
                (((0,), (0,)), ((), ())),
                precision=lax.Precision.HIGHEST,
                preferred_element_type=F32,
            )
            for z in range(n_z):
                out_ref[z, 3 * e + layer] = grad[z * share : (z + 1) * share]
    for e in range(ex_loc):
        out_ref[:, 3 * e + 2] = hidden_ref[e]


def gradients(d_hidden, factors, projs, model, hidden_grads, n_z):
    width = projs[0].shape[1]
    rows, hidden = d_hidden.shape
    ex_loc = model.shape[0]
    return pl.pallas_call(
        gradients_kernel,
        out_shape=jax.ShapeDtypeStruct((n_z, 3 * ex_loc, width // n_z, width), F32),
        compiler_params=pltpu.CompilerParams(vmem_limit_bytes=32 * 2**20),
        cost_estimate=pl.CostEstimate(
            flops=4 * rows * hidden * width, bytes_accessed=12 * rows * hidden, transcendentals=0
        ),
    )(d_hidden, *factors, *projs, model, hidden_grads)


def on_device(
    activations,
    out_grad,
    w_gate,
    w_up,
    w_down,
    proj_model,
    proj_hidden,
    test_grads,
    lengths,
    groups,
):
    ex_loc, seq_len, d_local = activations.shape
    tok_rows = ex_loc * seq_len
    width = proj_model.shape[1] // 3
    n_z = lax.axis_size("tensor")
    n_cores = lax.axis_size("test")
    core = lax.axis_index("test")
    n_ex = lax.axis_size("example")
    ex_index = lax.axis_index("example")
    hid_part = w_gate.shape[1] // n_cores

    def forward(tokens, weight):
        return pack(jnp.dot(tokens, weight, preferred_element_type=F32))

    def core_sum(product, begin, *earlier):
        packed = product.dtype == jnp.float16

        def share_of(index):
            return lax.dynamic_slice(product, (begin, index * hid_part), (tok_rows, hid_part))

        kept = share_of(core)
        if packed:
            kept = unpack(kept)
        for step in range(1, n_cores):
            sent = share_of(lax.rem(core + step, n_cores))
            got = shift(sent if packed else pack(sent), "test", step)
            kept = kept + unpack(after(got, *earlier))
        return kept

    flat_acts = activations.reshape(tok_rows, d_local)
    flat_grad = out_grad.reshape(tok_rows, d_local)
    model_acts = jnp.dot(flat_acts, proj_model[:, : 2 * width], preferred_element_type=F32)
    model_grad = jnp.dot(flat_grad, proj_model[:, 2 * width :], preferred_element_type=F32)
    model_part = jnp.concatenate([model_acts, model_grad], 1)

    hid_proj = lax.dynamic_slice_in_dim(proj_hidden, core * hid_part, hid_part, 0)
    projs = [hid_proj[:, layer * width : (layer + 1) * width] for layer in range(3)]
    positions = jnp.arange(seq_len, dtype=jnp.int32)
    token_mask = (positions[None, :] < lengths[:, None]).astype(F32)
    all_groups = gather_in_order(groups, "example")
    early = (all_groups, model_acts, model_grad, token_mask, *projs)

    direct = (n_z, n_ex, n_cores) == (4, 2, 2)
    examples = [slice(e * seq_len, (e + 1) * seq_len) for e in range(ex_loc)]
    arrived, arrived_down = [], []
    if direct:
        grad_crossed = cross_features(flat_grad)
        acts_all = arrived_features(spread_features(flat_acts), *early, grad_crossed)
    else:
        near, *acts_all = gathered_features(flat_acts, n_ex, n_cores)
        acts_all.append(near)
        grad_near, *grad_far = gathered_features(flat_grad, n_ex, n_cores)
    acts_all = jnp.concatenate(acts_all)
    gate_all = forward(acts_all, w_gate)
    up_all = forward(after(acts_all, gate_all), w_up)
    if direct:
        grad_far = spread_on_line(after(grad_crossed, up_all))
    for step in range(1, n_ex):
        begin = (step - 1) * tok_rows
        both = pack(jnp.stack([core_sum(gate_all, begin), core_sum(up_all, begin)]))
        received = shift(both, "example", step)
        arrived.append(received)
    if direct:
        grad_far = [arrived_on_line(grad_far, both)]
    for step, one in enumerate(grad_far, 1):
        down_far = dot_rows(one, w_down)
        sent = pack(core_sum(down_far, 0))
        arrived_down.append(shift(sent, "example", step))
    if direct:
        grad_near = spread_on_line(after(flat_grad, one))
        grad_near = arrived_on_line(grad_near, received)
    down_near = dot_rows(grad_near, w_down)
    begin = (n_ex - 1) * tok_rows
    own = [
        core_sum(gate_all, begin),
        core_sum(up_all, begin),
        core_sum(down_near, 0),
    ]
    if n_z > 8:
        model_sum = lax.psum(model_part, "tensor")
    else:
        model_sent = after(pack(model_part), received)
        others = [shift(model_sent, "tensor", step) for step in range(1, n_z)]
        model_sum = model_part + sum(unpack(one) for one in others)

    masked = model_sum.reshape(ex_loc, seq_len, 3 * width) * token_mask[:, :, None]

    def outer(outputs, inputs):
        product = lax.dot_general(
            outputs, inputs, (((0,), (0,)), ((), ())), precision=lax.Precision.HIGHEST
        )
        return product.reshape(n_z, width // n_z, width)

    gate_act, up_act = [
        kept + sum(unpack(one[which]) for one in arrived) for which, kept in enumerate(own[:2])
    ]
    d_hidden = own[2] + sum(unpack(one) for one in arrived_down)
    sigmoid_gate = jax.nn.sigmoid(gate_act)
    silu_gate = gate_act * sigmoid_gate
    hidden = (silu_gate * up_act).astype(jnp.bfloat16)
    gate_factor = up_act * sigmoid_gate * (1.0 + gate_act * (1.0 - sigmoid_gate))
    in_hidden = jnp.dot(hidden, projs[2], preferred_element_type=F32)
    hidden_grads = jnp.stack(
        [outer(masked[e, :, 2 * width :], in_hidden[rows]) for e, rows in enumerate(examples)]
    )
    factors = [gate_factor, silu_gate]
    grads = gradients(
        d_hidden, factors, projs[:2], masked[:, :, : 2 * width], hidden_grads, n_z
    )
    grads = scatter_sum(grads, "tensor")
    by_example = []
    for ex_step in range(n_ex):
        total = 0.0
        for core_step in range(n_cores):
            piece = grads
            if ex_step or core_step:
                pairs = [
                    (i * n_cores + c, (i + ex_step) % n_ex * n_cores + (c + core_step) % n_cores)
                    for i in range(n_ex)
                    for c in range(n_cores)
                ]
                piece = lax.ppermute(piece, ("example", "test"), pairs)
            total = total + piece
        by_example.append(total)
    grads = in_order(by_example, "example")
    partial_scores = lax.dot_general(
        grads.reshape(n_ex * ex_loc, -1),
        test_grads.astype(F32).reshape(-1, test_grads.shape[-1]),
        (((1,), (0,)), ((), ())),
        precision=lax.Precision.HIGHEST,
    )
    all_scores = jnp.sum(gather_in_order(partial_scores, "tensor"), 0)
    scores = lax.dynamic_slice_in_dim(all_scores, ex_index * ex_loc, ex_loc, 0)
    group_onehot = (
        all_groups.reshape(-1)[:, None] == jnp.arange(NGROUP, dtype=jnp.int32)[None, :]
    ).astype(F32)
    group_scores = jnp.dot(group_onehot.T, all_scores, precision=lax.Precision.HIGHEST)
    return (scores, group_scores)


def solution(mesh):
    placed = (
        P(("parts", "example"), None, "tensor"),
        P(("parts", "example"), None, "tensor"),
        P(("example", "test"), "tensor"),
        P(("example", "test"), "tensor"),
        P("tensor", ("example", "test")),
        P("tensor", None),
        P("tensor", None),
        P(None, "tensor", None, "test"),
        P(("parts", "example")),
        P(("parts", "example")),
    )
    return jax.shard_map(
        on_device,
        mesh=mesh,
        in_specs=placed,
        out_specs=(P(("parts", "example"), "test"), P("parts", "test")),
        check_vma=False,
    )
```

```python
import jax
import jax.numpy as jnp
from jax import lax
from jax.experimental import pallas as pl
from jax.experimental.pallas import tpu as pltpu
from jax.sharding import PartitionSpec as P

NGROUP = 4
F32 = jnp.float32
SEND_SCALE = 16.0


def shift(value, axis, step):
    n = lax.axis_size(axis)
    return lax.ppermute(value, axis, [(i, (i + step) % n) for i in range(n)])


def pack(value):
    return (value * SEND_SCALE).astype(jnp.float16)


def unpack(value):
    return value.astype(F32) * (1.0 / SEND_SCALE)


def in_order(pieces, axis):
    n = len(pieces)
    back = pieces[:0:-1] + pieces[:1]
    return lax.dynamic_slice_in_dim(jnp.stack(back + back), n - 1 - lax.axis_index(axis), n, 0)


def gather_in_order(value, axis):
    n = lax.axis_size(axis)
    if n > 8:
        return lax.all_gather(value, axis, axis=0)
    return in_order([value] + [shift(value, axis, step) for step in range(1, n)], axis)


def scatter_sum(blocks, axis):
    n = lax.axis_size(axis)
    if n > 8:
        return lax.psum_scatter(blocks, axis, scatter_dimension=0, tiled=True)[0]
    me = lax.axis_index(axis)
    total = lax.dynamic_index_in_dim(blocks, me, 0, keepdims=False)
    for step in range(1, n):
        block = lax.dynamic_index_in_dim(blocks, lax.rem(me + step, n), 0, keepdims=False)
        total = total + shift(block, axis, step)
    return total


def after(value, *earlier):
    return lax.optimization_barrier((value,) + earlier)[0]


def spread_features(flat):
    pieces = []
    for turn in range(2):
        pairs = []
        for block in range(4):
            example, core = block // 2, block % 2
            for far in range(2):
                for source_core in range(2):
                    target = block ^ (2 * (turn if far else 1 - turn) + (source_core ^ core))
                    source = block * 4 + (example ^ far) * 2 + source_core
                    pairs.append((source, target * 4 + example * 2 + core))
        pieces.append(lax.ppermute(flat, ("tensor", "example", "test"), pairs))
    return pieces


def arrived_features(pieces, *earlier):
    pieces = lax.optimization_barrier((*pieces, *earlier))
    holder = lax.axis_index("example") * 2 + lax.axis_index("test")
    far_first = (lax.axis_index("tensor") ^ holder) < 2
    return [jnp.where(far_first, *pieces[:2]), jnp.where(far_first, *pieces[1::-1])]


def gathered_features(flat, n_ex, n_cores):
    rows = flat.shape[0]
    part = rows // n_cores
    mine = lax.dynamic_slice_in_dim(flat, lax.axis_index("test") * part, part, 0)
    whole = lax.all_gather(mine, "tensor", axis=1, tiled=True)
    whole = lax.all_to_all(whole, ("example", "test"), split_axis=1, concat_axis=0, tiled=True)
    owners = [lax.rem(lax.axis_index("example") + step, n_ex) for step in range(n_ex)]
    return [lax.dynamic_slice_in_dim(whole, owner * rows, rows, 0) for owner in owners]


def dot_rows_kernel(tokens_ref, weight_ref, out_ref):
    out_ref[...] = lax.dot_general(
        tokens_ref[...], weight_ref[...], (((1,), (1,)), ((), ())), preferred_element_type=F32
    )


def dot_rows(tokens, weight):
    rows, depth = tokens.shape
    hidden = weight.shape[0]
    tile = min(512, hidden)
    return pl.pallas_call(
        dot_rows_kernel,
        out_shape=jax.ShapeDtypeStruct((rows, hidden), F32),
        grid=(hidden // tile,),
        in_specs=[
            pl.BlockSpec((rows, depth), lambda i: (0, 0)),
            pl.BlockSpec((tile, depth), lambda i: (i, 0)),
        ],
        out_specs=pl.BlockSpec((rows, tile), lambda i: (0, i)),
        compiler_params=pltpu.CompilerParams(vmem_limit_bytes=16 * 2**20),
        cost_estimate=pl.CostEstimate(flops=1, bytes_accessed=1, transcendentals=0),
    )(tokens, weight)


def gradients_kernel(down_ref, *refs):
    factor_refs, proj_refs, (model_ref, hidden_ref, out_ref) = refs[:2], refs[2:4], refs[4:]
    n_z, _, share, width = out_ref.shape
    ex_loc, seq_len, _ = model_ref.shape
    hidden = down_ref.shape[1]
    chunk = min(512, hidden)
    for layer in range(2):
        outputs = jnp.zeros((ex_loc * seq_len, width), F32)
        for begin in range(0, hidden, chunk):
            part = pl.ds(begin, chunk)
            rounded = (down_ref[:, part] * factor_refs[layer][:, part]).astype(jnp.bfloat16)
            outputs += jnp.dot(rounded, proj_refs[layer][part, :], preferred_element_type=F32)
        for e in range(ex_loc):
            grad = lax.dot_general(
                outputs[e * seq_len : (e + 1) * seq_len],
                model_ref[e, :, layer * width : (layer + 1) * width],
                (((0,), (0,)), ((), ())),
                precision=lax.Precision.HIGHEST,
                preferred_element_type=F32,
            )
            for z in range(n_z):
                out_ref[z, 3 * e + layer] = grad[z * share : (z + 1) * share]
    for e in range(ex_loc):
        out_ref[:, 3 * e + 2] = hidden_ref[e]


def gradients(d_hidden, factors, projs, model, hidden_grads, n_z):
    width = projs[0].shape[1]
    rows, hidden = d_hidden.shape
    ex_loc = model.shape[0]
    return pl.pallas_call(
        gradients_kernel,
        out_shape=jax.ShapeDtypeStruct((n_z, 3 * ex_loc, width // n_z, width), F32),
        compiler_params=pltpu.CompilerParams(vmem_limit_bytes=32 * 2**20),
        cost_estimate=pl.CostEstimate(
            flops=4 * rows * hidden * width, bytes_accessed=12 * rows * hidden, transcendentals=0
        ),
    )(d_hidden, *factors, *projs, model, hidden_grads)


def on_device(
    activations,
    out_grad,
    w_gate,
    w_up,
    w_down,
    proj_model,
    proj_hidden,
    test_grads,
    lengths,
    groups,
):
    ex_loc, seq_len, d_local = activations.shape
    tok_rows = ex_loc * seq_len
    width = proj_model.shape[1] // 3
    n_z = lax.axis_size("tensor")
    n_cores = lax.axis_size("test")
    core = lax.axis_index("test")
    n_ex = lax.axis_size("example")
    ex_index = lax.axis_index("example")
    hid_part = w_gate.shape[1] // n_cores

    def forward(tokens, weight):
        return pack(jnp.dot(tokens, weight, preferred_element_type=F32))

    def core_sum(product, begin, *earlier):
        packed = product.dtype == jnp.float16

        def share_of(index):
            return lax.dynamic_slice(product, (begin, index * hid_part), (tok_rows, hid_part))

        kept = share_of(core)
        if packed:
            kept = unpack(kept)
        for step in range(1, n_cores):
            sent = share_of(lax.rem(core + step, n_cores))
            got = shift(sent if packed else pack(sent), "test", step)
            kept = kept + unpack(after(got, *earlier))
        return kept

    flat_acts = activations.reshape(tok_rows, d_local)
    flat_grad = out_grad.reshape(tok_rows, d_local)
    model_acts = jnp.dot(flat_acts, proj_model[:, : 2 * width], preferred_element_type=F32)
    model_grad = jnp.dot(flat_grad, proj_model[:, 2 * width :], preferred_element_type=F32)
    model_part = jnp.concatenate([model_acts, model_grad], 1)

    hid_proj = lax.dynamic_slice_in_dim(proj_hidden, core * hid_part, hid_part, 0)
    projs = [hid_proj[:, layer * width : (layer + 1) * width] for layer in range(3)]
    positions = jnp.arange(seq_len, dtype=jnp.int32)
    token_mask = (positions[None, :] < lengths[:, None]).astype(F32)
    all_groups = gather_in_order(groups, "example")
    early = (all_groups, model_acts, model_grad, token_mask, *projs)

    direct = (n_z, n_ex, n_cores) == (4, 2, 2)
    examples = [slice(e * seq_len, (e + 1) * seq_len) for e in range(ex_loc)]
    arrived, arrived_down = [], []
    if direct:
        acts_all = arrived_features(spread_features(flat_acts), *early)
    else:
        near, *acts_all = gathered_features(flat_acts, n_ex, n_cores)
        acts_all.append(near)
        near, *grad_all = gathered_features(flat_grad, n_ex, n_cores)
        grad_all.append(near)
    acts_all = jnp.concatenate(acts_all)
    gate_all = forward(acts_all, w_gate)
    up_all = forward(after(acts_all, gate_all), w_up)
    if direct:
        grad_all = spread_features(after(flat_grad, up_all))
    for step in range(1, n_ex):
        begin = (step - 1) * tok_rows
        both = pack(jnp.stack([core_sum(gate_all, begin), core_sum(up_all, begin)]))
        received = shift(both, "example", step)
        arrived.append(received)
    if direct:
        grad_all = arrived_features(grad_all, both)
    down_all = dot_rows(jnp.concatenate(grad_all), w_down)
    for step in range(1, n_ex):
        sent = pack(core_sum(down_all, (step - 1) * tok_rows))
        arrived_down.append(shift(sent, "example", step))
    begin = (n_ex - 1) * tok_rows
    own = [
        core_sum(gate_all, begin),
        core_sum(up_all, begin),
        core_sum(after(down_all, received), begin),
    ]
    if n_z > 8:
        model_sum = lax.psum(model_part, "tensor")
    else:
        model_sent = after(pack(model_part), sent)
        others = [shift(model_sent, "tensor", step) for step in range(1, n_z)]
        others = lax.optimization_barrier((*others, received))[:-1]
        model_sum = model_part + sum(unpack(one) for one in others)

    masked = model_sum.reshape(ex_loc, seq_len, 3 * width) * token_mask[:, :, None]

    def outer(outputs, inputs):
        product = lax.dot_general(
            outputs, inputs, (((0,), (0,)), ((), ())), precision=lax.Precision.HIGHEST
        )
        return product.reshape(n_z, width // n_z, width)

    gate_act, up_act = [
        kept + sum(unpack(one[which]) for one in arrived) for which, kept in enumerate(own[:2])
    ]
    d_hidden = own[2] + sum(unpack(one) for one in arrived_down)
    sigmoid_gate = jax.nn.sigmoid(gate_act)
    silu_gate = gate_act * sigmoid_gate
    hidden = (silu_gate * up_act).astype(jnp.bfloat16)
    gate_factor = up_act * sigmoid_gate * (1.0 + gate_act * (1.0 - sigmoid_gate))
    in_hidden = jnp.dot(hidden, projs[2], preferred_element_type=F32)
    hidden_grads = jnp.stack(
        [outer(masked[e, :, 2 * width :], in_hidden[rows]) for e, rows in enumerate(examples)]
    )
    factors = [gate_factor, silu_gate]
    grads = gradients(
        d_hidden, factors, projs[:2], masked[:, :, : 2 * width], hidden_grads, n_z
    )
    grads = scatter_sum(grads, "tensor")
    by_example = []
    for ex_step in range(n_ex):
        total = 0.0
        for core_step in range(n_cores):
            piece = grads
            if ex_step or core_step:
                pairs = [
                    (i * n_cores + c, (i + ex_step) % n_ex * n_cores + (c + core_step) % n_cores)
                    for i in range(n_ex)
                    for c in range(n_cores)
                ]
                piece = lax.ppermute(piece, ("example", "test"), pairs)
            total = total + piece
        by_example.append(total)
    grads = in_order(by_example, "example")
    partial_scores = lax.dot_general(
        grads.reshape(n_ex * ex_loc, -1),
        test_grads.astype(F32).reshape(-1, test_grads.shape[-1]),
        (((1,), (0,)), ((), ())),
        precision=lax.Precision.HIGHEST,
    )
    all_scores = jnp.sum(gather_in_order(partial_scores, "tensor"), 0)
    scores = lax.dynamic_slice_in_dim(all_scores, ex_index * ex_loc, ex_loc, 0)
    group_onehot = (
        all_groups.reshape(-1)[:, None] == jnp.arange(NGROUP, dtype=jnp.int32)[None, :]
    ).astype(F32)
    group_scores = jnp.dot(group_onehot.T, all_scores, precision=lax.Precision.HIGHEST)
    return (scores, group_scores)


def solution(mesh):
    placed = (
        P(("parts", "example"), None, "tensor"),
        P(("parts", "example"), None, "tensor"),
        P(("example", "test"), "tensor"),
        P(("example", "test"), "tensor"),
        P("tensor", ("example", "test")),
        P("tensor", None),
        P("tensor", None),
        P(None, "tensor", None, "test"),
        P(("parts", "example")),
        P(("parts", "example")),
    )
    return jax.shard_map(
        on_device,
        mesh=mesh,
        in_specs=placed,
        out_specs=(P(("parts", "example"), "test"), P("parts", "test")),
        check_vma=False,
    )
```

```python
import jax
import jax.numpy as jnp
from jax import lax
from jax.experimental import pallas as pl
from jax.experimental.pallas import tpu as pltpu
from jax.sharding import PartitionSpec as P

NGROUP = 4
F32 = jnp.float32
SEND_SCALE = 16.0


def shift(value, axis, step):
    n = lax.axis_size(axis)
    return lax.ppermute(value, axis, [(i, (i + step) % n) for i in range(n)])


def pack(value):
    return (value * SEND_SCALE).astype(jnp.float16)


def unpack(value):
    return value.astype(F32) * (1.0 / SEND_SCALE)


def in_order(pieces, axis):
    n = len(pieces)
    back = pieces[:0:-1] + pieces[:1]
    return lax.dynamic_slice_in_dim(jnp.stack(back + back), n - 1 - lax.axis_index(axis), n, 0)


def gather_in_order(value, axis):
    n = lax.axis_size(axis)
    if n > 8:
        return lax.all_gather(value, axis, axis=0)
    return in_order([value] + [shift(value, axis, step) for step in range(1, n)], axis)


def scatter_sum(blocks, axis):
    n = lax.axis_size(axis)
    if n > 8:
        return lax.psum_scatter(blocks, axis, scatter_dimension=0, tiled=True)[0]
    me = lax.axis_index(axis)
    total = lax.dynamic_index_in_dim(blocks, me, 0, keepdims=False)
    for step in range(1, n):
        block = lax.dynamic_index_in_dim(blocks, lax.rem(me + step, n), 0, keepdims=False)
        total = total + shift(block, axis, step)
    return total


def after(value, *earlier):
    return lax.optimization_barrier((value,) + earlier)[0]


def spread_features(flat):
    pieces = []
    for turn in range(2):
        pairs = []
        for block in range(4):
            example, core = block // 2, block % 2
            for far in range(2):
                for source_core in range(2):
                    target = block ^ (2 * (turn if far else 1 - turn) + (source_core ^ core))
                    source = block * 4 + (example ^ far) * 2 + source_core
                    pairs.append((source, target * 4 + example * 2 + core))
        pieces.append(lax.ppermute(flat, ("tensor", "example", "test"), pairs))
    return pieces


def arrived_features(pieces, *earlier):
    pieces = lax.optimization_barrier((*pieces, *earlier))
    holder = lax.axis_index("example") * 2 + lax.axis_index("test")
    far_first = (lax.axis_index("tensor") ^ holder) < 2
    return [jnp.where(far_first, *pieces[:2]), jnp.where(far_first, *pieces[1::-1])]


def gathered_features(flat, n_ex, n_cores):
    rows = flat.shape[0]
    part = rows // n_cores
    mine = lax.dynamic_slice_in_dim(flat, lax.axis_index("test") * part, part, 0)
    whole = lax.all_gather(mine, "tensor", axis=1, tiled=True)
    whole = lax.all_to_all(whole, ("example", "test"), split_axis=1, concat_axis=0, tiled=True)
    owners = [lax.rem(lax.axis_index("example") + step, n_ex) for step in range(n_ex)]
    return [lax.dynamic_slice_in_dim(whole, owner * rows, rows, 0) for owner in owners]


def dot_rows_kernel(tokens_ref, weight_ref, out_ref):
    out_ref[...] = lax.dot_general(
        tokens_ref[...], weight_ref[...], (((1,), (1,)), ((), ())), preferred_element_type=F32
    )


def dot_rows(tokens, weight):
    rows, depth = tokens.shape
    hidden = weight.shape[0]
    tile = min(512, hidden)
    return pl.pallas_call(
        dot_rows_kernel,
        out_shape=jax.ShapeDtypeStruct((rows, hidden), F32),
        grid=(hidden // tile,),
        in_specs=[
            pl.BlockSpec((rows, depth), lambda i: (0, 0)),
            pl.BlockSpec((tile, depth), lambda i: (i, 0)),
        ],
        out_specs=pl.BlockSpec((rows, tile), lambda i: (0, i)),
        compiler_params=pltpu.CompilerParams(vmem_limit_bytes=16 * 2**20),
        cost_estimate=pl.CostEstimate(flops=1, bytes_accessed=1, transcendentals=0),
    )(tokens, weight)


def gradients_kernel(down_ref, *refs):
    factor_refs, proj_refs, (model_ref, hidden_ref, out_ref) = refs[:2], refs[2:4], refs[4:]
    n_z, _, share, width = out_ref.shape
    ex_loc, seq_len, _ = model_ref.shape
    hidden = down_ref.shape[1]
    chunk = min(512, hidden)
    for layer in range(2):
        outputs = jnp.zeros((ex_loc * seq_len, width), F32)
        for begin in range(0, hidden, chunk):
            part = pl.ds(begin, chunk)
            rounded = (down_ref[:, part] * factor_refs[layer][:, part]).astype(jnp.bfloat16)
            outputs += jnp.dot(rounded, proj_refs[layer][part, :], preferred_element_type=F32)
        for e in range(ex_loc):
            grad = lax.dot_general(
                outputs[e * seq_len : (e + 1) * seq_len],
                model_ref[e, :, layer * width : (layer + 1) * width],
                (((0,), (0,)), ((), ())),
                precision=lax.Precision.HIGHEST,
                preferred_element_type=F32,
            )
            for z in range(n_z):
                out_ref[z, 3 * e + layer] = grad[z * share : (z + 1) * share]
    for e in range(ex_loc):
        out_ref[:, 3 * e + 2] = hidden_ref[e]


def gradients(d_hidden, factors, projs, model, hidden_grads, n_z):
    width = projs[0].shape[1]
    rows, hidden = d_hidden.shape
    ex_loc = model.shape[0]
    return pl.pallas_call(
        gradients_kernel,
        out_shape=jax.ShapeDtypeStruct((n_z, 3 * ex_loc, width // n_z, width), F32),
        compiler_params=pltpu.CompilerParams(vmem_limit_bytes=32 * 2**20),
        cost_estimate=pl.CostEstimate(
            flops=4 * rows * hidden * width, bytes_accessed=12 * rows * hidden, transcendentals=0
        ),
    )(d_hidden, *factors, *projs, model, hidden_grads)


def on_device(
    activations,
    out_grad,
    w_gate,
    w_up,
    w_down,
    proj_model,
    proj_hidden,
    test_grads,
    lengths,
    groups,
):
    ex_loc, seq_len, d_local = activations.shape
    tok_rows = ex_loc * seq_len
    width = proj_model.shape[1] // 3
    n_z = lax.axis_size("tensor")
    n_cores = lax.axis_size("test")
    core = lax.axis_index("test")
    n_ex = lax.axis_size("example")
    ex_index = lax.axis_index("example")
    hid_part = w_gate.shape[1] // n_cores

    def forward(tokens, weight):
        return pack(jnp.dot(tokens, weight, preferred_element_type=F32))

    def core_sum(product, begin, *earlier):
        packed = product.dtype == jnp.float16

        def share_of(index):
            return lax.dynamic_slice(product, (begin, index * hid_part), (tok_rows, hid_part))

        kept = share_of(core)
        if packed:
            kept = unpack(kept)
        for step in range(1, n_cores):
            sent = share_of(lax.rem(core + step, n_cores))
            got = shift(sent if packed else pack(sent), "test", step)
            kept = kept + unpack(after(got, *earlier))
        return kept

    flat_acts = activations.reshape(tok_rows, d_local)
    flat_grad = out_grad.reshape(tok_rows, d_local)
    model_acts = jnp.dot(flat_acts, proj_model[:, : 2 * width], preferred_element_type=F32)
    model_grad = jnp.dot(flat_grad, proj_model[:, 2 * width :], preferred_element_type=F32)
    model_part = jnp.concatenate([model_acts, model_grad], 1)

    hid_proj = lax.dynamic_slice_in_dim(proj_hidden, core * hid_part, hid_part, 0)
    projs = [hid_proj[:, layer * width : (layer + 1) * width] for layer in range(3)]
    positions = jnp.arange(seq_len, dtype=jnp.int32)
    token_mask = (positions[None, :] < lengths[:, None]).astype(F32)
    all_groups = gather_in_order(groups, "example")
    early = (all_groups, model_acts, model_grad, token_mask, *projs)

    direct = (n_z, n_ex, n_cores) == (4, 2, 2)
    examples = [slice(e * seq_len, (e + 1) * seq_len) for e in range(ex_loc)]
    arrived, arrived_down = [], []
    if direct:
        acts_all = arrived_features(spread_features(flat_acts), *early)
    else:
        near, *acts_all = gathered_features(flat_acts, n_ex, n_cores)
        acts_all.append(near)
        near, *grad_all = gathered_features(flat_grad, n_ex, n_cores)
        grad_all.append(near)
    acts_all = jnp.concatenate(acts_all)
    gate_all = forward(acts_all, w_gate)
    up_all = forward(after(acts_all, gate_all), w_up)
    for step in range(1, n_ex):
        begin = (step - 1) * tok_rows
        both = pack(jnp.stack([core_sum(gate_all, begin), core_sum(up_all, begin)]))
        received = shift(both, "example", step)
        arrived.append(received)
    if direct:
        grad_all = spread_features(after(flat_grad, both))
        grad_all = arrived_features(grad_all, both)
    down_all = dot_rows(jnp.concatenate(grad_all), w_down)
    for step in range(1, n_ex):
        sent = pack(core_sum(down_all, (step - 1) * tok_rows))
        arrived_down.append(shift(sent, "example", step))
    begin = (n_ex - 1) * tok_rows
    own = [
        core_sum(gate_all, begin),
        core_sum(up_all, begin),
        core_sum(after(down_all, received), begin),
    ]
    if n_z > 8:
        model_sum = lax.psum(model_part, "tensor")
    else:
        model_sent = after(pack(model_part), sent)
        others = [shift(model_sent, "tensor", step) for step in range(1, n_z)]
        others = lax.optimization_barrier((*others, received))[:-1]
        model_sum = model_part + sum(unpack(one) for one in others)

    masked = model_sum.reshape(ex_loc, seq_len, 3 * width) * token_mask[:, :, None]

    def outer(outputs, inputs):
        product = lax.dot_general(
            outputs, inputs, (((0,), (0,)), ((), ())), precision=lax.Precision.HIGHEST
        )
        return product.reshape(n_z, width // n_z, width)

    gate_act, up_act = [
        kept + sum(unpack(one[which]) for one in arrived) for which, kept in enumerate(own[:2])
    ]
    d_hidden = lax.optimization_barrier(own[2]) + sum(unpack(one) for one in arrived_down)
    sigmoid_gate = jax.nn.sigmoid(gate_act)
    silu_gate = gate_act * sigmoid_gate
    hidden = (silu_gate * up_act).astype(jnp.bfloat16)
    gate_factor = up_act * sigmoid_gate * (1.0 + gate_act * (1.0 - sigmoid_gate))
    in_hidden = jnp.dot(hidden, projs[2], preferred_element_type=F32)
    hidden_grads = jnp.stack(
        [outer(masked[e, :, 2 * width :], in_hidden[rows]) for e, rows in enumerate(examples)]
    )
    factors = [gate_factor, silu_gate]
    grads = gradients(
        d_hidden, factors, projs[:2], masked[:, :, : 2 * width], hidden_grads, n_z
    )
    grads = scatter_sum(grads, "tensor")
    by_example = []
    for ex_step in range(n_ex):
        total = 0.0
        for core_step in range(n_cores):
            piece = grads
            if ex_step or core_step:
                pairs = [
                    (i * n_cores + c, (i + ex_step) % n_ex * n_cores + (c + core_step) % n_cores)
                    for i in range(n_ex)
                    for c in range(n_cores)
                ]
                piece = lax.ppermute(piece, ("example", "test"), pairs)
            total = total + piece
        by_example.append(total)
    grads = in_order(by_example, "example")
    partial_scores = lax.dot_general(
        grads.reshape(n_ex * ex_loc, -1),
        test_grads.astype(F32).reshape(-1, test_grads.shape[-1]),
        (((1,), (0,)), ((), ())),
        precision=lax.Precision.HIGHEST,
    )
    all_scores = jnp.sum(gather_in_order(partial_scores, "tensor"), 0)
    scores = lax.dynamic_slice_in_dim(all_scores, ex_index * ex_loc, ex_loc, 0)
    group_onehot = (
        all_groups.reshape(-1)[:, None] == jnp.arange(NGROUP, dtype=jnp.int32)[None, :]
    ).astype(F32)
    group_scores = jnp.dot(group_onehot.T, all_scores, precision=lax.Precision.HIGHEST)
    return (scores, group_scores)


def solution(mesh):
    placed = (
        P(("parts", "example"), None, "tensor"),
        P(("parts", "example"), None, "tensor"),
        P(("example", "test"), "tensor"),
        P(("example", "test"), "tensor"),
        P("tensor", ("example", "test")),
        P("tensor", None),
        P("tensor", None),
        P(None, "tensor", None, "test"),
        P(("parts", "example")),
        P(("parts", "example")),
    )
    return jax.shard_map(
        on_device,
        mesh=mesh,
        in_specs=placed,
        out_specs=(P(("parts", "example"), "test"), P("parts", "test")),
        check_vma=False,
    )
```

```python
import jax
import jax.numpy as jnp
from jax import lax
from jax.experimental import pallas as pl
from jax.experimental.pallas import tpu as pltpu
from jax.sharding import PartitionSpec as P

NGROUP = 4
F32 = jnp.float32
SEND_SCALE = 16.0


def shift(value, axis, step):
    n = lax.axis_size(axis)
    return lax.ppermute(value, axis, [(i, (i + step) % n) for i in range(n)])


def pack(value):
    return (value * SEND_SCALE).astype(jnp.float16)


def unpack(value):
    return value.astype(F32) * (1.0 / SEND_SCALE)


def in_order(pieces, axis):
    n = len(pieces)
    back = pieces[:0:-1] + pieces[:1]
    return lax.dynamic_slice_in_dim(jnp.stack(back + back), n - 1 - lax.axis_index(axis), n, 0)


def gather_in_order(value, axis):
    n = lax.axis_size(axis)
    if n > 8:
        return lax.all_gather(value, axis, axis=0)
    return in_order([value] + [shift(value, axis, step) for step in range(1, n)], axis)


def scatter_sum(blocks, axis):
    n = lax.axis_size(axis)
    if n > 8:
        return lax.psum_scatter(blocks, axis, scatter_dimension=0, tiled=True)[0]
    me = lax.axis_index(axis)
    total = lax.dynamic_index_in_dim(blocks, me, 0, keepdims=False)
    for step in range(1, n):
        block = lax.dynamic_index_in_dim(blocks, lax.rem(me + step, n), 0, keepdims=False)
        total = total + shift(block, axis, step)
    return total


def after(value, *earlier):
    return lax.optimization_barrier((value,) + earlier)[0]


def spread_features(flat, far):
    pieces = []
    for turn in range(2):
        pairs = []
        for block in range(4):
            example, core = block // 2, block % 2
            for source_core in range(2):
                target = block ^ (2 * turn + (source_core ^ core))
                source = block * 4 + (example ^ far) * 2 + source_core
                pairs.append((source, target * 4 + example * 2 + core))
        pieces.append(lax.ppermute(flat, ("tensor", "example", "test"), pairs))
    return pieces


def arrived_features(pieces, *earlier):
    pieces = lax.optimization_barrier((*pieces, *earlier))
    holder = lax.axis_index("example") * 2 + lax.axis_index("test")
    return jnp.where((lax.axis_index("tensor") ^ holder) < 2, pieces[0], pieces[1])


def gathered_features(flat, n_ex, n_cores):
    rows = flat.shape[0]
    part = rows // n_cores
    mine = lax.dynamic_slice_in_dim(flat, lax.axis_index("test") * part, part, 0)
    whole = lax.all_gather(mine, "tensor", axis=1, tiled=True)
    whole = lax.all_to_all(whole, ("example", "test"), split_axis=1, concat_axis=0, tiled=True)
    owners = [lax.rem(lax.axis_index("example") + step, n_ex) for step in range(n_ex)]
    return [lax.dynamic_slice_in_dim(whole, owner * rows, rows, 0) for owner in owners]


def dot_rows_kernel(tokens_ref, weight_ref, out_ref):
    out_ref[...] = lax.dot_general(
        tokens_ref[...], weight_ref[...], (((1,), (1,)), ((), ())), preferred_element_type=F32
    )


def dot_rows(tokens, weight):
    rows, depth = tokens.shape
    hidden = weight.shape[0]
    tile = min(512, hidden)
    return pl.pallas_call(
        dot_rows_kernel,
        out_shape=jax.ShapeDtypeStruct((rows, hidden), F32),
        grid=(hidden // tile,),
        in_specs=[
            pl.BlockSpec((rows, depth), lambda i: (0, 0)),
            pl.BlockSpec((tile, depth), lambda i: (i, 0)),
        ],
        out_specs=pl.BlockSpec((rows, tile), lambda i: (0, i)),
        compiler_params=pltpu.CompilerParams(vmem_limit_bytes=16 * 2**20),
        cost_estimate=pl.CostEstimate(flops=1, bytes_accessed=1, transcendentals=0),
    )(tokens, weight)


def gradients_kernel(down_ref, *refs):
    factor_refs, proj_refs, (model_ref, hidden_ref, out_ref) = refs[:2], refs[2:4], refs[4:]
    n_z, _, share, width = out_ref.shape
    ex_loc, seq_len, _ = model_ref.shape
    hidden = down_ref.shape[1]
    chunk = min(512, hidden)
    for layer in range(2):
        outputs = jnp.zeros((ex_loc * seq_len, width), F32)
        for begin in range(0, hidden, chunk):
            part = pl.ds(begin, chunk)
            rounded = (down_ref[:, part] * factor_refs[layer][:, part]).astype(jnp.bfloat16)
            outputs += jnp.dot(rounded, proj_refs[layer][part, :], preferred_element_type=F32)
        for e in range(ex_loc):
            grad = lax.dot_general(
                outputs[e * seq_len : (e + 1) * seq_len],
                model_ref[e, :, layer * width : (layer + 1) * width],
                (((0,), (0,)), ((), ())),
                precision=lax.Precision.HIGHEST,
                preferred_element_type=F32,
            )
            for z in range(n_z):
                out_ref[z, 3 * e + layer] = grad[z * share : (z + 1) * share]
    for e in range(ex_loc):
        out_ref[:, 3 * e + 2] = hidden_ref[e]


def gradients(d_hidden, factors, projs, model, hidden_grads, n_z):
    width = projs[0].shape[1]
    rows, hidden = d_hidden.shape
    ex_loc = model.shape[0]
    return pl.pallas_call(
        gradients_kernel,
        out_shape=jax.ShapeDtypeStruct((n_z, 3 * ex_loc, width // n_z, width), F32),
        compiler_params=pltpu.CompilerParams(vmem_limit_bytes=32 * 2**20),
        cost_estimate=pl.CostEstimate(
            flops=4 * rows * hidden * width, bytes_accessed=12 * rows * hidden, transcendentals=0
        ),
    )(d_hidden, *factors, *projs, model, hidden_grads)


def on_device(
    activations,
    out_grad,
    w_gate,
    w_up,
    w_down,
    proj_model,
    proj_hidden,
    test_grads,
    lengths,
    groups,
):
    ex_loc, seq_len, d_local = activations.shape
    tok_rows = ex_loc * seq_len
    width = proj_model.shape[1] // 3
    n_z = lax.axis_size("tensor")
    n_cores = lax.axis_size("test")
    core = lax.axis_index("test")
    n_ex = lax.axis_size("example")
    ex_index = lax.axis_index("example")
    hid_part = w_gate.shape[1] // n_cores

    def forward(tokens, weight):
        return jnp.dot(tokens, weight, preferred_element_type=F32)

    def core_sum(product, begin, *earlier):
        def share_of(index):
            return lax.dynamic_slice(product, (begin, index * hid_part), (tok_rows, hid_part))

        kept = share_of(core)
        for step in range(1, n_cores):
            sent = pack(share_of(lax.rem(core + step, n_cores)))
            kept = kept + unpack(after(shift(sent, "test", step), *earlier))
        return kept

    flat_acts = activations.reshape(tok_rows, d_local)
    flat_grad = out_grad.reshape(tok_rows, d_local)
    model_acts = jnp.dot(flat_acts, proj_model[:, : 2 * width], preferred_element_type=F32)
    model_grad = jnp.dot(flat_grad, proj_model[:, 2 * width :], preferred_element_type=F32)
    model_part = jnp.concatenate([model_acts, model_grad], 1)

    hid_proj = lax.dynamic_slice_in_dim(proj_hidden, core * hid_part, hid_part, 0)
    projs = [hid_proj[:, layer * width : (layer + 1) * width] for layer in range(3)]
    positions = jnp.arange(seq_len, dtype=jnp.int32)
    token_mask = (positions[None, :] < lengths[:, None]).astype(F32)
    all_groups = gather_in_order(groups, "example")
    early = (all_groups, model_acts, model_grad, token_mask, *projs)

    direct = (n_z, n_ex, n_cores) == (4, 2, 2)
    examples = [slice(e * seq_len, (e + 1) * seq_len) for e in range(ex_loc)]
    arrived, arrived_down = [], []
    if direct:
        acts_far = [arrived_features(spread_features(flat_acts, 1), *early)]
        acts_near = spread_features(flat_acts, 0)
    else:
        acts_near, *acts_far = gathered_features(flat_acts, n_ex, n_cores)
        grad_near, *grad_far = gathered_features(flat_grad, n_ex, n_cores)
    gate_far = [forward(one, w_gate) for one in acts_far]
    up_far = [forward(after(one, *gate_far), w_up) for one in acts_far]
    if direct:
        grad_ready = after(flat_grad, *up_far)
        grad_far, grad_near = spread_features(grad_ready, 1), spread_features(grad_ready, 0)
        acts_near = arrived_features(acts_near, *up_far)
    gate_near = forward(after(acts_near, *up_far), w_gate)
    up_near = forward(after(acts_near, gate_near), w_up)
    for step, (gate, up) in enumerate(zip(gate_far, up_far), 1):
        both = pack(jnp.stack([core_sum(gate, 0, up_near), core_sum(up, 0, up_near)]))
        received = shift(both, "example", step)
        arrived.append(received)
    if direct:
        grad_far = [arrived_features(grad_far, both)]
        grad_near = arrived_features(grad_near, both)
    down_all = dot_rows(jnp.concatenate([*grad_far, grad_near]), w_down)
    for step in range(1, n_ex):
        sent = pack(core_sum(down_all, (step - 1) * tok_rows))
        arrived_down.append(shift(sent, "example", step))
    down_near = after(down_all, received)
    own = [
        core_sum(gate_near, 0),
        core_sum(up_near, 0),
        core_sum(down_near, (n_ex - 1) * tok_rows),
    ]
    if n_z > 8:
        model_sum = lax.psum(model_part, "tensor")
    else:
        model_sent = after(pack(model_part), sent)
        others = [shift(model_sent, "tensor", step) for step in range(1, n_z)]
        others = lax.optimization_barrier((*others, received))[:-1]
        model_sum = model_part + sum(unpack(one) for one in others)

    masked = model_sum.reshape(ex_loc, seq_len, 3 * width) * token_mask[:, :, None]

    def outer(outputs, inputs):
        product = lax.dot_general(
            outputs, inputs, (((0,), (0,)), ((), ())), precision=lax.Precision.HIGHEST
        )
        return product.reshape(n_z, width // n_z, width)

    gate_act, up_act = [
        kept + sum(unpack(one[which]) for one in arrived) for which, kept in enumerate(own[:2])
    ]
    d_hidden = lax.optimization_barrier(own[2]) + sum(unpack(one) for one in arrived_down)
    sigmoid_gate = jax.nn.sigmoid(gate_act)
    silu_gate = gate_act * sigmoid_gate
    hidden = (silu_gate * up_act).astype(jnp.bfloat16)
    gate_factor = up_act * sigmoid_gate * (1.0 + gate_act * (1.0 - sigmoid_gate))
    in_hidden = jnp.dot(hidden, projs[2], preferred_element_type=F32)
    hidden_grads = jnp.stack(
        [outer(masked[e, :, 2 * width :], in_hidden[rows]) for e, rows in enumerate(examples)]
    )
    factors = [gate_factor, silu_gate]
    grads = gradients(
        d_hidden, factors, projs[:2], masked[:, :, : 2 * width], hidden_grads, n_z
    )
    grads = scatter_sum(grads, "tensor")
    by_example = []
    for ex_step in range(n_ex):
        total = 0.0
        for core_step in range(n_cores):
            piece = grads
            if ex_step or core_step:
                pairs = [
                    (i * n_cores + c, (i + ex_step) % n_ex * n_cores + (c + core_step) % n_cores)
                    for i in range(n_ex)
                    for c in range(n_cores)
                ]
                piece = lax.ppermute(piece, ("example", "test"), pairs)
            total = total + piece
        by_example.append(total)
    grads = in_order(by_example, "example")
    partial_scores = lax.dot_general(
        grads.reshape(n_ex * ex_loc, -1),
        test_grads.astype(F32).reshape(-1, test_grads.shape[-1]),
        (((1,), (0,)), ((), ())),
        precision=lax.Precision.HIGHEST,
    )
    all_scores = jnp.sum(gather_in_order(partial_scores, "tensor"), 0)
    scores = lax.dynamic_slice_in_dim(all_scores, ex_index * ex_loc, ex_loc, 0)
    group_onehot = (
        all_groups.reshape(-1)[:, None] == jnp.arange(NGROUP, dtype=jnp.int32)[None, :]
    ).astype(F32)
    group_scores = jnp.dot(group_onehot.T, all_scores, precision=lax.Precision.HIGHEST)
    return (scores, group_scores)


def solution(mesh):
    placed = (
        P(("parts", "example"), None, "tensor"),
        P(("parts", "example"), None, "tensor"),
        P(("example", "test"), "tensor"),
        P(("example", "test"), "tensor"),
        P("tensor", ("example", "test")),
        P("tensor", None),
        P("tensor", None),
        P(None, "tensor", None, "test"),
        P(("parts", "example")),
        P(("parts", "example")),
    )
    return jax.shard_map(
        on_device,
        mesh=mesh,
        in_specs=placed,
        out_specs=(P(("parts", "example"), "test"), P("parts", "test")),
        check_vma=False,
    )
```

```python
import jax
import jax.numpy as jnp
from jax import lax
from jax.experimental import pallas as pl
from jax.experimental.pallas import tpu as pltpu
from jax.sharding import PartitionSpec as P

NGROUP = 4
F32 = jnp.float32
SEND_SCALE = 16.0


def shift(value, axis, step):
    n = lax.axis_size(axis)
    return lax.ppermute(value, axis, [(i, (i + step) % n) for i in range(n)])


def pack(value):
    return (value * SEND_SCALE).astype(jnp.float16)


def unpack(value):
    return value.astype(F32) * (1.0 / SEND_SCALE)


def in_order(pieces, axis):
    n = len(pieces)
    back = pieces[:0:-1] + pieces[:1]
    return lax.dynamic_slice_in_dim(jnp.stack(back + back), n - 1 - lax.axis_index(axis), n, 0)


def gather_in_order(value, axis):
    n = lax.axis_size(axis)
    if n > 8:
        return lax.all_gather(value, axis, axis=0)
    return in_order([value] + [shift(value, axis, step) for step in range(1, n)], axis)


def scatter_sum(blocks, axis):
    n = lax.axis_size(axis)
    if n > 8:
        return lax.psum_scatter(blocks, axis, scatter_dimension=0, tiled=True)[0]
    me = lax.axis_index(axis)
    total = lax.dynamic_index_in_dim(blocks, me, 0, keepdims=False)
    for step in range(1, n):
        block = lax.dynamic_index_in_dim(blocks, lax.rem(me + step, n), 0, keepdims=False)
        total = total + shift(block, axis, step)
    return total


def after(value, *earlier):
    return lax.optimization_barrier((value,) + earlier)[0]


def spread_features(flat, far):
    pieces = []
    for turn in range(2):
        pairs = []
        for block in range(4):
            example, core = block // 2, block % 2
            for source_core in range(2):
                target = block ^ (2 * turn + (source_core ^ core))
                source = block * 4 + (example ^ far) * 2 + source_core
                pairs.append((source, target * 4 + example * 2 + core))
        pieces.append(lax.ppermute(flat, ("tensor", "example", "test"), pairs))
    return pieces


def arrived_features(pieces, *earlier):
    pieces = lax.optimization_barrier((*pieces, *earlier))
    holder = lax.axis_index("example") * 2 + lax.axis_index("test")
    return jnp.where((lax.axis_index("tensor") ^ holder) < 2, pieces[0], pieces[1])


def gathered_features(flat, n_ex, n_cores):
    rows = flat.shape[0]
    part = rows // n_cores
    mine = lax.dynamic_slice_in_dim(flat, lax.axis_index("test") * part, part, 0)
    whole = lax.all_gather(mine, "tensor", axis=1, tiled=True)
    whole = lax.all_to_all(whole, ("example", "test"), split_axis=1, concat_axis=0, tiled=True)
    owners = [lax.rem(lax.axis_index("example") + step, n_ex) for step in range(n_ex)]
    return [lax.dynamic_slice_in_dim(whole, owner * rows, rows, 0) for owner in owners]


def dot_rows_kernel(tokens_ref, weight_ref, out_ref):
    out_ref[...] = lax.dot_general(
        tokens_ref[...], weight_ref[...], (((1,), (1,)), ((), ())), preferred_element_type=F32
    )


def dot_rows(tokens, weight):
    rows, depth = tokens.shape
    hidden = weight.shape[0]
    tile = min(512, hidden)
    return pl.pallas_call(
        dot_rows_kernel,
        out_shape=jax.ShapeDtypeStruct((rows, hidden), F32),
        grid=(hidden // tile,),
        in_specs=[
            pl.BlockSpec((rows, depth), lambda i: (0, 0)),
            pl.BlockSpec((tile, depth), lambda i: (i, 0)),
        ],
        out_specs=pl.BlockSpec((rows, tile), lambda i: (0, i)),
        compiler_params=pltpu.CompilerParams(vmem_limit_bytes=16 * 2**20),
        cost_estimate=pl.CostEstimate(flops=1, bytes_accessed=1, transcendentals=0),
    )(tokens, weight)


def gradients_kernel(down_ref, *refs):
    factor_refs, proj_refs, (model_ref, hidden_ref, out_ref) = refs[:2], refs[2:4], refs[4:]
    n_z, _, share, width = out_ref.shape
    ex_loc, seq_len, _ = model_ref.shape
    hidden = down_ref.shape[1]
    chunk = min(512, hidden)
    for layer in range(2):
        outputs = jnp.zeros((ex_loc * seq_len, width), F32)
        for begin in range(0, hidden, chunk):
            part = pl.ds(begin, chunk)
            rounded = (down_ref[:, part] * factor_refs[layer][:, part]).astype(jnp.bfloat16)
            outputs += jnp.dot(rounded, proj_refs[layer][part, :], preferred_element_type=F32)
        for e in range(ex_loc):
            grad = lax.dot_general(
                outputs[e * seq_len : (e + 1) * seq_len],
                model_ref[e, :, layer * width : (layer + 1) * width],
                (((0,), (0,)), ((), ())),
                precision=lax.Precision.HIGHEST,
                preferred_element_type=F32,
            )
            for z in range(n_z):
                out_ref[z, 3 * e + layer] = grad[z * share : (z + 1) * share]
    for e in range(ex_loc):
        out_ref[:, 3 * e + 2] = hidden_ref[e]


def gradients(d_hidden, factors, projs, model, hidden_grads, n_z):
    width = projs[0].shape[1]
    rows, hidden = d_hidden.shape
    ex_loc = model.shape[0]
    return pl.pallas_call(
        gradients_kernel,
        out_shape=jax.ShapeDtypeStruct((n_z, 3 * ex_loc, width // n_z, width), F32),
        compiler_params=pltpu.CompilerParams(vmem_limit_bytes=32 * 2**20),
        cost_estimate=pl.CostEstimate(
            flops=4 * rows * hidden * width, bytes_accessed=12 * rows * hidden, transcendentals=0
        ),
    )(d_hidden, *factors, *projs, model, hidden_grads)


def on_device(
    activations,
    out_grad,
    w_gate,
    w_up,
    w_down,
    proj_model,
    proj_hidden,
    test_grads,
    lengths,
    groups,
):
    ex_loc, seq_len, d_local = activations.shape
    tok_rows = ex_loc * seq_len
    width = proj_model.shape[1] // 3
    n_z = lax.axis_size("tensor")
    n_cores = lax.axis_size("test")
    core = lax.axis_index("test")
    n_ex = lax.axis_size("example")
    ex_index = lax.axis_index("example")
    hid_part = w_gate.shape[1] // n_cores

    def forward(tokens, weight):
        return pack(jnp.dot(tokens, weight, preferred_element_type=F32))

    def core_sum(product, begin, *earlier):
        packed = product.dtype == jnp.float16

        def share_of(index):
            return lax.dynamic_slice(product, (begin, index * hid_part), (tok_rows, hid_part))

        kept = share_of(core)
        if packed:
            kept = unpack(kept)
        for step in range(1, n_cores):
            sent = share_of(lax.rem(core + step, n_cores))
            got = shift(sent if packed else pack(sent), "test", step)
            kept = kept + unpack(after(got, *earlier))
        return kept

    flat_acts = activations.reshape(tok_rows, d_local)
    flat_grad = out_grad.reshape(tok_rows, d_local)
    model_acts = jnp.dot(flat_acts, proj_model[:, : 2 * width], preferred_element_type=F32)
    model_grad = jnp.dot(flat_grad, proj_model[:, 2 * width :], preferred_element_type=F32)
    model_part = jnp.concatenate([model_acts, model_grad], 1)

    hid_proj = lax.dynamic_slice_in_dim(proj_hidden, core * hid_part, hid_part, 0)
    projs = [hid_proj[:, layer * width : (layer + 1) * width] for layer in range(3)]
    positions = jnp.arange(seq_len, dtype=jnp.int32)
    token_mask = (positions[None, :] < lengths[:, None]).astype(F32)
    all_groups = gather_in_order(groups, "example")
    early = (all_groups, model_acts, model_grad, token_mask, *projs)

    direct = (n_z, n_ex, n_cores) == (4, 2, 2)
    examples = [slice(e * seq_len, (e + 1) * seq_len) for e in range(ex_loc)]
    arrived, arrived_down = [], []
    if direct:
        acts_far = [arrived_features(spread_features(flat_acts, 1), *early)]
        acts_near = spread_features(flat_acts, 0)
    else:
        acts_near, *acts_far = gathered_features(flat_acts, n_ex, n_cores)
        grad_near, *grad_far = gathered_features(flat_grad, n_ex, n_cores)
    gate_far = [forward(one, w_gate) for one in acts_far]
    up_far = [forward(after(one, *gate_far), w_up) for one in acts_far]
    if direct:
        grad_ready = after(flat_grad, *up_far)
        grad_far, grad_near = spread_features(grad_ready, 1), spread_features(grad_ready, 0)
        acts_near = arrived_features(acts_near, *up_far)
    gate_near = forward(after(acts_near, *up_far), w_gate)
    up_near = forward(after(acts_near, gate_near), w_up)
    for step, (gate, up) in enumerate(zip(gate_far, up_far), 1):
        both = pack(jnp.stack([core_sum(gate, 0, up_near), core_sum(up, 0, up_near)]))
        received = shift(both, "example", step)
        arrived.append(received)
    if direct:
        grad_far = [arrived_features(grad_far, both)]
        grad_near = arrived_features(grad_near, both)
    down_all = dot_rows(jnp.concatenate([*grad_far, grad_near]), w_down)
    for step in range(1, n_ex):
        sent = pack(core_sum(down_all, (step - 1) * tok_rows))
        arrived_down.append(shift(sent, "example", step))
    down_near = after(down_all, received)
    own = [
        core_sum(gate_near, 0),
        core_sum(up_near, 0),
        core_sum(down_near, (n_ex - 1) * tok_rows),
    ]
    if n_z > 8:
        model_sum = lax.psum(model_part, "tensor")
    else:
        model_sent = after(pack(model_part), sent)
        others = [shift(model_sent, "tensor", step) for step in range(1, n_z)]
        others = lax.optimization_barrier((*others, received))[:-1]
        model_sum = model_part + sum(unpack(one) for one in others)

    masked = model_sum.reshape(ex_loc, seq_len, 3 * width) * token_mask[:, :, None]

    def outer(outputs, inputs):
        product = lax.dot_general(
            outputs, inputs, (((0,), (0,)), ((), ())), precision=lax.Precision.HIGHEST
        )
        return product.reshape(n_z, width // n_z, width)

    gate_act, up_act = [
        kept + sum(unpack(one[which]) for one in arrived) for which, kept in enumerate(own[:2])
    ]
    d_hidden = lax.optimization_barrier(own[2]) + sum(unpack(one) for one in arrived_down)
    sigmoid_gate = jax.nn.sigmoid(gate_act)
    silu_gate = gate_act * sigmoid_gate
    hidden = (silu_gate * up_act).astype(jnp.bfloat16)
    gate_factor = up_act * sigmoid_gate * (1.0 + gate_act * (1.0 - sigmoid_gate))
    in_hidden = jnp.dot(hidden, projs[2], preferred_element_type=F32)
    hidden_grads = jnp.stack(
        [outer(masked[e, :, 2 * width :], in_hidden[rows]) for e, rows in enumerate(examples)]
    )
    factors = [gate_factor, silu_gate]
    grads = gradients(
        d_hidden, factors, projs[:2], masked[:, :, : 2 * width], hidden_grads, n_z
    )
    grads = scatter_sum(grads, "tensor")
    by_example = []
    for ex_step in range(n_ex):
        total = 0.0
        for core_step in range(n_cores):
            piece = grads
            if ex_step or core_step:
                pairs = [
                    (i * n_cores + c, (i + ex_step) % n_ex * n_cores + (c + core_step) % n_cores)
                    for i in range(n_ex)
                    for c in range(n_cores)
                ]
                piece = lax.ppermute(piece, ("example", "test"), pairs)
            total = total + piece
        by_example.append(total)
    grads = in_order(by_example, "example")
    partial_scores = lax.dot_general(
        grads.reshape(n_ex * ex_loc, -1),
        test_grads.astype(F32).reshape(-1, test_grads.shape[-1]),
        (((1,), (0,)), ((), ())),
        precision=lax.Precision.HIGHEST,
    )
    all_scores = jnp.sum(gather_in_order(partial_scores, "tensor"), 0)
    scores = lax.dynamic_slice_in_dim(all_scores, ex_index * ex_loc, ex_loc, 0)
    group_onehot = (
        all_groups.reshape(-1)[:, None] == jnp.arange(NGROUP, dtype=jnp.int32)[None, :]
    ).astype(F32)
    group_scores = jnp.dot(group_onehot.T, all_scores, precision=lax.Precision.HIGHEST)
    return (scores, group_scores)


def solution(mesh):
    placed = (
        P(("parts", "example"), None, "tensor"),
        P(("parts", "example"), None, "tensor"),
        P(("example", "test"), "tensor"),
        P(("example", "test"), "tensor"),
        P("tensor", ("example", "test")),
        P("tensor", None),
        P("tensor", None),
        P(None, "tensor", None, "test"),
        P(("parts", "example")),
        P(("parts", "example")),
    )
    return jax.shard_map(
        on_device,
        mesh=mesh,
        in_specs=placed,
        out_specs=(P(("parts", "example"), "test"), P("parts", "test")),
        check_vma=False,
    )
```

```python
import jax
import jax.numpy as jnp
from jax import lax
from jax.experimental import pallas as pl
from jax.experimental.pallas import tpu as pltpu
from jax.sharding import PartitionSpec as P

NGROUP = 4
F32 = jnp.float32
SEND_SCALE = 16.0


def shift(value, axis, step):
    n = lax.axis_size(axis)
    return lax.ppermute(value, axis, [(i, (i + step) % n) for i in range(n)])


def pack(value):
    return (value * SEND_SCALE).astype(jnp.float16)


def unpack(value):
    return value.astype(F32) * (1.0 / SEND_SCALE)


def in_order(pieces, axis):
    n = len(pieces)
    back = pieces[:0:-1] + pieces[:1]
    return lax.dynamic_slice_in_dim(jnp.stack(back + back), n - 1 - lax.axis_index(axis), n, 0)


def gather_in_order(value, axis):
    n = lax.axis_size(axis)
    if n > 8:
        return lax.all_gather(value, axis, axis=0)
    return in_order([value] + [shift(value, axis, step) for step in range(1, n)], axis)


def scatter_sum(blocks, axis):
    n = lax.axis_size(axis)
    if n > 8:
        return lax.psum_scatter(blocks, axis, scatter_dimension=0, tiled=True)[0]
    me = lax.axis_index(axis)
    total = lax.dynamic_index_in_dim(blocks, me, 0, keepdims=False)
    for step in range(1, n):
        block = lax.dynamic_index_in_dim(blocks, lax.rem(me + step, n), 0, keepdims=False)
        total = total + shift(block, axis, step)
    return total


def after(value, *earlier):
    return lax.optimization_barrier((value,) + earlier)[0]


def spread_features(flat, far):
    pieces = []
    for turn in range(2):
        pairs = []
        for block in range(4):
            example, core = block // 2, block % 2
            for source_core in range(2):
                target = block ^ (2 * turn + (source_core ^ core))
                source = block * 4 + (example ^ far) * 2 + source_core
                pairs.append((source, target * 4 + example * 2 + core))
        pieces.append(lax.ppermute(flat, ("tensor", "example", "test"), pairs))
    return pieces


def arrived_features(pieces, *earlier):
    pieces = lax.optimization_barrier((*pieces, *earlier))
    holder = lax.axis_index("example") * 2 + lax.axis_index("test")
    return jnp.where((lax.axis_index("tensor") ^ holder) < 2, pieces[0], pieces[1])


def gathered_features(flat, n_ex, n_cores):
    rows = flat.shape[0]
    part = rows // n_cores
    mine = lax.dynamic_slice_in_dim(flat, lax.axis_index("test") * part, part, 0)
    whole = lax.all_gather(mine, "tensor", axis=1, tiled=True)
    whole = lax.all_to_all(whole, ("example", "test"), split_axis=1, concat_axis=0, tiled=True)
    owners = [lax.rem(lax.axis_index("example") + step, n_ex) for step in range(n_ex)]
    return [lax.dynamic_slice_in_dim(whole, owner * rows, rows, 0) for owner in owners]


def dot_rows_kernel(tokens_ref, weight_ref, out_ref):
    out_ref[...] = lax.dot_general(
        tokens_ref[...], weight_ref[...], (((1,), (1,)), ((), ())), preferred_element_type=F32
    )


def dot_rows(tokens, weight):
    rows, depth = tokens.shape
    hidden = weight.shape[0]
    tile = min(512, hidden)
    return pl.pallas_call(
        dot_rows_kernel,
        out_shape=jax.ShapeDtypeStruct((rows, hidden), F32),
        grid=(hidden // tile,),
        in_specs=[
            pl.BlockSpec((rows, depth), lambda i: (0, 0)),
            pl.BlockSpec((tile, depth), lambda i: (i, 0)),
        ],
        out_specs=pl.BlockSpec((rows, tile), lambda i: (0, i)),
        compiler_params=pltpu.CompilerParams(vmem_limit_bytes=16 * 2**20),
        cost_estimate=pl.CostEstimate(flops=1, bytes_accessed=1, transcendentals=0),
    )(tokens, weight)


def gradients_kernel(down_ref, *refs):
    factor_refs, proj_refs, (model_ref, hidden_ref, out_ref) = refs[:2], refs[2:4], refs[4:]
    n_z, _, share, width = out_ref.shape
    ex_loc, seq_len, _ = model_ref.shape
    hidden = down_ref.shape[1]
    chunk = min(512, hidden)
    for layer in range(2):
        outputs = jnp.zeros((ex_loc * seq_len, width), F32)
        for begin in range(0, hidden, chunk):
            part = pl.ds(begin, chunk)
            rounded = (down_ref[:, part] * factor_refs[layer][:, part]).astype(jnp.bfloat16)
            outputs += jnp.dot(rounded, proj_refs[layer][part, :], preferred_element_type=F32)
        for e in range(ex_loc):
            grad = lax.dot_general(
                outputs[e * seq_len : (e + 1) * seq_len],
                model_ref[e, :, layer * width : (layer + 1) * width],
                (((0,), (0,)), ((), ())),
                precision=lax.Precision.HIGHEST,
                preferred_element_type=F32,
            )
            for z in range(n_z):
                out_ref[z, 3 * e + layer] = grad[z * share : (z + 1) * share]
    for e in range(ex_loc):
        out_ref[:, 3 * e + 2] = hidden_ref[e]


def gradients(d_hidden, factors, projs, model, hidden_grads, n_z):
    width = projs[0].shape[1]
    rows, hidden = d_hidden.shape
    ex_loc = model.shape[0]
    return pl.pallas_call(
        gradients_kernel,
        out_shape=jax.ShapeDtypeStruct((n_z, 3 * ex_loc, width // n_z, width), F32),
        compiler_params=pltpu.CompilerParams(vmem_limit_bytes=32 * 2**20),
        cost_estimate=pl.CostEstimate(
            flops=4 * rows * hidden * width, bytes_accessed=12 * rows * hidden, transcendentals=0
        ),
    )(d_hidden, *factors, *projs, model, hidden_grads)


def on_device(
    activations,
    out_grad,
    w_gate,
    w_up,
    w_down,
    proj_model,
    proj_hidden,
    test_grads,
    lengths,
    groups,
):
    ex_loc, seq_len, d_local = activations.shape
    tok_rows = ex_loc * seq_len
    width = proj_model.shape[1] // 3
    n_z = lax.axis_size("tensor")
    n_cores = lax.axis_size("test")
    core = lax.axis_index("test")
    n_ex = lax.axis_size("example")
    ex_index = lax.axis_index("example")
    hid_part = w_gate.shape[1] // n_cores

    def forward(tokens, weight):
        return pack(jnp.dot(tokens, weight, preferred_element_type=F32))

    def core_sum(product, begin, *earlier):
        packed = product.dtype == jnp.float16

        def share_of(index):
            return lax.dynamic_slice(product, (begin, index * hid_part), (tok_rows, hid_part))

        kept = share_of(core)
        if packed:
            kept = unpack(kept)
        for step in range(1, n_cores):
            sent = share_of(lax.rem(core + step, n_cores))
            got = shift(sent if packed else pack(sent), "test", step)
            kept = kept + unpack(after(got, *earlier))
        return kept

    flat_acts = activations.reshape(tok_rows, d_local)
    flat_grad = out_grad.reshape(tok_rows, d_local)
    model_acts = jnp.dot(flat_acts, proj_model[:, : 2 * width], preferred_element_type=F32)
    model_grad = jnp.dot(flat_grad, proj_model[:, 2 * width :], preferred_element_type=F32)
    model_part = jnp.concatenate([model_acts, model_grad], 1)

    hid_proj = lax.dynamic_slice_in_dim(proj_hidden, core * hid_part, hid_part, 0)
    projs = [hid_proj[:, layer * width : (layer + 1) * width] for layer in range(3)]
    positions = jnp.arange(seq_len, dtype=jnp.int32)
    token_mask = (positions[None, :] < lengths[:, None]).astype(F32)
    all_groups = gather_in_order(groups, "example")
    early = (all_groups, model_acts, model_grad, token_mask, *projs)

    direct = (n_z, n_ex, n_cores) == (4, 2, 2)
    examples = [slice(e * seq_len, (e + 1) * seq_len) for e in range(ex_loc)]
    arrived, arrived_down = [], []
    if direct:
        acts_far = [arrived_features(spread_features(flat_acts, 1), *early)]
        acts_near = spread_features(flat_acts, 0)
    else:
        acts_near, *acts_far = gathered_features(flat_acts, n_ex, n_cores)
        grad_near, *grad_far = gathered_features(flat_grad, n_ex, n_cores)
    gate_far = [forward(one, w_gate) for one in acts_far]
    up_far = [forward(after(one, *gate_far), w_up) for one in acts_far]
    if direct:
        grad_ready = after(flat_grad, *up_far)
        grad_far, grad_near = spread_features(grad_ready, 1), spread_features(grad_ready, 0)
        acts_near = arrived_features(acts_near, *up_far)
    up_near = forward(after(acts_near, *up_far), w_up)
    gate_near = forward(after(acts_near, up_near), w_gate)
    for step, (gate, up) in enumerate(zip(gate_far, up_far), 1):
        both = pack(jnp.stack([core_sum(gate, 0, gate_near), core_sum(up, 0, gate_near)]))
        received = shift(both, "example", step)
        arrived.append(received)
    if direct:
        grad_far = [arrived_features(grad_far, both)]
        grad_near = arrived_features(grad_near, both)
    down_all = dot_rows(jnp.concatenate([*grad_far, grad_near]), w_down)
    for step in range(1, n_ex):
        sent = pack(core_sum(down_all, (step - 1) * tok_rows))
        arrived_down.append(shift(sent, "example", step))
    down_near = after(down_all, received)
    own = [
        core_sum(gate_near, 0),
        core_sum(up_near, 0),
        core_sum(down_near, (n_ex - 1) * tok_rows),
    ]
    if n_z > 8:
        model_sum = lax.psum(model_part, "tensor")
    else:
        model_sent = after(pack(model_part), sent)
        others = [shift(model_sent, "tensor", step) for step in range(1, n_z)]
        others = lax.optimization_barrier((*others, received))[:-1]
        model_sum = model_part + sum(unpack(one) for one in others)

    masked = model_sum.reshape(ex_loc, seq_len, 3 * width) * token_mask[:, :, None]

    def outer(outputs, inputs):
        product = lax.dot_general(
            outputs, inputs, (((0,), (0,)), ((), ())), precision=lax.Precision.HIGHEST
        )
        return product.reshape(n_z, width // n_z, width)

    gate_act, up_act = [
        kept + sum(unpack(one[which]) for one in arrived) for which, kept in enumerate(own[:2])
    ]
    d_hidden = lax.optimization_barrier(own[2]) + sum(unpack(one) for one in arrived_down)
    sigmoid_gate = jax.nn.sigmoid(gate_act)
    silu_gate = gate_act * sigmoid_gate
    hidden = (silu_gate * up_act).astype(jnp.bfloat16)
    gate_factor = up_act * sigmoid_gate * (1.0 + gate_act * (1.0 - sigmoid_gate))
    in_hidden = jnp.dot(hidden, projs[2], preferred_element_type=F32)
    hidden_grads = jnp.stack(
        [outer(masked[e, :, 2 * width :], in_hidden[rows]) for e, rows in enumerate(examples)]
    )
    factors = [gate_factor, silu_gate]
    grads = gradients(
        d_hidden, factors, projs[:2], masked[:, :, : 2 * width], hidden_grads, n_z
    )
    grads = scatter_sum(grads, "tensor")
    by_example = []
    for ex_step in range(n_ex):
        total = 0.0
        for core_step in range(n_cores):
            piece = grads
            if ex_step or core_step:
                pairs = [
                    (i * n_cores + c, (i + ex_step) % n_ex * n_cores + (c + core_step) % n_cores)
                    for i in range(n_ex)
                    for c in range(n_cores)
                ]
                piece = lax.ppermute(piece, ("example", "test"), pairs)
            total = total + piece
        by_example.append(total)
    grads = in_order(by_example, "example")
    partial_scores = lax.dot_general(
        grads.reshape(n_ex * ex_loc, -1),
        test_grads.astype(F32).reshape(-1, test_grads.shape[-1]),
        (((1,), (0,)), ((), ())),
        precision=lax.Precision.HIGHEST,
    )
    all_scores = jnp.sum(gather_in_order(partial_scores, "tensor"), 0)
    scores = lax.dynamic_slice_in_dim(all_scores, ex_index * ex_loc, ex_loc, 0)
    group_onehot = (
        all_groups.reshape(-1)[:, None] == jnp.arange(NGROUP, dtype=jnp.int32)[None, :]
    ).astype(F32)
    group_scores = jnp.dot(group_onehot.T, all_scores, precision=lax.Precision.HIGHEST)
    return (scores, group_scores)


def solution(mesh):
    placed = (
        P(("parts", "example"), None, "tensor"),
        P(("parts", "example"), None, "tensor"),
        P(("example", "test"), "tensor"),
        P(("example", "test"), "tensor"),
        P("tensor", ("example", "test")),
        P("tensor", None),
        P("tensor", None),
        P(None, "tensor", None, "test"),
        P(("parts", "example")),
        P(("parts", "example")),
    )
    return jax.shard_map(
        on_device,
        mesh=mesh,
        in_specs=placed,
        out_specs=(P(("parts", "example"), "test"), P("parts", "test")),
        check_vma=False,
    )
```

```python
import jax
import jax.numpy as jnp
from jax import lax
from jax.experimental import pallas as pl
from jax.experimental.pallas import tpu as pltpu
from jax.sharding import PartitionSpec as P

NGROUP = 4
F32 = jnp.float32
SEND_SCALE = 16.0


def shift(value, axis, step):
    n = lax.axis_size(axis)
    return lax.ppermute(value, axis, [(i, (i + step) % n) for i in range(n)])


def pack(value):
    return (value * SEND_SCALE).astype(jnp.float16)


def unpack(value):
    return value.astype(F32) * (1.0 / SEND_SCALE)


def in_order(pieces, axis):
    n = len(pieces)
    back = pieces[:0:-1] + pieces[:1]
    return lax.dynamic_slice_in_dim(jnp.stack(back + back), n - 1 - lax.axis_index(axis), n, 0)


def gather_in_order(value, axis):
    n = lax.axis_size(axis)
    if n > 8:
        return lax.all_gather(value, axis, axis=0)
    return in_order([value] + [shift(value, axis, step) for step in range(1, n)], axis)


def scatter_sum(blocks, axis):
    n = lax.axis_size(axis)
    if n > 8:
        return lax.psum_scatter(blocks, axis, scatter_dimension=0, tiled=True)[0]
    me = lax.axis_index(axis)
    total = lax.dynamic_index_in_dim(blocks, me, 0, keepdims=False)
    for step in range(1, n):
        block = lax.dynamic_index_in_dim(blocks, lax.rem(me + step, n), 0, keepdims=False)
        total = total + shift(block, axis, step)
    return total


def after(value, *earlier):
    return lax.optimization_barrier((value,) + earlier)[0]


def spread_features(flat):
    pieces = []
    for turn in range(2):
        pairs = []
        for block in range(4):
            example, core = block // 2, block % 2
            for far in range(2):
                for source_core in range(2):
                    target = block ^ (2 * (turn if far else 1 - turn) + (source_core ^ core))
                    source = block * 4 + (example ^ far) * 2 + source_core
                    pairs.append((source, target * 4 + example * 2 + core))
        pieces.append(lax.ppermute(flat, ("tensor", "example", "test"), pairs))
    return pieces


def arrived_features(pieces, *earlier):
    pieces = lax.optimization_barrier((*pieces, *earlier))
    holder = lax.axis_index("example") * 2 + lax.axis_index("test")
    far_first = (lax.axis_index("tensor") ^ holder) < 2
    return [jnp.where(far_first, *pieces[:2]), jnp.where(far_first, *pieces[1::-1])]


def gathered_features(flat, n_ex, n_cores):
    rows = flat.shape[0]
    part = rows // n_cores
    mine = lax.dynamic_slice_in_dim(flat, lax.axis_index("test") * part, part, 0)
    whole = lax.all_gather(mine, "tensor", axis=1, tiled=True)
    whole = lax.all_to_all(whole, ("example", "test"), split_axis=1, concat_axis=0, tiled=True)
    owners = [lax.rem(lax.axis_index("example") + step, n_ex) for step in range(n_ex)]
    return [lax.dynamic_slice_in_dim(whole, owner * rows, rows, 0) for owner in owners]


def dot_rows_kernel(tokens_ref, weight_ref, out_ref):
    out_ref[...] = lax.dot_general(
        tokens_ref[...], weight_ref[...], (((1,), (1,)), ((), ())), preferred_element_type=F32
    )


def dot_rows(tokens, weight):
    rows, depth = tokens.shape
    hidden = weight.shape[0]
    tile = min(512, hidden)
    return pl.pallas_call(
        dot_rows_kernel,
        out_shape=jax.ShapeDtypeStruct((rows, hidden), F32),
        grid=(hidden // tile,),
        in_specs=[
            pl.BlockSpec((rows, depth), lambda i: (0, 0)),
            pl.BlockSpec((tile, depth), lambda i: (i, 0)),
        ],
        out_specs=pl.BlockSpec((rows, tile), lambda i: (0, i)),
        compiler_params=pltpu.CompilerParams(vmem_limit_bytes=16 * 2**20),
        cost_estimate=pl.CostEstimate(flops=1, bytes_accessed=1, transcendentals=0),
    )(tokens, weight)


def gradients_kernel(down_ref, *refs):
    factor_refs, proj_refs, (model_ref, hidden_ref, out_ref) = refs[:2], refs[2:4], refs[4:]
    n_z, _, share, width = out_ref.shape
    ex_loc, seq_len, _ = model_ref.shape
    hidden = down_ref.shape[1]
    chunk = min(512, hidden)
    for layer in range(2):
        outputs = jnp.zeros((ex_loc * seq_len, width), F32)
        for begin in range(0, hidden, chunk):
            part = pl.ds(begin, chunk)
            rounded = (down_ref[:, part] * factor_refs[layer][:, part]).astype(jnp.bfloat16)
            outputs += jnp.dot(rounded, proj_refs[layer][part, :], preferred_element_type=F32)
        for e in range(ex_loc):
            grad = lax.dot_general(
                outputs[e * seq_len : (e + 1) * seq_len],
                model_ref[e, :, layer * width : (layer + 1) * width],
                (((0,), (0,)), ((), ())),
                precision=lax.Precision.HIGHEST,
                preferred_element_type=F32,
            )
            for z in range(n_z):
                out_ref[z, 3 * e + layer] = grad[z * share : (z + 1) * share]
    for e in range(ex_loc):
        out_ref[:, 3 * e + 2] = hidden_ref[e]


def gradients(d_hidden, factors, projs, model, hidden_grads, n_z):
    width = projs[0].shape[1]
    rows, hidden = d_hidden.shape
    ex_loc = model.shape[0]
    return pl.pallas_call(
        gradients_kernel,
        out_shape=jax.ShapeDtypeStruct((n_z, 3 * ex_loc, width // n_z, width), F32),
        compiler_params=pltpu.CompilerParams(vmem_limit_bytes=32 * 2**20),
        cost_estimate=pl.CostEstimate(
            flops=4 * rows * hidden * width, bytes_accessed=12 * rows * hidden, transcendentals=0
        ),
    )(d_hidden, *factors, *projs, model, hidden_grads)


def on_device(
    activations,
    out_grad,
    w_gate,
    w_up,
    w_down,
    proj_model,
    proj_hidden,
    test_grads,
    lengths,
    groups,
):
    ex_loc, seq_len, d_local = activations.shape
    tok_rows = ex_loc * seq_len
    width = proj_model.shape[1] // 3
    n_z = lax.axis_size("tensor")
    n_cores = lax.axis_size("test")
    core = lax.axis_index("test")
    n_ex = lax.axis_size("example")
    ex_index = lax.axis_index("example")
    hid_part = w_gate.shape[1] // n_cores

    def forward(tokens, weight):
        return pack(jnp.dot(tokens, weight, preferred_element_type=F32))

    def core_sum(product, begin, *earlier):
        packed = product.dtype == jnp.float16

        def share_of(index):
            return lax.dynamic_slice(product, (begin, index * hid_part), (tok_rows, hid_part))

        kept = share_of(core)
        if packed:
            kept = unpack(kept)
        for step in range(1, n_cores):
            sent = share_of(lax.rem(core + step, n_cores))
            got = shift(sent if packed else pack(sent), "test", step)
            kept = kept + unpack(after(got, *earlier))
        return kept

    flat_acts = activations.reshape(tok_rows, d_local)
    flat_grad = out_grad.reshape(tok_rows, d_local)
    model_acts = jnp.dot(flat_acts, proj_model[:, : 2 * width], preferred_element_type=F32)
    model_grad = jnp.dot(flat_grad, proj_model[:, 2 * width :], preferred_element_type=F32)
    model_part = jnp.concatenate([model_acts, model_grad], 1)

    hid_proj = lax.dynamic_slice_in_dim(proj_hidden, core * hid_part, hid_part, 0)
    projs = [hid_proj[:, layer * width : (layer + 1) * width] for layer in range(3)]
    positions = jnp.arange(seq_len, dtype=jnp.int32)
    token_mask = (positions[None, :] < lengths[:, None]).astype(F32)
    all_groups = gather_in_order(groups, "example")
    early = (all_groups, model_acts, model_grad, token_mask, *projs)

    direct = (n_z, n_ex, n_cores) == (4, 2, 2)
    examples = [slice(e * seq_len, (e + 1) * seq_len) for e in range(ex_loc)]
    arrived, arrived_down = [], []
    if direct:
        acts_far, acts_near = arrived_features(spread_features(flat_acts), *early)
        acts_far = [acts_far]
    else:
        acts_near, *acts_far = gathered_features(flat_acts, n_ex, n_cores)
        grad_near, *grad_far = gathered_features(flat_grad, n_ex, n_cores)
    gate_far = [forward(one, w_gate) for one in acts_far]
    up_far = [forward(after(one, *gate_far), w_up) for one in acts_far]
    if direct:
        grad_all = spread_features(after(flat_grad, *up_far))
    for step, (gate, up) in enumerate(zip(gate_far, up_far), 1):
        both = pack(jnp.stack([core_sum(gate, 0), core_sum(up, 0)]))
        received = shift(both, "example", step)
        arrived.append(received)
    gate_near = forward(after(acts_near, both), w_gate)
    up_near = forward(after(acts_near, gate_near), w_up)
    if direct:
        grad_all = arrived_features(grad_all, both)
    else:
        grad_all = [*grad_far, grad_near]
    down_all = dot_rows(jnp.concatenate(grad_all), w_down)
    for step in range(1, n_ex):
        sent = pack(core_sum(down_all, (step - 1) * tok_rows))
        arrived_down.append(shift(sent, "example", step))
    down_near = after(down_all, received)
    own = [
        core_sum(gate_near, 0),
        core_sum(up_near, 0),
        core_sum(down_near, (n_ex - 1) * tok_rows),
    ]
    if n_z > 8:
        model_sum = lax.psum(model_part, "tensor")
    else:
        model_sent = after(pack(model_part), sent)
        others = [shift(model_sent, "tensor", step) for step in range(1, n_z)]
        others = lax.optimization_barrier((*others, received))[:-1]
        model_sum = model_part + sum(unpack(one) for one in others)

    masked = model_sum.reshape(ex_loc, seq_len, 3 * width) * token_mask[:, :, None]

    def outer(outputs, inputs):
        product = lax.dot_general(
            outputs, inputs, (((0,), (0,)), ((), ())), precision=lax.Precision.HIGHEST
        )
        return product.reshape(n_z, width // n_z, width)

    gate_act, up_act = [
        kept + sum(unpack(one[which]) for one in arrived) for which, kept in enumerate(own[:2])
    ]
    d_hidden = own[2] + sum(unpack(one) for one in arrived_down)
    sigmoid_gate = jax.nn.sigmoid(gate_act)
    silu_gate = gate_act * sigmoid_gate
    hidden = (silu_gate * up_act).astype(jnp.bfloat16)
    gate_factor = up_act * sigmoid_gate * (1.0 + gate_act * (1.0 - sigmoid_gate))
    in_hidden = jnp.dot(hidden, projs[2], preferred_element_type=F32)
    hidden_grads = jnp.stack(
        [outer(masked[e, :, 2 * width :], in_hidden[rows]) for e, rows in enumerate(examples)]
    )
    factors = [gate_factor, silu_gate]
    grads = gradients(
        d_hidden, factors, projs[:2], masked[:, :, : 2 * width], hidden_grads, n_z
    )
    grads = scatter_sum(grads, "tensor")
    by_example = []
    for ex_step in range(n_ex):
        total = 0.0
        for core_step in range(n_cores):
            piece = grads
            if ex_step or core_step:
                pairs = [
                    (i * n_cores + c, (i + ex_step) % n_ex * n_cores + (c + core_step) % n_cores)
                    for i in range(n_ex)
                    for c in range(n_cores)
                ]
                piece = lax.ppermute(piece, ("example", "test"), pairs)
            total = total + piece
        by_example.append(total)
    grads = in_order(by_example, "example")
    partial_scores = lax.dot_general(
        grads.reshape(n_ex * ex_loc, -1),
        test_grads.astype(F32).reshape(-1, test_grads.shape[-1]),
        (((1,), (0,)), ((), ())),
        precision=lax.Precision.HIGHEST,
    )
    all_scores = jnp.sum(gather_in_order(partial_scores, "tensor"), 0)
    scores = lax.dynamic_slice_in_dim(all_scores, ex_index * ex_loc, ex_loc, 0)
    group_onehot = (
        all_groups.reshape(-1)[:, None] == jnp.arange(NGROUP, dtype=jnp.int32)[None, :]
    ).astype(F32)
    group_scores = jnp.dot(group_onehot.T, all_scores, precision=lax.Precision.HIGHEST)
    return (scores, group_scores)


def solution(mesh):
    placed = (
        P(("parts", "example"), None, "tensor"),
        P(("parts", "example"), None, "tensor"),
        P(("example", "test"), "tensor"),
        P(("example", "test"), "tensor"),
        P("tensor", ("example", "test")),
        P("tensor", None),
        P("tensor", None),
        P(None, "tensor", None, "test"),
        P(("parts", "example")),
        P(("parts", "example")),
    )
    return jax.shard_map(
        on_device,
        mesh=mesh,
        in_specs=placed,
        out_specs=(P(("parts", "example"), "test"), P("parts", "test")),
        check_vma=False,
    )
```
